512 devices in a mesh: row: 32 (over x, z_hi, core), col: 16 (over z_lo, y).
Axes of the slice: x: 4, y: 4, z: 16 (z_hi: 4, z_lo: 4; z = z_hi * 4 + z_lo), core: 2. Of those that a mesh axis runs over, the one named last changes fastest.
Arguments:
- matrix: float32 [8192, 8192], P('row', 'col'), as said below
Outputs:
- reduced: float32 [8192, 8192], P('row', 'col')
Inputs may be any that keep to these rules, and one draw needn't show every extreme that they name: matrix is symmetric.
All inputs are finite; a program needn't handle non-finite values.
Results may differ from the reference program's by a relative error of at most 0.0003.
Values sent between devices are 32-bit elements; how exact they have to be, the bound alone decides.
No kernel may reach another device: no remote copies, remote signals or barrier semaphores. Data moves between devices by JAX's collectives and lax.ppermute only.
A program may use at most 64 MiB of HBM per device.

```python
import math
import jax
import jax.numpy as jnp
from jax import lax

B = 32
M = 8192


def draw_matrix(key, part):
    key = jax.random.fold_in(key, 11)
    base = jnp.clip(jax.random.normal(key, (M, M), jnp.float32), -4.0, 4.0)
    symmetric = (base + base.T) * math.sqrt(0.5)
    return symmetric


def setup_inputs(seed: int = 0) -> dict:
    key_list = jax.random.split(jax.random.key(seed), 2)
    matrix = draw_matrix(jax.random.fold_in(key_list[1], 71), 0)
    return dict(matrix=matrix)


HIGHEST = lax.Precision.HIGHEST

def householder(panel_cols):
    count = panel_cols.shape[0]
    width = panel_cols.shape[1]
    rows_at = jnp.arange(count, dtype=jnp.int32)

    def sweep(column_at, carried):
        working, reflectors = carried
        column = lax.dynamic_slice_in_dim(working, column_at, 1, 1)[:, 0]
        pivot = width + column_at
        below = jnp.where(rows_at >= pivot, column, 0.0)
        col_norm = jnp.sqrt(jnp.sum(below * below))
        pivot_value = lax.dynamic_slice_in_dim(column, pivot, 1, 0)[0]
        pivot_sign = jnp.where(pivot_value >= 0.0, 1.0, -1.0)
        vector = below + jnp.where(rows_at == pivot, pivot_sign * col_norm, 0.0)
        vector = vector / jnp.sqrt(jnp.sum(vector * vector) + 1e-06)
        weights = jnp.dot(vector, working, precision=HIGHEST)
        working = working - 2.0 * vector[:, None] * weights[None, :]
        reflectors = lax.dynamic_update_slice_in_dim(reflectors, vector[:, None], column_at, 1)
        return (working, reflectors)
    finished, reflectors = lax.fori_loop(0, width, sweep, (panel_cols, jnp.zeros_like(panel_cols)))
    gram = jnp.dot(reflectors.T, reflectors, precision=HIGHEST)
    order = jnp.arange(width, dtype=jnp.int32)

    def extend(column_at, triangle):
        earlier = jnp.where(order < column_at, lax.dynamic_slice_in_dim(gram, column_at, 1, 1)[:, 0], 0.0)
        column = -2.0 * jnp.dot(triangle, earlier, precision=HIGHEST) + jnp.where(order == column_at, 2.0, 0.0)
        return lax.dynamic_update_slice_in_dim(triangle, column[:, None], column_at, 1)
    triangle = lax.fori_loop(0, width, extend, jnp.zeros((width, width), panel_cols.dtype))
    return (reflectors, triangle)

def reference(matrix):
    rows_at = jnp.arange(matrix.shape[0], dtype=jnp.int32)
    panel_cols = jnp.where(rows_at[:, None] >= B, matrix[:, :B], 0.0)
    reflectors, triangle = householder(panel_cols)
    product = jnp.dot(matrix, reflectors, precision=HIGHEST)
    scaled = jnp.dot(product, triangle, precision=HIGHEST)
    inner = jnp.dot(reflectors.T, scaled, precision=HIGHEST)
    correction = jnp.dot(triangle.T, inner, precision=HIGHEST)
    coupled = scaled - 0.5 * jnp.dot(reflectors, correction, precision=HIGHEST)
    left = jnp.concatenate([coupled, reflectors], axis=1)
    right = jnp.concatenate([reflectors, coupled], axis=1)
    return matrix - jnp.dot(left, right.T, precision=HIGHEST)
```

```python
import jax
import jax.numpy as jnp
from jax import lax
from jax.experimental import pallas as pl
from jax.experimental.pallas import tpu as pltpu
from jax.sharding import PartitionSpec as P

B = 32
ROWS = 32
COLS = 16
PIECE = 16
LANES = 128
EPS = 1e-06
AMPLIFY_MAX = 16.0
GRAM_MIN = 1e-06
GRAM_MAX = 1e08
VALUE_MAX = 1e25

HIGHEST = lax.Precision.HIGHEST


def from_root(shard, axis, root):
    mine = lax.axis_index(axis) == root
    return lax.psum(jnp.where(mine, shard, jnp.zeros_like(shard)), axis)


def householder(panel_cols):
    count = panel_cols.shape[0]
    width = panel_cols.shape[1]
    rows_at = jnp.arange(count, dtype=jnp.int32)

    def sweep(column_at, carried):
        working, reflectors = carried
        column = lax.dynamic_slice_in_dim(working, column_at, 1, 1)[:, 0]
        pivot = width + column_at
        below = jnp.where(rows_at >= pivot, column, 0.0)
        col_norm = jnp.sqrt(jnp.sum(below * below))
        pivot_value = lax.dynamic_slice_in_dim(column, pivot, 1, 0)[0]
        pivot_sign = jnp.where(pivot_value >= 0.0, 1.0, -1.0)
        vector = below + jnp.where(rows_at == pivot, pivot_sign * col_norm, 0.0)
        vector = vector / jnp.sqrt(jnp.sum(vector * vector) + EPS)
        weights = jnp.dot(vector, working, precision=HIGHEST)
        working = working - 2.0 * vector[:, None] * weights[None, :]
        reflectors = lax.dynamic_update_slice_in_dim(reflectors, vector[:, None], column_at, 1)
        return (working, reflectors)

    finished, reflectors = lax.fori_loop(0, width, sweep, (panel_cols, jnp.zeros_like(panel_cols)))
    gram = jnp.dot(reflectors.T, reflectors, precision=HIGHEST)
    order = jnp.arange(width, dtype=jnp.int32)

    def extend(column_at, triangle):
        earlier = jnp.where(
            order < column_at, lax.dynamic_slice_in_dim(gram, column_at, 1, 1)[:, 0], 0.0
        )
        column = -2.0 * jnp.dot(triangle, earlier, precision=HIGHEST) + jnp.where(
            order == column_at, 2.0, 0.0
        )
        return lax.dynamic_update_slice_in_dim(triangle, column[:, None], column_at, 1)

    triangle = lax.fori_loop(0, width, extend, jnp.zeros((width, width), panel_cols.dtype))
    return (reflectors, triangle)


def general_path(matrix):
    rows_dev = matrix.shape[0]
    cols_dev = matrix.shape[1]
    row_at = lax.axis_index("row")
    col_at = lax.axis_index("col")
    gathered = lax.all_gather(matrix[:, :B], "row", axis=0, tiled=True)
    gathered = from_root(gathered, "col", 0)
    rows_at = jnp.arange(gathered.shape[0], dtype=jnp.int32)
    panel_cols = jnp.where(rows_at[:, None] >= B, gathered, 0.0)
    reflectors, triangle = householder(panel_cols)
    own_rows = lax.dynamic_slice_in_dim(reflectors, row_at * rows_dev, rows_dev, 0)
    own_cols = lax.dynamic_slice_in_dim(reflectors, col_at * cols_dev, cols_dev, 0)
    row_product = lax.psum(jnp.dot(matrix, own_cols, precision=HIGHEST), "col")
    row_scaled = jnp.dot(row_product, triangle, precision=HIGHEST)
    whole = lax.all_gather(row_scaled, "row", axis=0, tiled=True)
    inner = jnp.dot(reflectors.T, whole, precision=HIGHEST)
    col_scaled = lax.dynamic_slice_in_dim(whole, col_at * cols_dev, cols_dev, 0)
    correction = jnp.dot(triangle.T, inner, precision=HIGHEST)
    row_coupled = row_scaled - 0.5 * jnp.dot(own_rows, correction, precision=HIGHEST)
    col_coupled = col_scaled - 0.5 * jnp.dot(own_cols, correction, precision=HIGHEST)
    left = jnp.concatenate([row_coupled, own_rows], axis=1)
    right = jnp.concatenate([own_cols, col_coupled], axis=1)
    return matrix - lax.dot_general(left, right, (((1,), (1,)), ((), ())), precision=HIGHEST)


def dot(a, b, over=((1,), (0,))):
    return lax.dot_general(
        a, b, (over, ((), ())), precision=HIGHEST, preferred_element_type=jnp.float32
    )


def dot_nt(a, b):
    return dot(a, b, ((1,), (1,)))


def dot_tn(a, b):
    return dot(a, b, ((0,), (0,)))


def iota(shape, axis):
    return lax.broadcasted_iota(jnp.int32, shape, axis)


def partial_kernel(a_ref, strip_ref, out_ref):
    first_col = lax.axis_index("col") == 0
    strip = strip_ref[0:B, :]
    start = jnp.where(first_col, 2 * B, 0)
    below_t = jnp.where(iota(strip.shape, 1) >= start, strip, 0.0)
    padded = jnp.concatenate([below_t, jnp.zeros((LANES - B, strip.shape[1]), jnp.float32)], axis=0)
    a = a_ref[...]
    rows = a.shape[0]
    product = dot_nt(a, padded)
    near = pltpu.roll(a[:, :LANES], B, 1)
    piece = jnp.where(iota((rows, LANES), 1) < B, product, near)
    out_ref[:, 0:PIECE, :] = piece.reshape(COLS, PIECE, LANES)
    gram = dot_nt(below_t, padded)
    corner = pltpu.roll(strip_ref[B : 2 * B, :LANES], B, 1)
    both = jnp.where(iota((B, LANES), 1) < B, gram, corner)
    out_ref[:, PIECE : PIECE + B, :] = jnp.broadcast_to(both[None], (COLS, B, LANES))


def sum_kernel(in_ref, out_ref, piece_ref, gram_ref):
    lane = iota((PIECE, LANES), 1)
    total = jnp.sum(in_ref[:, 0:PIECE, :], axis=0)
    piece = jnp.where(lane < B, total, in_ref[0, 0:PIECE, :])
    largest = jnp.max(jnp.where(lane < 3 * B, jnp.abs(piece), 0.0), keepdims=True)
    bad = jnp.where(largest <= VALUE_MAX, 0.0, jnp.inf)
    piece = jnp.where(lane < B, piece + bad, piece)
    piece_ref[...] = piece
    half = PIECE // 2
    folded = jnp.where(
        iota((half, LANES), 1) < 2 * B, piece[:half], pltpu.roll(piece[half:], LANES // 2, 1)
    )
    out_ref[...] = jnp.broadcast_to(folded[None], (ROWS, half, LANES))
    gram = jnp.sum(in_ref[:, PIECE : PIECE + B, :], axis=0)
    gram_ref[...] = jnp.where(iota((B, LANES), 1) < B, gram, in_ref[0, PIECE : PIECE + B, :])


def factor_kernel(gram_ref, out_ref, flag_ref):
    both = gram_ref[...]
    gram = both[:, :B]
    top0 = pltpu.roll(both, LANES - B, 1)[:, :B]
    sub = iota((B, B), 0)
    lane = iota((B, B), 1)
    eye = jnp.where(sub == lane, 1.0, 0.0)
    work = top0
    coef = eye
    image = gram
    top = jnp.zeros((B, B), jnp.float32)
    coefs = jnp.zeros((B, B), jnp.float32)
    for j in range(B):
        x_top = jnp.broadcast_to(work[:, j : j + 1], (B, B))
        x_top = jnp.where(sub >= j, x_top, 0.0)
        x_coef = jnp.broadcast_to(coef[:, j : j + 1], (B, B))
        x_image = jnp.broadcast_to(image[:, j : j + 1], (B, B))
        inner = jnp.sum(x_top * work + x_coef * image, axis=0, keepdims=True)
        norm2 = jnp.broadcast_to(inner[:, j : j + 1], (1, B))
        pivot = jnp.broadcast_to(work[j : j + 1, j : j + 1], (1, B))
        norm = jnp.sqrt(norm2)
        signed = jnp.where(pivot >= 0.0, norm, -norm)
        scale = lax.rsqrt(2.0 * (norm2 + signed * pivot) + EPS)
        weights = scale * (inner + signed * work[j : j + 1, :])
        x_top = scale * jnp.where(sub == j, x_top + signed, x_top)
        x_coef = scale * x_coef
        x_image = scale * x_image
        twice = 2.0 * weights
        work = work - x_top * twice
        coef = coef - x_coef * twice
        image = image - x_image * twice
        top = jnp.where(lane == j, x_top, top)
        coefs = jnp.where(lane == j, x_coef, coefs)
    overlap = dot_tn(top, top) + dot_tn(coefs, dot(gram, coefs))
    upper = jnp.where(sub < lane, overlap, 0.0)
    triangle = 2.0 * eye
    width = 1
    while width < B:
        joined = (sub // (2 * width) == lane // (2 * width)) & (sub // width != lane // width)
        triangle = triangle - dot(triangle, dot(jnp.where(joined, upper, 0.0), triangle))
        width *= 2
    out_ref[0] = coefs
    out_ref[1] = top
    out_ref[2] = dot(coefs, triangle)
    out_ref[3] = dot(top, triangle)
    diag = jnp.sum(jnp.where(sub == lane, gram, 0.0), axis=1, keepdims=True)
    growth = jnp.sum(jnp.abs(coefs) * jnp.sqrt(diag), axis=0, keepdims=True)
    worst = jnp.max(growth, keepdims=True)
    low = jnp.min(diag, keepdims=True)
    high = jnp.max(diag, keepdims=True)
    fine = (worst <= AMPLIFY_MAX) & (low >= GRAM_MIN) & (high <= GRAM_MAX)
    flag_ref[...] = jnp.broadcast_to(jnp.where(fine, 0.0, jnp.inf), flag_ref.shape)


def inner_kernel(in_ref, piece_ref, flag_ref, out_ref):
    col_at = lax.axis_index("col")
    half = PIECE // 2
    folded = in_ref[...]
    second = pltpu.roll(folded.reshape(ROWS * half, LANES), LANES // 2, 1).reshape(folded.shape)
    rows = jnp.concatenate([folded, second], axis=1)
    order = iota(rows.shape, 0) * (COLS * PIECE) + col_at * PIECE + iota(rows.shape, 1)
    lane = iota(rows.shape, 2)
    product = jnp.where(lane < B, rows, 0.0)
    below = jnp.where((order >= 2 * B) & (lane >= B) & (lane < 2 * B), rows, 0.0)
    count = ROWS * PIECE
    square = dot_tn(below.reshape(count, LANES), product.reshape(count, LANES))[B : 2 * B, :]
    largest = jnp.max(jnp.abs(product).reshape(count, LANES), keepdims=True)
    bad = jnp.where(largest <= VALUE_MAX, flag_ref[0:1, 0:1], jnp.inf)
    square = square + bad
    lane8 = iota((8, LANES), 1)
    packed = jnp.zeros((8, LANES), jnp.float32)
    for k in range(B // 8):
        part = square[8 * k : 8 * k + 8]
        part = part if k == 0 else pltpu.roll(part, B * k, 1)
        packed = jnp.where(lane8 // B == k, part, packed)
    out_ref[:, 0:PIECE, :] = jnp.broadcast_to(piece_ref[...][None], (COLS, PIECE, LANES))
    out_ref[:, PIECE : 2 * PIECE, :] = folded.reshape(COLS, PIECE, LANES)
    out_ref[:, 2 * PIECE : 2 * PIECE + 8, :] = jnp.broadcast_to(in_ref[0][None], (COLS, 8, LANES))
    out_ref[:, 2 * PIECE + 8 : 2 * PIECE + 16, :] = jnp.broadcast_to(packed[None], (COLS, 8, LANES))


def update_kernel(a_ref, strip_ref, in_ref, gram_ref, factor_ref, out_ref, ok_ref):
    first_row = lax.axis_index("row") == 0
    first_col = lax.axis_index("col") == 0
    half_lanes = LANES // 2
    packed = jnp.sum(in_ref[:, 2 * PIECE + 8 : 2 * PIECE + 16, :], axis=0)
    square = jnp.concatenate(
        [packed] + [pltpu.roll(packed, LANES - B * k, 1) for k in range(1, B // 8)], axis=0
    )[:, :B]
    near = []
    for source in (2, 3):
        block = in_ref[source, 2 * PIECE : 2 * PIECE + 8, :]
        near += [block, pltpu.roll(block, half_lanes, 1)]
    near = jnp.concatenate(near, axis=0)[:, :B]
    corner = pltpu.roll(gram_ref[...], LANES - 2 * B, 1)[:, :B]
    largest = jnp.max(jnp.abs(square), keepdims=True)
    ok_ref[0, 0] = (jnp.max(jnp.where(largest <= VALUE_MAX, 1.0, 0.0)) > 0.5).astype(jnp.int32)
    coefs, top, coefs_t, top_t = (factor_ref[k] for k in range(4))
    inner = dot_tn(coefs_t, dot(square, coefs_t) + dot_tn(near, top_t)) + dot_tn(
        top_t, dot(near, coefs_t) + dot(corner, top_t)
    )
    shift = 0.5 * inner
    zero = jnp.zeros((B, B), jnp.float32)
    vector = jnp.concatenate([zero, coefs, zero, top], axis=0)
    coupled = jnp.concatenate([coefs_t, zero, top_t, zero], axis=0) - dot(vector, shift)
    middle = dot_nt(coupled, vector) + dot_nt(vector, coupled)
    rows = a_ref.shape[0]
    cols = a_ref.shape[1]
    left = in_ref[:, 0:PIECE, :].reshape(rows, LANES)
    at = iota(left.shape, 0)
    lane = iota(left.shape, 1)
    start = jnp.where(first_row, 2 * B, 0)
    left = jnp.where((lane >= B) & (lane < 2 * B) & (at < start), 0.0, left)
    unit = jnp.where(first_row & (at - B == lane - 3 * B), 1.0, 0.0)
    left = jnp.where(lane >= 3 * B, unit, left)
    scaled = dot(left, middle)
    strip = strip_ref[0:B, :]
    lane_c = iota(strip.shape, 1)
    start_c = jnp.where(first_col, 2 * B, 0)
    below_t = jnp.where(lane_c >= start_c, strip, 0.0)
    unit_t = jnp.where(first_col & (iota(strip.shape, 0) == lane_c - B), 1.0, 0.0)
    parts = []
    for k in range(2):
        block = in_ref[:, PIECE + 8 * k : PIECE + 8 * k + 8, :]
        other = pltpu.roll(block.reshape(COLS * 8, LANES), half_lanes, 1).reshape(block.shape)
        unfolded = jnp.concatenate([block, other], axis=1).reshape(COLS * PIECE, LANES)
        parts.append(jnp.transpose(unfolded)[:B])
    product_t = jnp.concatenate(parts, axis=1)
    right = jnp.concatenate([product_t, below_t, strip_ref[B : 2 * B, :], unit_t], axis=0)
    out_ref[...] = a_ref[...] - dot(scaled, right)


def call(kernel, *shapes, smem=()):
    vmem = pl.BlockSpec(memory_space=pltpu.VMEM)
    specs = [
        pl.BlockSpec(memory_space=pltpu.SMEM) if k in smem else vmem for k in range(len(shapes))
    ]
    return pl.pallas_call(
        kernel,
        out_shape=list(shapes),
        out_specs=specs,
        compiler_params=pltpu.CompilerParams(vmem_limit_bytes=32 * 1024 * 1024),
    )


def array(*shape, dtype=jnp.float32):
    return jax.ShapeDtypeStruct(shape, dtype)


def spread(strip):
    at = lax.axis_index("row")
    for pairs_of in (
        [[(0, 2 * z)] for z in (2, 1, 3)],
        [[(2 * z, 8 * x + 2 * z) for z in range(4)] for x in (2, 1, 3)],
        [[(k, k + 1) for k in range(0, ROWS, 2)]],
    ):
        held = strip
        for pairs in pairs_of:
            arrived = lax.ppermute(strip, "row", pairs)
            here = jnp.zeros((), jnp.bool_)
            for _, target in pairs:
                here = here | (at == target)
            held = jnp.where(here, arrived, held)
        strip = held
    return strip


def on_device(matrix):
    strip = spread(matrix[: 2 * B, :])
    (sent,) = call(partial_kernel, array(COLS, PIECE + B, LANES))(matrix, strip)
    got = lax.all_to_all(sent, "col", 0, 0)
    sent, piece, gram = call(
        sum_kernel, array(ROWS, PIECE // 2, LANES), array(PIECE, LANES), array(B, LANES)
    )(got)
    factor, flag = call(factor_kernel, array(4, B, B), array(8, LANES))(gram)
    got = lax.all_to_all(sent, "row", 0, 0)
    (sent,) = call(inner_kernel, array(COLS, 3 * PIECE, LANES))(got, piece, flag)
    got = lax.all_to_all(sent, "col", 0, 0)
    fast, fine = call(
        update_kernel, array(*matrix.shape), array(1, 1, dtype=jnp.int32), smem=(1,)
    )(matrix, strip, got, gram, factor)
    return lax.cond(fine[0, 0] > 0, lambda: fast, lambda: general_path(matrix))


def solution(mesh):
    return jax.shard_map(
        on_device,
        mesh=mesh,
        in_specs=(P("row", "col"),),
        out_specs=P("row", "col"),
        check_vma=False,
    )
```

```python
import jax
import jax.numpy as jnp
from jax import lax
from jax.experimental import pallas as pl
from jax.experimental.pallas import tpu as pltpu
from jax.sharding import PartitionSpec as P

B = 32
ROWS = 32
COLS = 16
PIECE = 16
LANES = 128
EPS = 1e-06
AMPLIFY_MAX = 16.0
GRAM_MIN = 1e-06
GRAM_MAX = 1e08
VALUE_MAX = 1e25

HIGHEST = lax.Precision.HIGHEST


def gather(shard, axis, count):
    return lax.all_to_all(jnp.broadcast_to(shard[None], (count, *shard.shape)), axis, 0, 0)


def householder(panel_cols):
    count = panel_cols.shape[0]
    width = panel_cols.shape[1]
    rows_at = jnp.arange(count, dtype=jnp.int32)

    def sweep(column_at, carried):
        working, reflectors = carried
        column = lax.dynamic_slice_in_dim(working, column_at, 1, 1)[:, 0]
        pivot = width + column_at
        below = jnp.where(rows_at >= pivot, column, 0.0)
        col_norm = jnp.sqrt(jnp.sum(below * below))
        pivot_value = lax.dynamic_slice_in_dim(column, pivot, 1, 0)[0]
        pivot_sign = jnp.where(pivot_value >= 0.0, 1.0, -1.0)
        vector = below + jnp.where(rows_at == pivot, pivot_sign * col_norm, 0.0)
        vector = vector / jnp.sqrt(jnp.sum(vector * vector) + EPS)
        weights = jnp.dot(vector, working, precision=HIGHEST)
        working = working - 2.0 * vector[:, None] * weights[None, :]
        reflectors = lax.dynamic_update_slice_in_dim(reflectors, vector[:, None], column_at, 1)
        return (working, reflectors)

    finished, reflectors = lax.fori_loop(0, width, sweep, (panel_cols, jnp.zeros_like(panel_cols)))
    gram = jnp.dot(reflectors.T, reflectors, precision=HIGHEST)
    order = jnp.arange(width, dtype=jnp.int32)

    def extend(column_at, triangle):
        earlier = jnp.where(
            order < column_at, lax.dynamic_slice_in_dim(gram, column_at, 1, 1)[:, 0], 0.0
        )
        column = -2.0 * jnp.dot(triangle, earlier, precision=HIGHEST) + jnp.where(
            order == column_at, 2.0, 0.0
        )
        return lax.dynamic_update_slice_in_dim(triangle, column[:, None], column_at, 1)

    triangle = lax.fori_loop(0, width, extend, jnp.zeros((width, width), panel_cols.dtype))
    return (reflectors, triangle)


def general_path(matrix, strip):
    rows_dev = matrix.shape[0]
    cols_dev = matrix.shape[1]
    row_at = lax.axis_index("row")
    col_at = lax.axis_index("col")
    gathered = gather(strip[:B], "col", COLS).transpose(0, 2, 1).reshape(COLS * cols_dev, B)
    rows_at = jnp.arange(gathered.shape[0], dtype=jnp.int32)
    panel_cols = jnp.where(rows_at[:, None] >= B, gathered, 0.0)
    reflectors, triangle = householder(panel_cols)
    own_rows = lax.dynamic_slice_in_dim(reflectors, row_at * rows_dev, rows_dev, 0)
    own_cols = lax.dynamic_slice_in_dim(reflectors, col_at * cols_dev, cols_dev, 0)
    row_product = jnp.sum(gather(jnp.dot(matrix, own_cols, precision=HIGHEST), "col", COLS), axis=0)
    row_scaled = jnp.dot(row_product, triangle, precision=HIGHEST)
    whole = gather(row_scaled, "row", ROWS).reshape(ROWS * rows_dev, B)
    inner = jnp.dot(reflectors.T, whole, precision=HIGHEST)
    col_scaled = lax.dynamic_slice_in_dim(whole, col_at * cols_dev, cols_dev, 0)
    correction = jnp.dot(triangle.T, inner, precision=HIGHEST)
    row_coupled = row_scaled - 0.5 * jnp.dot(own_rows, correction, precision=HIGHEST)
    col_coupled = col_scaled - 0.5 * jnp.dot(own_cols, correction, precision=HIGHEST)
    left = jnp.concatenate([row_coupled, own_rows], axis=1)
    right = jnp.concatenate([own_cols, col_coupled], axis=1)
    return matrix - lax.dot_general(left, right, (((1,), (1,)), ((), ())), precision=HIGHEST)


def dot(a, b, over=((1,), (0,))):
    return lax.dot_general(
        a, b, (over, ((), ())), precision=HIGHEST, preferred_element_type=jnp.float32
    )


def dot_nt(a, b):
    return dot(a, b, ((1,), (1,)))


def dot_tn(a, b):
    return dot(a, b, ((0,), (0,)))


def iota(shape, axis):
    return lax.broadcasted_iota(jnp.int32, shape, axis)


def beyond(x):
    return jnp.max(jnp.where(jnp.abs(x) <= VALUE_MAX, 0.0, 1.0), keepdims=True)


def fold(square):
    group = iota((8, LANES), 1) // B
    packed = square[0:8]
    for k in range(1, B // 8):
        packed = jnp.where(group == k, pltpu.roll(square[8 * k : 8 * k + 8], B * k, 1), packed)
    return packed


def unfold(packed):
    parts = [packed] + [pltpu.roll(packed, LANES - B * k, 1) for k in range(1, B // 8)]
    return jnp.concatenate(parts, axis=0)[:, :B]


def partial_kernel(a_ref, strip_ref, out_ref):
    first_col = lax.axis_index("col") == 0
    strip = strip_ref[0:B, :]
    start = jnp.where(first_col, 2 * B, 0)
    below_t = jnp.where(iota(strip.shape, 1) >= start, strip, 0.0)
    padded = jnp.concatenate([below_t, jnp.zeros((LANES - B, strip.shape[1]), jnp.float32)], axis=0)
    a = a_ref[...]
    rows = a.shape[0]
    product = dot_nt(a, padded)
    near = pltpu.roll(a[:, :LANES], B, 1)
    piece = jnp.where(iota((rows, LANES), 1) < B, product, near)
    out_ref[:, 0:PIECE, :] = piece.reshape(COLS, PIECE, LANES)
    gram = fold(dot_nt(below_t, padded))
    corner = fold(strip_ref[B : 2 * B, :LANES])
    out_ref[:, PIECE : PIECE + 8, :] = jnp.broadcast_to(gram[None], (COLS, 8, LANES))
    out_ref[:, PIECE + 8 : PIECE + 16, :] = jnp.broadcast_to(corner[None], (COLS, 8, LANES))


def sum_kernel(in_ref, out_ref, piece_ref, gram_ref):
    lane = iota((PIECE, LANES), 1)
    total = jnp.sum(in_ref[:, 0:PIECE, :], axis=0)
    piece = jnp.where(lane < B, total, in_ref[0, 0:PIECE, :])
    bad = jnp.where(beyond(jnp.where(lane < 3 * B, piece, 0.0)) > 0.0, jnp.inf, 0.0)
    piece = jnp.where(lane < B, piece + bad, piece)
    piece_ref[...] = piece
    half = PIECE // 2
    folded = jnp.where(
        iota((half, LANES), 1) < 2 * B, piece[:half], pltpu.roll(piece[half:], LANES // 2, 1)
    )
    out_ref[...] = jnp.broadcast_to(folded[None], (ROWS, half, LANES))
    gram_ref[0:8, :] = jnp.sum(in_ref[:, PIECE : PIECE + 8, :], axis=0)
    gram_ref[8:16, :] = in_ref[0, PIECE + 8 : PIECE + 16, :]


def factor_kernel(gram_ref, out_ref, flag_ref):
    gram = unfold(gram_ref[0:8, :])
    sub = iota((B, B), 0)
    lane = iota((B, B), 1)
    eye = jnp.where(sub == lane, 1.0, 0.0)

    def column(of, j):
        return jnp.broadcast_to(of[:, j : j + 1], (B, B))

    def total(x):
        return jnp.sum(x, axis=0, keepdims=True)

    work = unfold(gram_ref[8:16, :])
    coef = eye
    image = gram
    top = jnp.zeros((B, B), jnp.float32)
    coefs = jnp.zeros((B, B), jnp.float32)
    images = jnp.zeros((B, B), jnp.float32)
    wrong = jnp.zeros((1, B), jnp.float32)
    x_top, x_coef, x_image = column(work, 0), column(coef, 0), column(image, 0)
    for j in range(B):
        pivot = x_top[j : j + 1, :]
        norm2 = total(x_top * x_top + x_coef * x_image)
        inner = total(x_top * work + x_coef * image)
        wrong = jnp.where(norm2 > 0.0, wrong, 1.0)
        norm = norm2 * lax.rsqrt(norm2)
        scale = lax.rsqrt(2.0 * (norm2 + jnp.abs(pivot) * norm) + EPS)
        signed = jnp.where(pivot >= 0.0, norm, -norm)
        v_top = scale * jnp.where(sub == j, x_top + signed, x_top)
        v_coef = scale * x_coef
        v_image = scale * x_image
        top = jnp.where(lane == j, v_top, top)
        coefs = jnp.where(lane == j, v_coef, coefs)
        images = jnp.where(lane == j, v_image, images)
        if j + 1 < B:
            y_top, y_coef, y_image = column(work, j + 1), column(coef, j + 1), column(image, j + 1)
            near = total(x_top * y_top + x_coef * y_image)
            near = (2.0 * scale) * (near + signed * y_top[j : j + 1, :])
            twice = (2.0 * scale) * (inner + signed * work[j : j + 1, :])
            work = work - v_top * twice
            coef = coef - v_coef * twice
            image = image - v_image * twice
            x_top = jnp.where(sub > j, y_top - v_top * near, 0.0)
            x_coef = y_coef - v_coef * near
            x_image = y_image - v_image * near
    vectors = jnp.concatenate([coefs, top], axis=0)
    overlap = dot_tn(vectors, jnp.concatenate([images, top], axis=0))
    upper = jnp.where(sub < lane, overlap, 0.0)
    triangle = 2.0 * eye
    for k in range(B - 1, 0, -1):
        triangle = triangle - (2.0 * column(upper, k)) * triangle[k : k + 1, :]
    out_ref[0] = vectors
    out_ref[1] = dot(vectors, triangle)
    diag = jnp.sum(jnp.where(sub == lane, gram, 0.0), axis=1, keepdims=True)
    growth = total(jnp.abs(coefs) * jnp.sqrt(diag))
    wrong = jnp.where(growth <= AMPLIFY_MAX, wrong, 1.0)
    outside = jnp.where((diag >= GRAM_MIN) & (diag <= GRAM_MAX), 0.0, 1.0)
    wrong = jnp.maximum(jnp.max(wrong, keepdims=True), jnp.max(outside, keepdims=True))
    flag_ref[...] = jnp.broadcast_to(jnp.where(wrong > 0.0, jnp.inf, 0.0), flag_ref.shape)


def inner_kernel(in_ref, piece_ref, factor_ref, flag_ref, strip_ref, out_ref):
    col_at = lax.axis_index("col")
    half = PIECE // 2
    count = ROWS * PIECE
    folded = in_ref[...]
    second = pltpu.roll(folded.reshape(ROWS * half, LANES), LANES // 2, 1).reshape(folded.shape)
    rows = jnp.concatenate([folded, second], axis=1)
    order = iota(rows.shape, 0) * (COLS * PIECE) + col_at * PIECE + iota(rows.shape, 1)
    lane = iota(rows.shape, 2)
    product = jnp.where(lane < B, rows, 0.0)
    below = jnp.where((order >= 2 * B) & (lane >= B) & (lane < 2 * B), rows, 0.0)
    square = dot_tn(below.reshape(count, LANES), product.reshape(count, LANES))[B : 2 * B, :B]
    bad = beyond(product.reshape(count, LANES)) > 0.0
    near = jnp.concatenate(
        [jnp.where(col_at == k, product[0], 0.0) for k in (2, 3)], axis=0
    )[:, :B]
    corner = pltpu.roll(strip_ref[B : 2 * B, :LANES], LANES - B, 1)[:, :B]
    corner = jnp.where(col_at == 0, corner, 0.0)
    vectors_t = factor_ref[1]
    coefs_t = vectors_t[:B]
    top_t = vectors_t[B:]
    images = jnp.concatenate(
        [dot(square, coefs_t) + dot_tn(near, top_t), dot(near, coefs_t) + dot(corner, top_t)], axis=0
    )
    padded = jnp.concatenate([images, jnp.zeros((2 * B, LANES - B), jnp.float32)], axis=1)
    inner = fold(dot_tn(vectors_t, padded))
    inner = inner + jnp.where(bad, jnp.inf, flag_ref[0:1, 0:1])
    out_ref[:, 0:PIECE, :] = jnp.broadcast_to(piece_ref[...][None], (COLS, PIECE, LANES))
    pairs = in_ref[...].reshape(COLS, 2, half, LANES)
    flat = (COLS * half, LANES)
    even, odd = pairs[:, 0].reshape(flat), pairs[:, 1].reshape(flat)
    group = iota(flat, 1) // B
    packed = jnp.where(group == 0, even, pltpu.roll(even, LANES - B, 1))
    packed = jnp.where(group == 2, pltpu.roll(odd, 2 * B, 1), packed)
    packed = jnp.where(group == 3, pltpu.roll(odd, B, 1), packed)
    out_ref[:, PIECE : PIECE + 8, :] = packed.reshape(COLS, half, LANES)
    out_ref[:, PIECE + 8 : PIECE + 16, :] = jnp.broadcast_to(inner[None], (COLS, 8, LANES))


def update_kernel(a_ref, strip_ref, in_ref, factor_ref, out_ref, ok_ref):
    first_row = lax.axis_index("row") == 0
    first_col = lax.axis_index("col") == 0
    packed = jnp.sum(in_ref[:, PIECE + 8 : PIECE + 16, :], axis=0)
    ok_ref[0, 0] = 1 - jnp.max(beyond(packed)).astype(jnp.int32)
    shift = 0.5 * unfold(packed)
    vectors = factor_ref[0]
    vectors_t = factor_ref[1]
    zero = jnp.zeros((B, B), jnp.float32)
    vector = jnp.concatenate([zero, vectors[:B], zero, vectors[B:]], axis=0)
    coupled = jnp.concatenate([vectors_t[:B], zero, vectors_t[B:], zero], axis=0)
    coupled = coupled - dot(vector, shift)
    middle = dot_nt(coupled, vector) + dot_nt(vector, coupled)
    rows = a_ref.shape[0]
    left = in_ref[:, 0:PIECE, :].reshape(rows, LANES)
    at = iota(left.shape, 0)
    lane = iota(left.shape, 1)
    start = jnp.where(first_row, 2 * B, 0)
    left = jnp.where((lane >= B) & (lane < 2 * B) & (at < start), 0.0, left)
    unit = jnp.where(first_row & (at - B == lane - 3 * B), 1.0, 0.0)
    left = jnp.where(lane >= 3 * B, unit, left)
    scaled = dot(left, middle)
    strip = strip_ref[0:B, :]
    lane_c = iota(strip.shape, 1)
    start_c = jnp.where(first_col, 2 * B, 0)
    below_t = jnp.where(lane_c >= start_c, strip, 0.0)
    unit_t = jnp.where(first_col & (iota(strip.shape, 0) == lane_c - B), 1.0, 0.0)
    block = in_ref[:, PIECE : PIECE + 8, :]
    flat = block.reshape(COLS * 8, LANES)
    quarter = [block] + [pltpu.roll(flat, LANES - B * k, 1).reshape(block.shape) for k in (1, 2, 3)]
    parts = []
    for k in (0, 2):
        unfolded = jnp.concatenate([quarter[k], quarter[k + 1]], axis=1)
        parts.append(jnp.transpose(unfolded.reshape(COLS * PIECE, LANES))[:B])
    product_t = jnp.concatenate(parts, axis=1)
    right = jnp.concatenate([product_t, below_t, strip_ref[B : 2 * B, :], unit_t], axis=0)
    out_ref[...] = a_ref[...] - dot(scaled, right)


def call(kernel, *shapes, smem=()):
    vmem = pl.BlockSpec(memory_space=pltpu.VMEM)
    specs = [
        pl.BlockSpec(memory_space=pltpu.SMEM) if k in smem else vmem for k in range(len(shapes))
    ]
    return pl.pallas_call(
        kernel,
        out_shape=list(shapes),
        out_specs=specs,
        compiler_params=pltpu.CompilerParams(vmem_limit_bytes=32 * 1024 * 1024),
    )


def array(*shape, dtype=jnp.float32):
    return jax.ShapeDtypeStruct(shape, dtype)


def spread(strip):
    strip = jnp.where(lax.axis_index("row") == 0, strip, 0.0)
    held = [0]
    for step in (4, 2, 16, 8, 1):
        strip = strip + lax.ppermute(strip, "row", [(k, k + step) for k in held])
        held = held + [k + step for k in held]
    return strip


def on_device(matrix):
    strip = spread(matrix[: 2 * B, :])
    (sent,) = call(partial_kernel, array(COLS, 2 * PIECE, LANES))(matrix, strip)
    got = lax.all_to_all(sent, "col", 0, 0)
    sent, piece, gram = call(
        sum_kernel, array(ROWS, PIECE // 2, LANES), array(PIECE, LANES), array(16, LANES)
    )(got)
    factor, flag = call(factor_kernel, array(2, 2 * B, B), array(8, LANES))(gram)
    got = lax.all_to_all(sent, "row", 0, 0)
    (sent,) = call(inner_kernel, array(COLS, 2 * PIECE, LANES))(got, piece, factor, flag, strip)
    got = lax.all_to_all(sent, "col", 0, 0)
    fast, fine = call(
        update_kernel, array(*matrix.shape), array(1, 1, dtype=jnp.int32), smem=(1,)
    )(matrix, strip, got, factor)
    return lax.cond(fine[0, 0] > 0, lambda: fast, lambda: general_path(matrix, strip))


def solution(mesh):
    return jax.shard_map(
        on_device,
        mesh=mesh,
        in_specs=(P("row", "col"),),
        out_specs=P("row", "col"),
        check_vma=False,
    )
```

```python
import jax
import jax.numpy as jnp
from jax import lax
from jax.experimental import pallas as pl
from jax.experimental.pallas import tpu as pltpu
from jax.sharding import PartitionSpec as P

B = 32
ROWS = 32
COLS = 16
PIECE = 16
LANES = 128
EPS = 1e-06
AMPLIFY_MAX = 16.0
GRAM_MIN = 1e-06
GRAM_MAX = 1e08
VALUE_MAX = 1e25

HIGHEST = lax.Precision.HIGHEST


def gather(shard, axis, count):
    return lax.all_to_all(jnp.broadcast_to(shard[None], (count, *shard.shape)), axis, 0, 0)


def householder(panel_cols):
    count = panel_cols.shape[0]
    width = panel_cols.shape[1]
    rows_at = jnp.arange(count, dtype=jnp.int32)

    def sweep(column_at, carried):
        working, reflectors = carried
        column = lax.dynamic_slice_in_dim(working, column_at, 1, 1)[:, 0]
        pivot = width + column_at
        below = jnp.where(rows_at >= pivot, column, 0.0)
        col_norm = jnp.sqrt(jnp.sum(below * below))
        pivot_value = lax.dynamic_slice_in_dim(column, pivot, 1, 0)[0]
        pivot_sign = jnp.where(pivot_value >= 0.0, 1.0, -1.0)
        vector = below + jnp.where(rows_at == pivot, pivot_sign * col_norm, 0.0)
        vector = vector / jnp.sqrt(jnp.sum(vector * vector) + EPS)
        weights = jnp.dot(vector, working, precision=HIGHEST)
        working = working - 2.0 * vector[:, None] * weights[None, :]
        reflectors = lax.dynamic_update_slice_in_dim(reflectors, vector[:, None], column_at, 1)
        return (working, reflectors)

    finished, reflectors = lax.fori_loop(0, width, sweep, (panel_cols, jnp.zeros_like(panel_cols)))
    gram = jnp.dot(reflectors.T, reflectors, precision=HIGHEST)
    order = jnp.arange(width, dtype=jnp.int32)

    def extend(column_at, triangle):
        earlier = jnp.where(
            order < column_at, lax.dynamic_slice_in_dim(gram, column_at, 1, 1)[:, 0], 0.0
        )
        column = -2.0 * jnp.dot(triangle, earlier, precision=HIGHEST) + jnp.where(
            order == column_at, 2.0, 0.0
        )
        return lax.dynamic_update_slice_in_dim(triangle, column[:, None], column_at, 1)

    triangle = lax.fori_loop(0, width, extend, jnp.zeros((width, width), panel_cols.dtype))
    return (reflectors, triangle)


def general_path(matrix, strip):
    rows_dev = matrix.shape[0]
    cols_dev = matrix.shape[1]
    row_at = lax.axis_index("row")
    col_at = lax.axis_index("col")
    gathered = gather(strip[:B], "col", COLS).transpose(0, 2, 1).reshape(COLS * cols_dev, B)
    rows_at = jnp.arange(gathered.shape[0], dtype=jnp.int32)
    panel_cols = jnp.where(rows_at[:, None] >= B, gathered, 0.0)
    reflectors, triangle = householder(panel_cols)
    own_rows = lax.dynamic_slice_in_dim(reflectors, row_at * rows_dev, rows_dev, 0)
    own_cols = lax.dynamic_slice_in_dim(reflectors, col_at * cols_dev, cols_dev, 0)
    row_product = jnp.sum(gather(jnp.dot(matrix, own_cols, precision=HIGHEST), "col", COLS), axis=0)
    row_scaled = jnp.dot(row_product, triangle, precision=HIGHEST)
    whole = gather(row_scaled, "row", ROWS).reshape(ROWS * rows_dev, B)
    inner = jnp.dot(reflectors.T, whole, precision=HIGHEST)
    col_scaled = lax.dynamic_slice_in_dim(whole, col_at * cols_dev, cols_dev, 0)
    correction = jnp.dot(triangle.T, inner, precision=HIGHEST)
    row_coupled = row_scaled - 0.5 * jnp.dot(own_rows, correction, precision=HIGHEST)
    col_coupled = col_scaled - 0.5 * jnp.dot(own_cols, correction, precision=HIGHEST)
    left = jnp.concatenate([row_coupled, own_rows], axis=1)
    right = jnp.concatenate([own_cols, col_coupled], axis=1)
    return matrix - lax.dot_general(left, right, (((1,), (1,)), ((), ())), precision=HIGHEST)


def dot(a, b, over=((1,), (0,))):
    return lax.dot_general(
        a, b, (over, ((), ())), precision=HIGHEST, preferred_element_type=jnp.float32
    )


def dot_nt(a, b):
    return dot(a, b, ((1,), (1,)))


def dot_tn(a, b):
    return dot(a, b, ((0,), (0,)))


def iota(shape, axis):
    return lax.broadcasted_iota(jnp.int32, shape, axis)


def beyond(x):
    return jnp.max(jnp.where(jnp.abs(x) <= VALUE_MAX, 0.0, 1.0), keepdims=True)


def fold(square):
    group = iota((8, LANES), 1) // B
    packed = square[0:8]
    for k in range(1, B // 8):
        packed = jnp.where(group == k, pltpu.roll(square[8 * k : 8 * k + 8], B * k, 1), packed)
    return packed


def unfold(packed):
    parts = [packed] + [pltpu.roll(packed, LANES - B * k, 1) for k in range(1, B // 8)]
    return jnp.concatenate(parts, axis=0)[:, :B]


def partial_kernel(a_ref, strip_ref, out_ref):
    first_col = lax.axis_index("col") == 0
    strip = strip_ref[...]
    start = jnp.where(first_col, 2 * B, 0)
    below_t = jnp.where(iota(strip.shape, 1) >= start, strip, 0.0)
    padded = jnp.concatenate([below_t, jnp.zeros((LANES - B, strip.shape[1]), jnp.float32)], axis=0)
    a = a_ref[...]
    rows = a.shape[0]
    product = dot_nt(a, padded)
    zero = jnp.zeros((B, rows), jnp.float32)
    panel = jnp.transpose(
        jnp.concatenate([zero, strip[:, :rows], strip[:, rows:], zero], axis=0)
    )
    lane = iota((rows, LANES), 1)
    piece = jnp.where(lane < B, product, panel)
    piece = jnp.where(lane >= 3 * B, pltpu.roll(a[:, :LANES], 2 * B, 1), piece)
    out_ref[:, 0:PIECE, :] = piece.reshape(COLS, PIECE, LANES)
    gram = fold(dot_nt(below_t, padded))
    corner = fold(pltpu.roll(panel[B : 2 * B], LANES - B, 1))
    out_ref[:, PIECE : PIECE + 8, :] = jnp.broadcast_to(gram[None], (COLS, 8, LANES))
    out_ref[:, PIECE + 8 : PIECE + 16, :] = jnp.broadcast_to(corner[None], (COLS, 8, LANES))


def sum_kernel(in_ref, out_ref, piece_ref, gram_ref):
    row_at = lax.axis_index("row")
    lane = iota((PIECE, LANES), 1)
    total = jnp.sum(in_ref[:, 0:PIECE, :], axis=0)
    panel = in_ref[row_at // 2, 0:PIECE, :]
    panel = jnp.where(row_at % 2 == 0, panel, pltpu.roll(panel, LANES - B, 1))
    other = pltpu.roll(in_ref[0, 0:PIECE, :], LANES - B, 1)
    piece = jnp.where(lane < B, total, jnp.where(lane < 2 * B, panel, other))
    bad = jnp.where(beyond(jnp.where(lane < 3 * B, piece, 0.0)) > 0.0, jnp.inf, 0.0)
    piece = jnp.where(lane < B, piece + bad, piece)
    piece_ref[...] = piece
    half = PIECE // 2
    near = jnp.where(lane < B, piece, pltpu.roll(piece, LANES - B, 1))
    folded = jnp.where(
        iota((half, LANES), 1) < 2 * B, near[:half], pltpu.roll(near[half:], LANES // 2, 1)
    )
    out_ref[...] = jnp.broadcast_to(folded[None], (ROWS, half, LANES))
    gram_ref[0:8, :] = jnp.sum(in_ref[:, PIECE : PIECE + 8, :], axis=0)
    gram_ref[8:16, :] = in_ref[0, PIECE + 8 : PIECE + 16, :]


def factor_kernel(gram_ref, out_ref, flag_ref):
    gram = unfold(gram_ref[0:8, :])
    sub = iota((B, B), 0)
    lane = iota((B, B), 1)
    eye = jnp.where(sub == lane, 1.0, 0.0)

    def column(of, j):
        return jnp.broadcast_to(of[:, j : j + 1], (B, B))

    def total(x):
        return jnp.sum(x, axis=0, keepdims=True)

    work = unfold(gram_ref[8:16, :])
    coef = eye
    image = gram
    top = jnp.zeros((B, B), jnp.float32)
    coefs = jnp.zeros((B, B), jnp.float32)
    images = jnp.zeros((B, B), jnp.float32)
    wrong = jnp.zeros((1, B), jnp.float32)
    x_top, x_coef, x_image = column(work, 0), column(coef, 0), column(image, 0)
    for j in range(B):
        pivot = x_top[j : j + 1, :]
        norm2 = total(x_top * x_top + x_coef * x_image)
        inner = total(x_top * work + x_coef * image)
        wrong = jnp.where(norm2 > 0.0, wrong, 1.0)
        norm = norm2 * lax.rsqrt(norm2)
        scale = lax.rsqrt(2.0 * (norm2 + jnp.abs(pivot) * norm) + EPS)
        signed = jnp.where(pivot >= 0.0, norm, -norm)
        v_top = scale * jnp.where(sub == j, x_top + signed, x_top)
        v_coef = scale * x_coef
        v_image = scale * x_image
        top = jnp.where(lane == j, v_top, top)
        coefs = jnp.where(lane == j, v_coef, coefs)
        images = jnp.where(lane == j, v_image, images)
        if j + 1 < B:
            y_top, y_coef, y_image = column(work, j + 1), column(coef, j + 1), column(image, j + 1)
            near = total(x_top * y_top + x_coef * y_image)
            near = (2.0 * scale) * (near + signed * y_top[j : j + 1, :])
            twice = (2.0 * scale) * (inner + signed * work[j : j + 1, :])
            work = work - v_top * twice
            coef = coef - v_coef * twice
            image = image - v_image * twice
            x_top = jnp.where(sub > j, y_top - v_top * near, 0.0)
            x_coef = y_coef - v_coef * near
            x_image = y_image - v_image * near
    vectors = jnp.concatenate([coefs, top], axis=0)
    overlap = dot_tn(vectors, jnp.concatenate([images, top], axis=0))
    upper = jnp.where(sub < lane, overlap, 0.0)
    triangle = 2.0 * eye
    for k in range(B - 1, 0, -1):
        triangle = triangle - (2.0 * column(upper, k)) * triangle[k : k + 1, :]
    out_ref[0] = vectors
    out_ref[1] = dot(vectors, triangle)
    diag = jnp.sum(jnp.where(sub == lane, gram, 0.0), axis=1, keepdims=True)
    growth = total(jnp.abs(coefs) * jnp.sqrt(diag))
    wrong = jnp.where(growth <= AMPLIFY_MAX, wrong, 1.0)
    outside = jnp.where((diag >= GRAM_MIN) & (diag <= GRAM_MAX), 0.0, 1.0)
    wrong = jnp.maximum(jnp.max(wrong, keepdims=True), jnp.max(outside, keepdims=True))
    flag_ref[...] = jnp.broadcast_to(jnp.where(wrong > 0.0, jnp.inf, 0.0), flag_ref.shape)


def unfold_rows(block):
    flat = block.reshape(COLS * 8, LANES)
    upper = pltpu.roll(flat, LANES // 2, 1).reshape(block.shape)
    return jnp.concatenate([block, upper], axis=1).reshape(COLS * PIECE, LANES)


def inner_kernel(in_ref, panel_ref, piece_ref, factor_ref, flag_ref, out_ref):
    col_at = lax.axis_index("col")
    pairs = in_ref[...].reshape(COLS, 2, PIECE // 2, LANES)
    first, second = unfold_rows(pairs[:, 0]), unfold_rows(pairs[:, 1])
    panel = panel_ref[:, 0:PIECE, :]
    source = iota(panel.shape, 0)
    order = iota(panel.shape, 1) + col_at * PIECE
    above = (source == 0) & (order < 2 * B) & (iota(panel.shape, 2) < 2 * B)
    below = jnp.where(above, 0.0, panel).reshape(COLS * PIECE, LANES)
    square = dot_tn(below, first)[B : 2 * B, :B] + dot_tn(below, second)[2 * B : 3 * B, :B]
    bad = beyond(in_ref[...].reshape(ROWS * PIECE // 2, LANES)) > 0.0
    near = jnp.concatenate(
        [jnp.where(col_at == k, first[:PIECE], 0.0) for k in (2, 3)], axis=0
    )
    corner = pltpu.roll(near, LANES - B, 1)[:, :B]
    near = near[:, :B]
    vectors_t = factor_ref[1]
    coefs_t = vectors_t[:B]
    top_t = vectors_t[B:]
    images = jnp.concatenate(
        [dot(square, coefs_t) + dot_tn(near, top_t), dot(near, coefs_t) + dot(corner, top_t)], axis=0
    )
    padded = jnp.concatenate([images, jnp.zeros((2 * B, LANES - B), jnp.float32)], axis=1)
    inner = fold(dot_tn(vectors_t, padded))
    inner = inner + jnp.where(bad, jnp.inf, flag_ref[0:1, 0:1])
    out_ref[:, 0:PIECE, :] = jnp.broadcast_to(piece_ref[...][None], (COLS, PIECE, LANES))
    out_ref[:, PIECE : 2 * PIECE, :] = in_ref[...].reshape(COLS, PIECE, LANES)
    out_ref[:, 2 * PIECE : 2 * PIECE + 8, :] = jnp.broadcast_to(inner[None], (COLS, 8, LANES))


def update_kernel(a_ref, strip_ref, in_ref, factor_ref, out_ref, ok_ref):
    first_row = lax.axis_index("row") == 0
    first_col = lax.axis_index("col") == 0
    packed = jnp.sum(in_ref[:, 2 * PIECE : 2 * PIECE + 8, :], axis=0)
    ok_ref[0, 0] = 1 - jnp.max(beyond(packed)).astype(jnp.int32)
    shift = 0.5 * unfold(packed)
    vectors = factor_ref[0]
    vectors_t = factor_ref[1]
    zero = jnp.zeros((B, B), jnp.float32)
    vector = jnp.concatenate([zero, vectors[:B], zero, vectors[B:]], axis=0)
    coupled = jnp.concatenate([vectors_t[:B], zero, vectors_t[B:], zero], axis=0)
    coupled = coupled - dot(vector, shift)
    middle = dot_nt(coupled, vector) + dot_nt(vector, coupled)
    rows = a_ref.shape[0]
    left = in_ref[:, 0:PIECE, :].reshape(rows, LANES)
    at = iota(left.shape, 0)
    lane = iota(left.shape, 1)
    start = jnp.where(first_row, 2 * B, 0)
    left = jnp.where((lane >= B) & (lane < 2 * B) & (at < start), 0.0, left)
    unit = jnp.where(first_row & (at - B == lane - 3 * B), 1.0, 0.0)
    left = jnp.where(lane >= 3 * B, unit, left)
    scaled = dot(left, middle)
    strip = strip_ref[...]
    lane_c = iota(strip.shape, 1)
    start_c = jnp.where(first_col, 2 * B, 0)
    below_t = jnp.where(lane_c >= start_c, strip, 0.0)
    unit_t = jnp.where(first_col & (iota(strip.shape, 0) == lane_c - B), 1.0, 0.0)
    halves = [
        jnp.transpose(unfold_rows(in_ref[:, PIECE + 8 * k : PIECE + 8 * k + 8, :]))[: 2 * B]
        for k in range(2)
    ]
    both = jnp.concatenate(halves, axis=1)
    right = jnp.concatenate([both[:B], below_t, both[B:], unit_t], axis=0)
    out_ref[...] = a_ref[...] - dot(scaled, right)


def call(kernel, *shapes, smem=()):
    vmem = pl.BlockSpec(memory_space=pltpu.VMEM)
    specs = [
        pl.BlockSpec(memory_space=pltpu.SMEM) if k in smem else vmem for k in range(len(shapes))
    ]
    return pl.pallas_call(
        kernel,
        out_shape=list(shapes),
        out_specs=specs,
        compiler_params=pltpu.CompilerParams(vmem_limit_bytes=32 * 1024 * 1024),
    )


def array(*shape, dtype=jnp.float32):
    return jax.ShapeDtypeStruct(shape, dtype)


def spread(strip):
    strip = jnp.where(lax.axis_index("row") == 0, strip, 0.0)
    for stage in (
        [[(0, 8 * x)] for x in (2, 1, 3)],
        [[(8 * x, 8 * x + 2 * z) for x in range(4)] for z in (1, 3)],
        [[(8 * x + 2, 8 * x + 4) for x in range(4)]],
        [[(k, k + 1) for k in range(0, ROWS, 2)]],
    ):
        held = strip
        for pairs in stage:
            held = held + lax.ppermute(strip, "row", pairs)
        strip = held
    return strip


def on_device(matrix):
    strip = spread(matrix[:B, :])
    (sent,) = call(partial_kernel, array(COLS, 2 * PIECE, LANES))(matrix, strip)
    panel = lax.all_to_all(sent, "col", 0, 0)
    sent, piece, gram = call(
        sum_kernel, array(ROWS, PIECE // 2, LANES), array(PIECE, LANES), array(16, LANES)
    )(panel)
    factor, flag = call(factor_kernel, array(2, 2 * B, B), array(8, LANES))(gram)
    got = lax.all_to_all(sent, "row", 0, 0)
    (sent,) = call(inner_kernel, array(COLS, 2 * PIECE + 8, LANES))(got, panel, piece, factor, flag)
    got = lax.all_to_all(sent, "col", 0, 0)
    fast, fine = call(
        update_kernel, array(*matrix.shape), array(1, 1, dtype=jnp.int32), smem=(1,)
    )(matrix, strip, got, factor)
    return lax.cond(fine[0, 0] > 0, lambda: fast, lambda: general_path(matrix, strip))


def solution(mesh):
    return jax.shard_map(
        on_device,
        mesh=mesh,
        in_specs=(P("row", "col"),),
        out_specs=P("row", "col"),
        check_vma=False,
    )
```

```python
import jax
import jax.numpy as jnp
from jax import lax
from jax.experimental import pallas as pl
from jax.experimental.pallas import tpu as pltpu
from jax.sharding import PartitionSpec as P

B = 32
ROWS = 32
COLS = 16
PIECE = 16
LANES = 128
EPS = 1e-06
AMPLIFY_MAX = 16.0
GRAM_MIN = 1e-06
GRAM_MAX = 1e08
VALUE_MAX = 1e25

HIGHEST = lax.Precision.HIGHEST


def gather(shard, axis, count):
    return lax.all_to_all(jnp.broadcast_to(shard[None], (count, *shard.shape)), axis, 0, 0)


def householder(panel_cols):
    count = panel_cols.shape[0]
    width = panel_cols.shape[1]
    rows_at = jnp.arange(count, dtype=jnp.int32)

    def sweep(column_at, carried):
        working, reflectors = carried
        column = lax.dynamic_slice_in_dim(working, column_at, 1, 1)[:, 0]
        pivot = width + column_at
        below = jnp.where(rows_at >= pivot, column, 0.0)
        col_norm = jnp.sqrt(jnp.sum(below * below))
        pivot_value = lax.dynamic_slice_in_dim(column, pivot, 1, 0)[0]
        pivot_sign = jnp.where(pivot_value >= 0.0, 1.0, -1.0)
        vector = below + jnp.where(rows_at == pivot, pivot_sign * col_norm, 0.0)
        vector = vector / jnp.sqrt(jnp.sum(vector * vector) + EPS)
        weights = jnp.dot(vector, working, precision=HIGHEST)
        working = working - 2.0 * vector[:, None] * weights[None, :]
        reflectors = lax.dynamic_update_slice_in_dim(reflectors, vector[:, None], column_at, 1)
        return (working, reflectors)

    finished, reflectors = lax.fori_loop(0, width, sweep, (panel_cols, jnp.zeros_like(panel_cols)))
    gram = jnp.dot(reflectors.T, reflectors, precision=HIGHEST)
    order = jnp.arange(width, dtype=jnp.int32)

    def extend(column_at, triangle):
        earlier = jnp.where(
            order < column_at, lax.dynamic_slice_in_dim(gram, column_at, 1, 1)[:, 0], 0.0
        )
        column = -2.0 * jnp.dot(triangle, earlier, precision=HIGHEST) + jnp.where(
            order == column_at, 2.0, 0.0
        )
        return lax.dynamic_update_slice_in_dim(triangle, column[:, None], column_at, 1)

    triangle = lax.fori_loop(0, width, extend, jnp.zeros((width, width), panel_cols.dtype))
    return (reflectors, triangle)


def general_path(matrix, strip):
    rows_dev = matrix.shape[0]
    cols_dev = matrix.shape[1]
    row_at = lax.axis_index("row")
    col_at = lax.axis_index("col")
    gathered = gather(strip[:B], "col", COLS).transpose(0, 2, 1).reshape(COLS * cols_dev, B)
    rows_at = jnp.arange(gathered.shape[0], dtype=jnp.int32)
    panel_cols = jnp.where(rows_at[:, None] >= B, gathered, 0.0)
    reflectors, triangle = householder(panel_cols)
    own_rows = lax.dynamic_slice_in_dim(reflectors, row_at * rows_dev, rows_dev, 0)
    own_cols = lax.dynamic_slice_in_dim(reflectors, col_at * cols_dev, cols_dev, 0)
    row_product = jnp.sum(gather(jnp.dot(matrix, own_cols, precision=HIGHEST), "col", COLS), axis=0)
    row_scaled = jnp.dot(row_product, triangle, precision=HIGHEST)
    whole = gather(row_scaled, "row", ROWS).reshape(ROWS * rows_dev, B)
    inner = jnp.dot(reflectors.T, whole, precision=HIGHEST)
    col_scaled = lax.dynamic_slice_in_dim(whole, col_at * cols_dev, cols_dev, 0)
    correction = jnp.dot(triangle.T, inner, precision=HIGHEST)
    row_coupled = row_scaled - 0.5 * jnp.dot(own_rows, correction, precision=HIGHEST)
    col_coupled = col_scaled - 0.5 * jnp.dot(own_cols, correction, precision=HIGHEST)
    left = jnp.concatenate([row_coupled, own_rows], axis=1)
    right = jnp.concatenate([own_cols, col_coupled], axis=1)
    return matrix - lax.dot_general(left, right, (((1,), (1,)), ((), ())), precision=HIGHEST)


def dot(a, b, over=((1,), (0,))):
    return lax.dot_general(
        a, b, (over, ((), ())), precision=HIGHEST, preferred_element_type=jnp.float32
    )


def dot_nt(a, b):
    return dot(a, b, ((1,), (1,)))


def dot_tn(a, b):
    return dot(a, b, ((0,), (0,)))


def iota(shape, axis):
    return lax.broadcasted_iota(jnp.int32, shape, axis)


def beyond(x):
    return jnp.max(jnp.where(jnp.abs(x) <= VALUE_MAX, 0.0, 1.0), keepdims=True)


def fold(square):
    group = iota((8, LANES), 1) // B
    packed = square[0:8]
    for k in range(1, B // 8):
        packed = jnp.where(group == k, pltpu.roll(square[8 * k : 8 * k + 8], B * k, 1), packed)
    return packed


def unfold(packed):
    parts = [packed] + [pltpu.roll(packed, LANES - B * k, 1) for k in range(1, B // 8)]
    return jnp.concatenate(parts, axis=0)[:, :B]


def partial_kernel(a_ref, strip_ref, out_ref):
    first_col = lax.axis_index("col") == 0
    strip = strip_ref[...]
    start = jnp.where(first_col, 2 * B, 0)
    below_t = jnp.where(iota(strip.shape, 1) >= start, strip, 0.0)
    padded = jnp.concatenate([below_t, jnp.zeros((LANES - B, strip.shape[1]), jnp.float32)], axis=0)
    a = a_ref[...]
    rows = a.shape[0]
    product = dot_nt(a, padded)
    zero = jnp.zeros((B, rows), jnp.float32)
    panel = jnp.transpose(
        jnp.concatenate([zero, strip[:, :rows], strip[:, rows:], zero], axis=0)
    )
    lane = iota((rows, LANES), 1)
    piece = jnp.where(lane < B, product, panel)
    piece = jnp.where(lane >= 3 * B, pltpu.roll(a[:, :LANES], 2 * B, 1), piece)
    out_ref[:, 0:PIECE, :] = piece.reshape(COLS, PIECE, LANES)
    gram = fold(dot_nt(below_t, padded))
    corner = fold(pltpu.roll(panel[B : 2 * B], LANES - B, 1))
    out_ref[:, PIECE : PIECE + 8, :] = jnp.broadcast_to(gram[None], (COLS, 8, LANES))
    out_ref[:, PIECE + 8 : PIECE + 16, :] = jnp.broadcast_to(corner[None], (COLS, 8, LANES))


def sum_kernel(in_ref, out_ref, piece_ref, gram_ref):
    row_at = lax.axis_index("row")
    lane = iota((PIECE, LANES), 1)
    total = jnp.sum(in_ref[:, 0:PIECE, :], axis=0)
    panel = in_ref[row_at // 2, 0:PIECE, :]
    panel = jnp.where(row_at % 2 == 0, panel, pltpu.roll(panel, LANES - B, 1))
    other = pltpu.roll(in_ref[0, 0:PIECE, :], LANES - B, 1)
    piece = jnp.where(lane < B, total, jnp.where(lane < 2 * B, panel, other))
    bad = jnp.where(beyond(jnp.where(lane < 3 * B, piece, 0.0)) > 0.0, jnp.inf, 0.0)
    piece = jnp.where(lane < B, piece + bad, piece)
    piece_ref[...] = piece
    half = PIECE // 2
    near = jnp.where(lane < B, piece, pltpu.roll(piece, LANES - B, 1))
    folded = jnp.where(
        iota((half, LANES), 1) < 2 * B, near[:half], pltpu.roll(near[half:], LANES // 2, 1)
    )
    out_ref[...] = jnp.broadcast_to(folded[None], (ROWS, half, LANES))
    gram_ref[0:8, :] = jnp.sum(in_ref[:, PIECE : PIECE + 8, :], axis=0)
    gram_ref[8:16, :] = in_ref[0, PIECE + 8 : PIECE + 16, :]


def factor_kernel(gram_ref, out_ref, flag_ref):
    gram = unfold(gram_ref[0:8, :])
    sub = iota((B, B), 0)
    lane = iota((B, B), 1)
    eye = jnp.where(sub == lane, 1.0, 0.0)

    def column(of, j):
        return jnp.broadcast_to(of[:, j : j + 1], (B, B))

    def total(x):
        return jnp.sum(x, axis=0, keepdims=True)

    work = unfold(gram_ref[8:16, :])
    coef = eye
    image = gram
    top = jnp.zeros((B, B), jnp.float32)
    coefs = jnp.zeros((B, B), jnp.float32)
    images = jnp.zeros((B, B), jnp.float32)
    wrong = jnp.zeros((1, B), jnp.float32)
    x_top, x_coef, x_image = column(work, 0), column(coef, 0), column(image, 0)
    for j in range(B):
        pivot = x_top[j : j + 1, :]
        norm2 = total(x_top * x_top + x_coef * x_image)
        inner = total(x_top * work + x_coef * image)
        wrong = jnp.where(norm2 > 0.0, wrong, 1.0)
        norm = norm2 * lax.rsqrt(norm2)
        scale = lax.rsqrt(2.0 * (norm2 + jnp.abs(pivot) * norm) + EPS)
        signed = jnp.where(pivot >= 0.0, norm, -norm)
        v_top = scale * jnp.where(sub == j, x_top + signed, x_top)
        v_coef = scale * x_coef
        v_image = scale * x_image
        top = jnp.where(lane == j, v_top, top)
        coefs = jnp.where(lane == j, v_coef, coefs)
        images = jnp.where(lane == j, v_image, images)
        if j + 1 < B:
            y_top, y_coef, y_image = column(work, j + 1), column(coef, j + 1), column(image, j + 1)
            near = total(x_top * y_top + x_coef * y_image)
            near = (2.0 * scale) * (near + signed * y_top[j : j + 1, :])
            twice = (2.0 * scale) * (inner + signed * work[j : j + 1, :])
            work = work - v_top * twice
            coef = coef - v_coef * twice
            image = image - v_image * twice
            x_top = jnp.where(sub > j, y_top - v_top * near, 0.0)
            x_coef = y_coef - v_coef * near
            x_image = y_image - v_image * near
    vectors = jnp.concatenate([coefs, top], axis=0)
    overlap = dot_tn(vectors, jnp.concatenate([images, top], axis=0))
    upper = jnp.where(sub < lane, overlap, 0.0)
    triangle = 2.0 * eye
    for k in range(B - 1, 0, -1):
        triangle = triangle - (2.0 * column(upper, k)) * triangle[k : k + 1, :]
    out_ref[0] = vectors
    out_ref[1] = dot(vectors, triangle)
    diag = jnp.sum(jnp.where(sub == lane, gram, 0.0), axis=1, keepdims=True)
    growth = total(jnp.abs(coefs) * jnp.sqrt(diag))
    wrong = jnp.where(growth <= AMPLIFY_MAX, wrong, 1.0)
    outside = jnp.where((diag >= GRAM_MIN) & (diag <= GRAM_MAX), 0.0, 1.0)
    wrong = jnp.maximum(jnp.max(wrong, keepdims=True), jnp.max(outside, keepdims=True))
    flag_ref[...] = jnp.broadcast_to(jnp.where(wrong > 0.0, jnp.inf, 0.0), flag_ref.shape)


def unfold_rows(block):
    flat = block.reshape(COLS * 8, LANES)
    upper = pltpu.roll(flat, LANES // 2, 1).reshape(block.shape)
    return jnp.concatenate([block, upper], axis=1).reshape(COLS * PIECE, LANES)


def inner_kernel(in_ref, panel_ref, piece_ref, factor_ref, flag_ref, out_ref):
    col_at = lax.axis_index("col")
    pairs = in_ref[...].reshape(COLS, 2, PIECE // 2, LANES)
    first, second = unfold_rows(pairs[:, 0]), unfold_rows(pairs[:, 1])
    panel = panel_ref[:, 0:PIECE, :]
    source = iota(panel.shape, 0)
    order = iota(panel.shape, 1) + col_at * PIECE
    above = (source == 0) & (order < 2 * B) & (iota(panel.shape, 2) < 2 * B)
    below = jnp.where(above, 0.0, panel).reshape(COLS * PIECE, LANES)
    square = dot_tn(below, first)[B : 2 * B, :B] + dot_tn(below, second)[2 * B : 3 * B, :B]
    bad = beyond(in_ref[...].reshape(ROWS * PIECE // 2, LANES)) > 0.0
    near = jnp.concatenate(
        [jnp.where(col_at == k, first[:PIECE], 0.0) for k in (2, 3)], axis=0
    )
    corner = pltpu.roll(near, LANES - B, 1)[:, :B]
    near = near[:, :B]
    vectors_t = factor_ref[1]
    coefs_t = vectors_t[:B]
    top_t = vectors_t[B:]
    images = jnp.concatenate(
        [dot(square, coefs_t) + dot_tn(near, top_t), dot(near, coefs_t) + dot(corner, top_t)], axis=0
    )
    padded = jnp.concatenate([images, jnp.zeros((2 * B, LANES - B), jnp.float32)], axis=1)
    inner = fold(dot_tn(vectors_t, padded))
    inner = inner + jnp.where(bad, jnp.inf, flag_ref[0:1, 0:1])
    out_ref[:, 0:PIECE, :] = jnp.broadcast_to(piece_ref[...][None], (COLS, PIECE, LANES))
    out_ref[:, PIECE : 2 * PIECE, :] = in_ref[...].reshape(COLS, PIECE, LANES)
    out_ref[:, 2 * PIECE : 2 * PIECE + 8, :] = jnp.broadcast_to(inner[None], (COLS, 8, LANES))


def update_kernel(a_ref, strip_ref, in_ref, factor_ref, out_ref, ok_ref):
    first_row = lax.axis_index("row") == 0
    first_col = lax.axis_index("col") == 0
    packed = jnp.sum(in_ref[:, 2 * PIECE : 2 * PIECE + 8, :], axis=0)
    ok_ref[0, 0] = 1 - jnp.max(beyond(packed)).astype(jnp.int32)
    shift = 0.5 * unfold(packed)
    vectors = factor_ref[0]
    vectors_t = factor_ref[1]
    zero = jnp.zeros((B, B), jnp.float32)
    vector = jnp.concatenate([zero, vectors[:B], zero, vectors[B:]], axis=0)
    coupled = jnp.concatenate([vectors_t[:B], zero, vectors_t[B:], zero], axis=0)
    coupled = coupled - dot(vector, shift)
    middle = dot_nt(coupled, vector) + dot_nt(vector, coupled)
    rows = a_ref.shape[0]
    left = in_ref[:, 0:PIECE, :].reshape(rows, LANES)
    at = iota(left.shape, 0)
    lane = iota(left.shape, 1)
    start = jnp.where(first_row, 2 * B, 0)
    left = jnp.where((lane >= B) & (lane < 2 * B) & (at < start), 0.0, left)
    unit = jnp.where(first_row & (at - B == lane - 3 * B), 1.0, 0.0)
    left = jnp.where(lane >= 3 * B, unit, left)
    scaled = dot(left, middle)
    strip = strip_ref[...]
    lane_c = iota(strip.shape, 1)
    start_c = jnp.where(first_col, 2 * B, 0)
    below_t = jnp.where(lane_c >= start_c, strip, 0.0)
    unit_t = jnp.where(first_col & (iota(strip.shape, 0) == lane_c - B), 1.0, 0.0)
    halves = [
        jnp.transpose(unfold_rows(in_ref[:, PIECE + 8 * k : PIECE + 8 * k + 8, :]))[: 2 * B]
        for k in range(2)
    ]
    both = jnp.concatenate(halves, axis=1)
    right = jnp.concatenate([both[:B], below_t, both[B:], unit_t], axis=0)
    out_ref[...] = a_ref[...] - dot(scaled, right)


def call(kernel, *shapes, smem=()):
    vmem = pl.BlockSpec(memory_space=pltpu.VMEM)
    specs = [
        pl.BlockSpec(memory_space=pltpu.SMEM) if k in smem else vmem for k in range(len(shapes))
    ]
    return pl.pallas_call(
        kernel,
        out_shape=list(shapes),
        out_specs=specs,
        compiler_params=pltpu.CompilerParams(vmem_limit_bytes=32 * 1024 * 1024),
    )


def array(*shape, dtype=jnp.float32):
    return jax.ShapeDtypeStruct(shape, dtype)


def spread(strip):
    row_at = lax.axis_index("row")
    x_at = row_at // 8
    strip = lax.optimization_barrier(jnp.where(row_at == 0, strip, 0.0))
    width = strip.shape[1] // 4
    held = strip[:, :width]
    for x in (2, 1, 3):
        held = held + lax.ppermute(strip[:, x * width : (x + 1) * width], "row", [(0, 8 * x)])
    near = held
    for z in (1, 3):
        near = near + lax.ppermute(held, "row", [(8 * x, 8 * x + 2 * z) for x in range(4)])
    own = near + lax.ppermute(near, "row", [(8 * x + 2, 8 * x + 4) for x in range(4)])
    of = [own]
    for step in (1, 2, 3):
        pairs = [(8 * x + z, 8 * ((x + step) % 4) + z) for x in range(4) for z in (0, 2, 4, 6)]
        of.append(lax.ppermute(own, "row", pairs))
    quarters = []
    for quarter in range(4):
        found = of[0]
        for step in (1, 2, 3):
            found = jnp.where(x_at == (quarter + step) % 4, of[step], found)
        quarters.append(found)
    strip = jnp.concatenate(quarters, axis=1)
    return strip + lax.ppermute(strip, "row", [(k, k + 1) for k in range(0, ROWS, 2)])


def on_device(matrix):
    strip = spread(matrix[:B, :])
    (sent,) = call(partial_kernel, array(COLS, 2 * PIECE, LANES))(matrix, strip)
    panel = lax.all_to_all(sent, "col", 0, 0)
    sent, piece, gram = call(
        sum_kernel, array(ROWS, PIECE // 2, LANES), array(PIECE, LANES), array(16, LANES)
    )(panel)
    factor, flag = call(factor_kernel, array(2, 2 * B, B), array(8, LANES))(gram)
    got = lax.all_to_all(sent, "row", 0, 0)
    (sent,) = call(inner_kernel, array(COLS, 2 * PIECE + 8, LANES))(got, panel, piece, factor, flag)
    got = lax.all_to_all(sent, "col", 0, 0)
    fast, fine = call(
        update_kernel, array(*matrix.shape), array(1, 1, dtype=jnp.int32), smem=(1,)
    )(matrix, strip, got, factor)
    return lax.cond(fine[0, 0] > 0, lambda: fast, lambda: general_path(matrix, strip))


def solution(mesh):
    return jax.shard_map(
        on_device,
        mesh=mesh,
        in_specs=(P("row", "col"),),
        out_specs=P("row", "col"),
        check_vma=False,
    )
```

```python
import jax
import jax.numpy as jnp
from jax import lax
from jax.experimental import pallas as pl
from jax.experimental.pallas import tpu as pltpu
from jax.sharding import PartitionSpec as P

B = 32
ROWS = 32
COLS = 16
PIECE = 16
LANES = 128
EPS = 1e-06
AMPLIFY_MAX = 16.0
GRAM_MIN = 1e-06
GRAM_MAX = 1e08
VALUE_MAX = 1e25

HIGHEST = lax.Precision.HIGHEST


def gather(shard, axis, count):
    return lax.all_to_all(jnp.broadcast_to(shard[None], (count, *shard.shape)), axis, 0, 0)


def householder(panel_cols):
    count = panel_cols.shape[0]
    width = panel_cols.shape[1]
    rows_at = jnp.arange(count, dtype=jnp.int32)

    def sweep(column_at, carried):
        working, reflectors = carried
        column = lax.dynamic_slice_in_dim(working, column_at, 1, 1)[:, 0]
        pivot = width + column_at
        below = jnp.where(rows_at >= pivot, column, 0.0)
        col_norm = jnp.sqrt(jnp.sum(below * below))
        pivot_value = lax.dynamic_slice_in_dim(column, pivot, 1, 0)[0]
        pivot_sign = jnp.where(pivot_value >= 0.0, 1.0, -1.0)
        vector = below + jnp.where(rows_at == pivot, pivot_sign * col_norm, 0.0)
        vector = vector / jnp.sqrt(jnp.sum(vector * vector) + EPS)
        weights = jnp.dot(vector, working, precision=HIGHEST)
        working = working - 2.0 * vector[:, None] * weights[None, :]
        reflectors = lax.dynamic_update_slice_in_dim(reflectors, vector[:, None], column_at, 1)
        return (working, reflectors)

    finished, reflectors = lax.fori_loop(0, width, sweep, (panel_cols, jnp.zeros_like(panel_cols)))
    gram = jnp.dot(reflectors.T, reflectors, precision=HIGHEST)
    order = jnp.arange(width, dtype=jnp.int32)

    def extend(column_at, triangle):
        earlier = jnp.where(
            order < column_at, lax.dynamic_slice_in_dim(gram, column_at, 1, 1)[:, 0], 0.0
        )
        column = -2.0 * jnp.dot(triangle, earlier, precision=HIGHEST) + jnp.where(
            order == column_at, 2.0, 0.0
        )
        return lax.dynamic_update_slice_in_dim(triangle, column[:, None], column_at, 1)

    triangle = lax.fori_loop(0, width, extend, jnp.zeros((width, width), panel_cols.dtype))
    return (reflectors, triangle)


def general_path(matrix, strip):
    rows_dev = matrix.shape[0]
    cols_dev = matrix.shape[1]
    row_at = lax.axis_index("row")
    col_at = lax.axis_index("col")
    gathered = gather(strip[:B], "col", COLS).transpose(0, 2, 1).reshape(COLS * cols_dev, B)
    rows_at = jnp.arange(gathered.shape[0], dtype=jnp.int32)
    panel_cols = jnp.where(rows_at[:, None] >= B, gathered, 0.0)
    reflectors, triangle = householder(panel_cols)
    own_rows = lax.dynamic_slice_in_dim(reflectors, row_at * rows_dev, rows_dev, 0)
    own_cols = lax.dynamic_slice_in_dim(reflectors, col_at * cols_dev, cols_dev, 0)
    row_product = jnp.sum(gather(jnp.dot(matrix, own_cols, precision=HIGHEST), "col", COLS), axis=0)
    row_scaled = jnp.dot(row_product, triangle, precision=HIGHEST)
    whole = gather(row_scaled, "row", ROWS).reshape(ROWS * rows_dev, B)
    inner = jnp.dot(reflectors.T, whole, precision=HIGHEST)
    col_scaled = lax.dynamic_slice_in_dim(whole, col_at * cols_dev, cols_dev, 0)
    correction = jnp.dot(triangle.T, inner, precision=HIGHEST)
    row_coupled = row_scaled - 0.5 * jnp.dot(own_rows, correction, precision=HIGHEST)
    col_coupled = col_scaled - 0.5 * jnp.dot(own_cols, correction, precision=HIGHEST)
    left = jnp.concatenate([row_coupled, own_rows], axis=1)
    right = jnp.concatenate([own_cols, col_coupled], axis=1)
    return matrix - lax.dot_general(left, right, (((1,), (1,)), ((), ())), precision=HIGHEST)


def dot(a, b, over=((1,), (0,))):
    return lax.dot_general(
        a, b, (over, ((), ())), precision=HIGHEST, preferred_element_type=jnp.float32
    )


def dot_nt(a, b):
    return dot(a, b, ((1,), (1,)))


def dot_tn(a, b):
    return dot(a, b, ((0,), (0,)))


def iota(shape, axis):
    return lax.broadcasted_iota(jnp.int32, shape, axis)


def beyond(x):
    return jnp.max(jnp.where(jnp.abs(x) <= VALUE_MAX, 0.0, 1.0), keepdims=True)


def fold(square):
    group = iota((8, LANES), 1) // B
    packed = square[0:8]
    for k in range(1, B // 8):
        packed = jnp.where(group == k, pltpu.roll(square[8 * k : 8 * k + 8], B * k, 1), packed)
    return packed


def unfold(packed):
    parts = [packed] + [pltpu.roll(packed, LANES - B * k, 1) for k in range(1, B // 8)]
    return jnp.concatenate(parts, axis=0)[:, :B]


def partial_kernel(a_ref, strip_ref, out_ref):
    first_col = lax.axis_index("col") == 0
    strip = strip_ref[...]
    start = jnp.where(first_col, 2 * B, 0)
    below_t = jnp.where(iota(strip.shape, 1) >= start, strip, 0.0)
    padded = jnp.concatenate([below_t, jnp.zeros((LANES - B, strip.shape[1]), jnp.float32)], axis=0)
    a = a_ref[...]
    rows = a.shape[0]
    product = dot_nt(a, padded)
    zero = jnp.zeros((B, rows), jnp.float32)
    panel = jnp.transpose(
        jnp.concatenate([zero, strip[:, :rows], strip[:, rows:], zero], axis=0)
    )
    lane = iota((rows, LANES), 1)
    piece = jnp.where(lane < B, product, panel)
    piece = jnp.where(lane >= 3 * B, pltpu.roll(a[:, :LANES], 2 * B, 1), piece)
    out_ref[:, 0:PIECE, :] = piece.reshape(COLS, PIECE, LANES)
    gram = fold(dot_nt(below_t, padded))
    corner = fold(pltpu.roll(panel[B : 2 * B], LANES - B, 1))
    out_ref[:, PIECE : PIECE + 8, :] = jnp.broadcast_to(gram[None], (COLS, 8, LANES))
    out_ref[:, PIECE + 8 : PIECE + 16, :] = jnp.broadcast_to(corner[None], (COLS, 8, LANES))


def sum_kernel(in_ref, out_ref, piece_ref, gram_ref):
    row_at = lax.axis_index("row")
    lane = iota((PIECE, LANES), 1)
    total = jnp.sum(in_ref[:, 0:PIECE, :], axis=0)
    panel = in_ref[row_at // 2, 0:PIECE, :]
    panel = jnp.where(row_at % 2 == 0, panel, pltpu.roll(panel, LANES - B, 1))
    other = pltpu.roll(in_ref[0, 0:PIECE, :], LANES - B, 1)
    piece = jnp.where(lane < B, total, jnp.where(lane < 2 * B, panel, other))
    bad = jnp.where(beyond(jnp.where(lane < 3 * B, piece, 0.0)) > 0.0, jnp.inf, 0.0)
    piece = jnp.where(lane < B, piece + bad, piece)
    piece_ref[...] = piece
    half = PIECE // 2
    near = jnp.where(lane < B, piece, pltpu.roll(piece, LANES - B, 1))
    folded = jnp.where(
        iota((half, LANES), 1) < 2 * B, near[:half], pltpu.roll(near[half:], LANES // 2, 1)
    )
    out_ref[...] = jnp.broadcast_to(folded[None], (ROWS, half, LANES))
    gram_ref[0:8, :] = jnp.sum(in_ref[:, PIECE : PIECE + 8, :], axis=0)
    gram_ref[8:16, :] = in_ref[0, PIECE + 8 : PIECE + 16, :]


def factor_kernel(gram_ref, out_ref, flag_ref):
    gram = unfold(gram_ref[0:8, :])
    sub = iota((B, B), 0)
    lane = iota((B, B), 1)
    eye = jnp.where(sub == lane, 1.0, 0.0)

    def column(of, j):
        return jnp.broadcast_to(of[:, j : j + 1], (B, B))

    def total(x):
        return jnp.sum(x, axis=0, keepdims=True)

    work = unfold(gram_ref[8:16, :])
    coef = eye
    image = gram
    top = jnp.zeros((B, B), jnp.float32)
    coefs = jnp.zeros((B, B), jnp.float32)
    images = jnp.zeros((B, B), jnp.float32)
    wrong = jnp.zeros((1, B), jnp.float32)
    x_top, x_coef, x_image = column(work, 0), column(coef, 0), column(image, 0)
    for j in range(B):
        pivot = x_top[j : j + 1, :]
        norm2 = total(x_top * x_top + x_coef * x_image)
        inner = total(x_top * work + x_coef * image)
        wrong = jnp.where(norm2 > 0.0, wrong, 1.0)
        norm = norm2 * lax.rsqrt(norm2)
        scale = lax.rsqrt(2.0 * (norm2 + jnp.abs(pivot) * norm) + EPS)
        signed = jnp.where(pivot >= 0.0, norm, -norm)
        v_top = scale * jnp.where(sub == j, x_top + signed, x_top)
        v_coef = scale * x_coef
        v_image = scale * x_image
        top = jnp.where(lane == j, v_top, top)
        coefs = jnp.where(lane == j, v_coef, coefs)
        images = jnp.where(lane == j, v_image, images)
        if j + 1 < B:
            y_top, y_coef, y_image = column(work, j + 1), column(coef, j + 1), column(image, j + 1)
            near = total(x_top * y_top + x_coef * y_image)
            near = (2.0 * scale) * (near + signed * y_top[j : j + 1, :])
            twice = (2.0 * scale) * (inner + signed * work[j : j + 1, :])
            work = work - v_top * twice
            coef = coef - v_coef * twice
            image = image - v_image * twice
            x_top = jnp.where(sub > j, y_top - v_top * near, 0.0)
            x_coef = y_coef - v_coef * near
            x_image = y_image - v_image * near
    vectors = jnp.concatenate([coefs, top], axis=0)
    overlap = dot_tn(vectors, jnp.concatenate([images, top], axis=0))
    upper = jnp.where(sub < lane, overlap, 0.0)
    triangle = 2.0 * eye
    for k in range(B - 1, 0, -1):
        triangle = triangle - (2.0 * column(upper, k)) * triangle[k : k + 1, :]
    out_ref[0] = vectors
    out_ref[1] = dot(vectors, triangle)
    diag = jnp.sum(jnp.where(sub == lane, gram, 0.0), axis=1, keepdims=True)
    growth = total(jnp.abs(coefs) * jnp.sqrt(diag))
    wrong = jnp.where(growth <= AMPLIFY_MAX, wrong, 1.0)
    outside = jnp.where((diag >= GRAM_MIN) & (diag <= GRAM_MAX), 0.0, 1.0)
    wrong = jnp.maximum(jnp.max(wrong, keepdims=True), jnp.max(outside, keepdims=True))
    flag_ref[...] = jnp.broadcast_to(jnp.where(wrong > 0.0, jnp.inf, 0.0), flag_ref.shape)


def unfold_rows(block):
    flat = block.reshape(COLS * 8, LANES)
    upper = pltpu.roll(flat, LANES // 2, 1).reshape(block.shape)
    return jnp.concatenate([block, upper], axis=1).reshape(COLS * PIECE, LANES)


def inner_kernel(in_ref, panel_ref, piece_ref, factor_ref, flag_ref, out_ref):
    col_at = lax.axis_index("col")
    pairs = in_ref[...].reshape(COLS, 2, PIECE // 2, LANES)
    first, second = unfold_rows(pairs[:, 0]), unfold_rows(pairs[:, 1])
    panel = panel_ref[:, 0:PIECE, :]
    source = iota(panel.shape, 0)
    order = iota(panel.shape, 1) + col_at * PIECE
    above = (source == 0) & (order < 2 * B) & (iota(panel.shape, 2) < 2 * B)
    below = jnp.where(above, 0.0, panel).reshape(COLS * PIECE, LANES)
    square = dot_tn(below, first)[B : 2 * B, :B] + dot_tn(below, second)[2 * B : 3 * B, :B]
    bad = beyond(in_ref[...].reshape(ROWS * PIECE // 2, LANES)) > 0.0
    near = jnp.concatenate(
        [jnp.where(col_at == k, first[:PIECE], 0.0) for k in (2, 3)], axis=0
    )
    corner = pltpu.roll(near, LANES - B, 1)[:, :B]
    near = near[:, :B]
    vectors_t = factor_ref[1]
    coefs_t = vectors_t[:B]
    top_t = vectors_t[B:]
    images = jnp.concatenate(
        [dot(square, coefs_t) + dot_tn(near, top_t), dot(near, coefs_t) + dot(corner, top_t)], axis=0
    )
    padded = jnp.concatenate([images, jnp.zeros((2 * B, LANES - B), jnp.float32)], axis=1)
    inner = fold(dot_tn(vectors_t, padded))
    inner = inner + jnp.where(bad, jnp.inf, flag_ref[0:1, 0:1])
    out_ref[:, 0:PIECE, :] = jnp.broadcast_to(piece_ref[...][None], (COLS, PIECE, LANES))
    out_ref[:, PIECE : 2 * PIECE, :] = in_ref[...].reshape(COLS, PIECE, LANES)
    out_ref[:, 2 * PIECE : 2 * PIECE + 8, :] = jnp.broadcast_to(inner[None], (COLS, 8, LANES))


def update_kernel(a_ref, strip_ref, in_ref, factor_ref, out_ref, ok_ref):
    first_row = lax.axis_index("row") == 0
    first_col = lax.axis_index("col") == 0
    packed = jnp.sum(in_ref[:, 2 * PIECE : 2 * PIECE + 8, :], axis=0)
    ok_ref[0, 0] = 1 - jnp.max(beyond(packed)).astype(jnp.int32)
    shift = 0.5 * unfold(packed)
    vectors = factor_ref[0]
    vectors_t = factor_ref[1]
    zero = jnp.zeros((B, B), jnp.float32)
    vector = jnp.concatenate([zero, vectors[:B], zero, vectors[B:]], axis=0)
    coupled = jnp.concatenate([vectors_t[:B], zero, vectors_t[B:], zero], axis=0)
    coupled = coupled - dot(vector, shift)
    middle = dot_nt(coupled, vector) + dot_nt(vector, coupled)
    rows = a_ref.shape[0]
    left = in_ref[:, 0:PIECE, :].reshape(rows, LANES)
    at = iota(left.shape, 0)
    lane = iota(left.shape, 1)
    start = jnp.where(first_row, 2 * B, 0)
    left = jnp.where((lane >= B) & (lane < 2 * B) & (at < start), 0.0, left)
    unit = jnp.where(first_row & (at - B == lane - 3 * B), 1.0, 0.0)
    left = jnp.where(lane >= 3 * B, unit, left)
    scaled = dot(left, middle)
    strip = strip_ref[...]
    lane_c = iota(strip.shape, 1)
    start_c = jnp.where(first_col, 2 * B, 0)
    below_t = jnp.where(lane_c >= start_c, strip, 0.0)
    unit_t = jnp.where(first_col & (iota(strip.shape, 0) == lane_c - B), 1.0, 0.0)
    halves = [
        jnp.transpose(unfold_rows(in_ref[:, PIECE + 8 * k : PIECE + 8 * k + 8, :]))[: 2 * B]
        for k in range(2)
    ]
    both = jnp.concatenate(halves, axis=1)
    right = jnp.concatenate([both[:B], below_t, both[B:], unit_t], axis=0)
    out_ref[...] = a_ref[...] - dot(scaled, right)


def call(kernel, *shapes, smem=()):
    vmem = pl.BlockSpec(memory_space=pltpu.VMEM)
    specs = [
        pl.BlockSpec(memory_space=pltpu.SMEM) if k in smem else vmem for k in range(len(shapes))
    ]
    return pl.pallas_call(
        kernel,
        out_shape=list(shapes),
        out_specs=specs,
        compiler_params=pltpu.CompilerParams(vmem_limit_bytes=32 * 1024 * 1024),
    )


def array(*shape, dtype=jnp.float32):
    return jax.ShapeDtypeStruct(shape, dtype)


def spread(strip):
    strip = lax.optimization_barrier(jnp.where(lax.axis_index("row") == 0, strip, 0.0))
    for pairs in (
        [(0, 16)],
        [(0, 8), (16, 24)],
        [(8 * x, 8 * x + 2) for x in range(4)],
        [(8 * x + z, 8 * x + (z + 2 if z else 6)) for x in range(4) for z in (0, 2)],
        [(k, k + 1) for k in range(0, ROWS, 2)],
    ):
        strip = strip + lax.ppermute(strip, "row", pairs)
    return strip


def on_device(matrix):
    strip = spread(matrix[:B, :])
    (sent,) = call(partial_kernel, array(COLS, 2 * PIECE, LANES))(matrix, strip)
    panel = lax.all_to_all(sent, "col", 0, 0)
    sent, piece, gram = call(
        sum_kernel, array(ROWS, PIECE // 2, LANES), array(PIECE, LANES), array(16, LANES)
    )(panel)
    factor, flag = call(factor_kernel, array(2, 2 * B, B), array(8, LANES))(gram)
    got = lax.all_to_all(sent, "row", 0, 0)
    (sent,) = call(inner_kernel, array(COLS, 2 * PIECE + 8, LANES))(got, panel, piece, factor, flag)
    got = lax.all_to_all(sent, "col", 0, 0)
    fast, fine = call(
        update_kernel, array(*matrix.shape), array(1, 1, dtype=jnp.int32), smem=(1,)
    )(matrix, strip, got, factor)
    return lax.cond(fine[0, 0] > 0, lambda: fast, lambda: general_path(matrix, strip))


def solution(mesh):
    return jax.shard_map(
        on_device,
        mesh=mesh,
        in_specs=(P("row", "col"),),
        out_specs=P("row", "col"),
        check_vma=False,
    )
```

```python
import jax
import jax.numpy as jnp
from jax import lax
from jax.experimental import pallas as pl
from jax.experimental.pallas import tpu as pltpu
from jax.sharding import PartitionSpec as P

B = 32
ROWS = 32
COLS = 16
PIECE = 16
LANES = 128
EPS = 1e-06
AMPLIFY_MAX = 16.0
GRAM_MIN = 1e-06
GRAM_MAX = 1e08
VALUE_MAX = 1e25

HIGHEST = lax.Precision.HIGHEST


def gather(shard, axis, count):
    return lax.all_to_all(jnp.broadcast_to(shard[None], (count, *shard.shape)), axis, 0, 0)


def householder(panel_cols):
    count = panel_cols.shape[0]
    width = panel_cols.shape[1]
    rows_at = jnp.arange(count, dtype=jnp.int32)

    def sweep(column_at, carried):
        working, reflectors = carried
        column = lax.dynamic_slice_in_dim(working, column_at, 1, 1)[:, 0]
        pivot = width + column_at
        below = jnp.where(rows_at >= pivot, column, 0.0)
        col_norm = jnp.sqrt(jnp.sum(below * below))
        pivot_value = lax.dynamic_slice_in_dim(column, pivot, 1, 0)[0]
        pivot_sign = jnp.where(pivot_value >= 0.0, 1.0, -1.0)
        vector = below + jnp.where(rows_at == pivot, pivot_sign * col_norm, 0.0)
        vector = vector / jnp.sqrt(jnp.sum(vector * vector) + EPS)
        weights = jnp.dot(vector, working, precision=HIGHEST)
        working = working - 2.0 * vector[:, None] * weights[None, :]
        reflectors = lax.dynamic_update_slice_in_dim(reflectors, vector[:, None], column_at, 1)
        return (working, reflectors)

    finished, reflectors = lax.fori_loop(0, width, sweep, (panel_cols, jnp.zeros_like(panel_cols)))
    gram = jnp.dot(reflectors.T, reflectors, precision=HIGHEST)
    order = jnp.arange(width, dtype=jnp.int32)

    def extend(column_at, triangle):
        earlier = jnp.where(
            order < column_at, lax.dynamic_slice_in_dim(gram, column_at, 1, 1)[:, 0], 0.0
        )
        column = -2.0 * jnp.dot(triangle, earlier, precision=HIGHEST) + jnp.where(
            order == column_at, 2.0, 0.0
        )
        return lax.dynamic_update_slice_in_dim(triangle, column[:, None], column_at, 1)

    triangle = lax.fori_loop(0, width, extend, jnp.zeros((width, width), panel_cols.dtype))
    return (reflectors, triangle)


def general_path(matrix, strip):
    rows_dev = matrix.shape[0]
    cols_dev = matrix.shape[1]
    row_at = lax.axis_index("row")
    col_at = lax.axis_index("col")
    gathered = gather(strip[:B], "col", COLS).transpose(0, 2, 1).reshape(COLS * cols_dev, B)
    rows_at = jnp.arange(gathered.shape[0], dtype=jnp.int32)
    panel_cols = jnp.where(rows_at[:, None] >= B, gathered, 0.0)
    reflectors, triangle = householder(panel_cols)
    own_rows = lax.dynamic_slice_in_dim(reflectors, row_at * rows_dev, rows_dev, 0)
    own_cols = lax.dynamic_slice_in_dim(reflectors, col_at * cols_dev, cols_dev, 0)
    row_product = jnp.sum(gather(jnp.dot(matrix, own_cols, precision=HIGHEST), "col", COLS), axis=0)
    row_scaled = jnp.dot(row_product, triangle, precision=HIGHEST)
    whole = gather(row_scaled, "row", ROWS).reshape(ROWS * rows_dev, B)
    inner = jnp.dot(reflectors.T, whole, precision=HIGHEST)
    col_scaled = lax.dynamic_slice_in_dim(whole, col_at * cols_dev, cols_dev, 0)
    correction = jnp.dot(triangle.T, inner, precision=HIGHEST)
    row_coupled = row_scaled - 0.5 * jnp.dot(own_rows, correction, precision=HIGHEST)
    col_coupled = col_scaled - 0.5 * jnp.dot(own_cols, correction, precision=HIGHEST)
    left = jnp.concatenate([row_coupled, own_rows], axis=1)
    right = jnp.concatenate([own_cols, col_coupled], axis=1)
    return matrix - lax.dot_general(left, right, (((1,), (1,)), ((), ())), precision=HIGHEST)


def dot(a, b, over=((1,), (0,))):
    return lax.dot_general(
        a, b, (over, ((), ())), precision=HIGHEST, preferred_element_type=jnp.float32
    )


def dot_nt(a, b):
    return dot(a, b, ((1,), (1,)))


def dot_tn(a, b):
    return dot(a, b, ((0,), (0,)))


def iota(shape, axis):
    return lax.broadcasted_iota(jnp.int32, shape, axis)


def beyond(x):
    return jnp.max(jnp.where(jnp.abs(x) <= VALUE_MAX, 0.0, 1.0), keepdims=True)


def fold(square):
    group = iota((8, LANES), 1) // B
    packed = square[0:8]
    for k in range(1, B // 8):
        packed = jnp.where(group == k, pltpu.roll(square[8 * k : 8 * k + 8], B * k, 1), packed)
    return packed


def unfold(packed):
    parts = [packed] + [pltpu.roll(packed, LANES - B * k, 1) for k in range(1, B // 8)]
    return jnp.concatenate(parts, axis=0)[:, :B]


def partial_kernel(a_ref, strip_ref, out_ref):
    first_col = lax.axis_index("col") == 0
    strip = strip_ref[...]
    start = jnp.where(first_col, 2 * B, 0)
    below_t = jnp.where(iota(strip.shape, 1) >= start, strip, 0.0)
    padded = jnp.concatenate([below_t, jnp.zeros((LANES - B, strip.shape[1]), jnp.float32)], axis=0)
    a = a_ref[...]
    rows = a.shape[0]
    product = dot_nt(a, padded)
    zero = jnp.zeros((B, rows), jnp.float32)
    panel = jnp.transpose(
        jnp.concatenate([zero, strip[:, :rows], strip[:, rows:], zero], axis=0)
    )
    lane = iota((rows, LANES), 1)
    piece = jnp.where(lane < B, product, panel)
    piece = jnp.where(lane >= 3 * B, pltpu.roll(a[:, :LANES], 2 * B, 1), piece)
    out_ref[:, 0:PIECE, :] = piece.reshape(COLS, PIECE, LANES)
    gram = fold(dot_nt(below_t, padded))
    corner = fold(pltpu.roll(panel[B : 2 * B], LANES - B, 1))
    out_ref[:, PIECE : PIECE + 8, :] = jnp.broadcast_to(gram[None], (COLS, 8, LANES))
    out_ref[:, PIECE + 8 : PIECE + 16, :] = jnp.broadcast_to(corner[None], (COLS, 8, LANES))


def sum_kernel(in_ref, out_ref, piece_ref, gram_ref):
    row_at = lax.axis_index("row")
    lane = iota((PIECE, LANES), 1)
    total = jnp.sum(in_ref[:, 0:PIECE, :], axis=0)
    panel = in_ref[row_at // 2, 0:PIECE, :]
    panel = jnp.where(row_at % 2 == 0, panel, pltpu.roll(panel, LANES - B, 1))
    other = pltpu.roll(in_ref[0, 0:PIECE, :], LANES - B, 1)
    piece = jnp.where(lane < B, total, jnp.where(lane < 2 * B, panel, other))
    bad = jnp.where(beyond(jnp.where(lane < 3 * B, piece, 0.0)) > 0.0, jnp.inf, 0.0)
    piece = jnp.where(lane < B, piece + bad, piece)
    piece_ref[...] = piece
    half = PIECE // 2
    near = jnp.where(lane < B, piece, pltpu.roll(piece, LANES - B, 1))
    folded = jnp.where(
        iota((half, LANES), 1) < 2 * B, near[:half], pltpu.roll(near[half:], LANES // 2, 1)
    )
    out_ref[...] = jnp.broadcast_to(folded[None], (ROWS, half, LANES))
    gram_ref[0:8, :] = jnp.sum(in_ref[:, PIECE : PIECE + 8, :], axis=0)
    gram_ref[8:16, :] = in_ref[0, PIECE + 8 : PIECE + 16, :]


def placed(blocks):
    wide = []
    for block, quarter in blocks:
        block = jnp.concatenate([block, jnp.zeros((B, LANES - B), jnp.float32)], axis=1)
        wide.append(pltpu.roll(block, B * quarter, 1) if quarter else block)
    return jnp.concatenate(wide, axis=0)


def factor_kernel(gram_ref, strip_ref, mix_ref, vectors_ref, out_ref, flag_ref):
    gram = unfold(gram_ref[0:8, :])
    sub = iota((B, B), 0)
    lane = iota((B, B), 1)
    eye = jnp.where(sub == lane, 1.0, 0.0)

    def column(of, j):
        return jnp.broadcast_to(of[:, j : j + 1], (B, B))

    def total(x):
        return jnp.sum(x, axis=0, keepdims=True)

    work = unfold(gram_ref[8:16, :])
    coef = eye
    image = gram
    top = jnp.zeros((B, B), jnp.float32)
    coefs = jnp.zeros((B, B), jnp.float32)
    images = jnp.zeros((B, B), jnp.float32)
    wrong = jnp.zeros((1, B), jnp.float32)
    x_top, x_coef, x_image = column(work, 0), column(coef, 0), column(image, 0)
    for j in range(B):
        pivot = x_top[j : j + 1, :]
        norm2 = total(x_top * x_top + x_coef * x_image)
        inner = total(x_top * work + x_coef * image)
        wrong = jnp.where(norm2 > 0.0, wrong, 1.0)
        norm = norm2 * lax.rsqrt(norm2)
        scale = lax.rsqrt(2.0 * (norm2 + jnp.abs(pivot) * norm) + EPS)
        signed = jnp.where(pivot >= 0.0, norm, -norm)
        v_top = scale * jnp.where(sub == j, x_top + signed, x_top)
        v_coef = scale * x_coef
        v_image = scale * x_image
        top = jnp.where(lane == j, v_top, top)
        coefs = jnp.where(lane == j, v_coef, coefs)
        images = jnp.where(lane == j, v_image, images)
        if j + 1 < B:
            y_top, y_coef, y_image = column(work, j + 1), column(coef, j + 1), column(image, j + 1)
            near = total(x_top * y_top + x_coef * y_image)
            near = (2.0 * scale) * (near + signed * y_top[j : j + 1, :])
            twice = (2.0 * scale) * (inner + signed * work[j : j + 1, :])
            work = work - v_top * twice
            coef = coef - v_coef * twice
            image = image - v_image * twice
            x_top = jnp.where(sub > j, y_top - v_top * near, 0.0)
            x_coef = y_coef - v_coef * near
            x_image = y_image - v_image * near
    vectors = jnp.concatenate([coefs, top], axis=0)
    overlap = dot_tn(vectors, jnp.concatenate([images, top], axis=0))
    upper = jnp.where(sub < lane, overlap, 0.0)
    triangle = 2.0 * eye
    for k in range(B - 1, 0, -1):
        triangle = triangle - (2.0 * column(upper, k)) * triangle[k : k + 1, :]
    vectors_t = dot(vectors, triangle)
    vectors_ref[...] = vectors_t
    coefs_t, top_t = vectors_t[:B], vectors_t[B:]
    mix_ref[0] = placed([(coefs_t, 0), (coefs, 1), (top_t, 0), (top, 1)])
    mix_ref[1] = placed([(coefs_t, 0), (top_t, 0), (coefs_t, 1), (top_t, 1)])
    mix_ref[2] = placed([(coefs_t, 2), (top_t, 2), (coefs_t, 3), (top_t, 3)])
    first_col = lax.axis_index("col") == 0
    strip = strip_ref[...]
    lane_c = iota(strip.shape, 1)
    below_t = jnp.where(lane_c >= jnp.where(first_col, 2 * B, 0), strip, 0.0)
    unit_t = jnp.where(first_col & (iota(strip.shape, 0) == lane_c - B), 1.0, 0.0)
    out_ref[...] = dot_tn(vectors, jnp.concatenate([below_t, unit_t], axis=0))
    diag = jnp.sum(jnp.where(sub == lane, gram, 0.0), axis=1, keepdims=True)
    growth = total(jnp.abs(coefs) * jnp.sqrt(diag))
    wrong = jnp.where(growth <= AMPLIFY_MAX, wrong, 1.0)
    outside = jnp.where((diag >= GRAM_MIN) & (diag <= GRAM_MAX), 0.0, 1.0)
    wrong = jnp.maximum(jnp.max(wrong, keepdims=True), jnp.max(outside, keepdims=True))
    flag_ref[...] = jnp.broadcast_to(jnp.where(wrong > 0.0, jnp.inf, 0.0), flag_ref.shape)


def unfold_rows(block):
    flat = block.reshape(COLS * 8, LANES)
    upper = pltpu.roll(flat, LANES // 2, 1).reshape(block.shape)
    return jnp.concatenate([block, upper], axis=1).reshape(COLS * PIECE, LANES)


def inner_kernel(in_ref, panel_ref, piece_ref, mix_ref, vectors_ref, flag_ref, out_ref):
    row_at = lax.axis_index("row")
    col_at = lax.axis_index("col")
    half = PIECE // 2
    pairs = in_ref[...].reshape(COLS, 2, half, LANES)
    even, odd = pairs[:, 0], pairs[:, 1]
    first, second = unfold_rows(even), unfold_rows(odd)
    panel = panel_ref[:, 0:PIECE, :]
    source = iota(panel.shape, 0)
    order = iota(panel.shape, 1) + col_at * PIECE
    above = (source == 0) & (order < 2 * B) & (iota(panel.shape, 2) < 2 * B)
    below = jnp.where(above, 0.0, panel).reshape(COLS * PIECE, LANES)
    square = dot_tn(below, first)[B : 2 * B, :B] + dot_tn(below, second)[2 * B : 3 * B, :B]
    bad = beyond(in_ref[...].reshape(ROWS * half, LANES)) > 0.0
    near = jnp.concatenate(
        [jnp.where(col_at == k, first[:PIECE], 0.0) for k in (2, 3)], axis=0
    )
    corner = pltpu.roll(near, LANES - B, 1)[:, :B]
    near = near[:, :B]
    vectors_t = vectors_ref[...]
    coefs_t = vectors_t[:B]
    top_t = vectors_t[B:]
    images = jnp.concatenate(
        [dot(square, coefs_t) + dot_tn(near, top_t), dot(near, coefs_t) + dot(corner, top_t)], axis=0
    )
    padded = jnp.concatenate([images, jnp.zeros((2 * B, LANES - B), jnp.float32)], axis=1)
    inner = fold(dot_tn(vectors_t, padded))
    inner = inner + jnp.where(bad, jnp.inf, flag_ref[0:1, 0:1])
    piece = piece_ref[...]
    lane = iota(piece.shape, 1)
    at = iota(piece.shape, 0) + (row_at * COLS + col_at) * PIECE
    piece = jnp.where((lane >= B) & (lane < 2 * B) & (at < 2 * B), 0.0, piece)
    piece = jnp.where(lane >= 3 * B, jnp.where(at - B == lane - 3 * B, 1.0, 0.0), piece)
    piece = dot(piece, mix_ref[0])
    piece = jnp.where(lane[:half] < 2 * B, piece[:half], pltpu.roll(piece[half:], LANES // 2, 1))
    flat = (COLS * half, LANES)
    columns = dot(even.reshape(flat), mix_ref[1]) + dot(odd.reshape(flat), mix_ref[2])
    out_ref[:, 0:half, :] = jnp.broadcast_to(piece[None], (COLS, half, LANES))
    out_ref[:, half : 2 * half, :] = columns.reshape(COLS, half, LANES)
    out_ref[:, 2 * half : 3 * half, :] = jnp.broadcast_to(inner[None], (COLS, half, LANES))


def update_kernel(a_ref, in_ref, right_ref, out_ref, ok_ref):
    half = PIECE // 2
    packed = jnp.sum(in_ref[:, 2 * half : 3 * half, :], axis=0)
    ok_ref[0, 0] = 1 - jnp.max(beyond(packed)).astype(jnp.int32)
    inner = unfold(packed)
    shift = 0.5 * (inner + jnp.transpose(inner))
    left = unfold_rows(in_ref[:, 0:half, :])[:, : 2 * B]
    zero = jnp.zeros((B, B), jnp.float32)
    shift = jnp.concatenate([zero, shift], axis=0)
    shift = jnp.concatenate([shift, jnp.zeros((2 * B, B), jnp.float32)], axis=1)
    left = left - dot(left, shift)
    flat = in_ref[:, half : 2 * half, :].reshape(COLS * half, LANES)
    quarter = [flat] + [pltpu.roll(flat, LANES - B * k, 1) for k in (1, 2, 3)]
    quarter = [part.reshape(COLS, half, LANES) for part in quarter]
    halves = []
    for k in (0, 2):
        unfolded = jnp.concatenate([quarter[k], quarter[k + 1]], axis=1)
        halves.append(jnp.transpose(unfolded.reshape(COLS * PIECE, LANES))[:B])
    right = jnp.concatenate([right_ref[...], jnp.concatenate(halves, axis=1)], axis=0)
    out_ref[...] = a_ref[...] - dot(left, right)


def call(kernel, *shapes, smem=()):
    vmem = pl.BlockSpec(memory_space=pltpu.VMEM)
    specs = [
        pl.BlockSpec(memory_space=pltpu.SMEM) if k in smem else vmem for k in range(len(shapes))
    ]
    return pl.pallas_call(
        kernel,
        out_shape=list(shapes),
        out_specs=specs,
        compiler_params=pltpu.CompilerParams(vmem_limit_bytes=32 * 1024 * 1024),
    )


def array(*shape, dtype=jnp.float32):
    return jax.ShapeDtypeStruct(shape, dtype)


def spread(strip):
    strip = lax.optimization_barrier(jnp.where(lax.axis_index("row") == 0, strip, 0.0))
    for pairs in (
        [(0, 16)],
        [(0, 8), (16, 24)],
        [(8 * x, 8 * x + 2) for x in range(4)],
        [(8 * x + z, 8 * x + (z + 2 if z else 6)) for x in range(4) for z in (0, 2)],
        [(k, k + 1) for k in range(0, ROWS, 2)],
    ):
        strip = strip + lax.ppermute(strip, "row", pairs)
    return strip


def on_device(matrix):
    strip = spread(matrix[:B, :])
    (sent,) = call(partial_kernel, array(COLS, 2 * PIECE, LANES))(matrix, strip)
    panel = lax.all_to_all(sent, "col", 0, 0)
    sent, piece, gram = call(
        sum_kernel, array(ROWS, PIECE // 2, LANES), array(PIECE, LANES), array(16, LANES)
    )(panel)
    mix, vectors, right, flag = call(
        factor_kernel,
        array(3, LANES, LANES),
        array(2 * B, B),
        array(B, matrix.shape[1]),
        array(8, LANES),
    )(gram, strip)
    got = lax.all_to_all(sent, "row", 0, 0)
    (sent,) = call(inner_kernel, array(COLS, 3 * PIECE // 2, LANES))(
        got, panel, piece, mix, vectors, flag
    )
    got = lax.all_to_all(sent, "col", 0, 0)
    fast, fine = call(
        update_kernel, array(*matrix.shape), array(1, 1, dtype=jnp.int32), smem=(1,)
    )(matrix, got, right)
    return lax.cond(fine[0, 0] > 0, lambda: fast, lambda: general_path(matrix, strip))


def solution(mesh):
    return jax.shard_map(
        on_device,
        mesh=mesh,
        in_specs=(P("row", "col"),),
        out_specs=P("row", "col"),
        check_vma=False,
    )
```

```python
import jax
import jax.numpy as jnp
from jax import lax
from jax.experimental import pallas as pl
from jax.experimental.pallas import tpu as pltpu
from jax.sharding import PartitionSpec as P

B = 32
ROWS = 32
COLS = 16
PIECE = 16
LANES = 128
EPS = 1e-06
AMPLIFY_MAX = 16.0
GRAM_MIN = 1e-06
GRAM_MAX = 1e08
VALUE_MAX = 1e12
MIXED_MAX = 1e08
FINITE_MAX = 3e38

HIGHEST = lax.Precision.HIGHEST


def gather(shard, axis, count):
    return lax.all_to_all(jnp.broadcast_to(shard[None], (count, *shard.shape)), axis, 0, 0)


def householder(panel_cols):
    count = panel_cols.shape[0]
    width = panel_cols.shape[1]
    rows_at = jnp.arange(count, dtype=jnp.int32)

    def sweep(column_at, carried):
        working, reflectors = carried
        column = lax.dynamic_slice_in_dim(working, column_at, 1, 1)[:, 0]
        pivot = width + column_at
        below = jnp.where(rows_at >= pivot, column, 0.0)
        col_norm = jnp.sqrt(jnp.sum(below * below))
        pivot_value = lax.dynamic_slice_in_dim(column, pivot, 1, 0)[0]
        pivot_sign = jnp.where(pivot_value >= 0.0, 1.0, -1.0)
        vector = below + jnp.where(rows_at == pivot, pivot_sign * col_norm, 0.0)
        vector = vector / jnp.sqrt(jnp.sum(vector * vector) + EPS)
        weights = jnp.dot(vector, working, precision=HIGHEST)
        working = working - 2.0 * vector[:, None] * weights[None, :]
        reflectors = lax.dynamic_update_slice_in_dim(reflectors, vector[:, None], column_at, 1)
        return (working, reflectors)

    finished, reflectors = lax.fori_loop(0, width, sweep, (panel_cols, jnp.zeros_like(panel_cols)))
    gram = jnp.dot(reflectors.T, reflectors, precision=HIGHEST)
    order = jnp.arange(width, dtype=jnp.int32)

    def extend(column_at, triangle):
        earlier = jnp.where(
            order < column_at, lax.dynamic_slice_in_dim(gram, column_at, 1, 1)[:, 0], 0.0
        )
        column = -2.0 * jnp.dot(triangle, earlier, precision=HIGHEST) + jnp.where(
            order == column_at, 2.0, 0.0
        )
        return lax.dynamic_update_slice_in_dim(triangle, column[:, None], column_at, 1)

    triangle = lax.fori_loop(0, width, extend, jnp.zeros((width, width), panel_cols.dtype))
    return (reflectors, triangle)


def general_path(matrix, strip):
    rows_dev = matrix.shape[0]
    cols_dev = matrix.shape[1]
    row_at = lax.axis_index("row")
    col_at = lax.axis_index("col")
    gathered = gather(strip[:B], "col", COLS).transpose(0, 2, 1).reshape(COLS * cols_dev, B)
    rows_at = jnp.arange(gathered.shape[0], dtype=jnp.int32)
    panel_cols = jnp.where(rows_at[:, None] >= B, gathered, 0.0)
    reflectors, triangle = householder(panel_cols)
    own_rows = lax.dynamic_slice_in_dim(reflectors, row_at * rows_dev, rows_dev, 0)
    own_cols = lax.dynamic_slice_in_dim(reflectors, col_at * cols_dev, cols_dev, 0)
    row_product = jnp.sum(gather(jnp.dot(matrix, own_cols, precision=HIGHEST), "col", COLS), axis=0)
    row_scaled = jnp.dot(row_product, triangle, precision=HIGHEST)
    whole = gather(row_scaled, "row", ROWS).reshape(ROWS * rows_dev, B)
    inner = jnp.dot(reflectors.T, whole, precision=HIGHEST)
    col_scaled = lax.dynamic_slice_in_dim(whole, col_at * cols_dev, cols_dev, 0)
    correction = jnp.dot(triangle.T, inner, precision=HIGHEST)
    row_coupled = row_scaled - 0.5 * jnp.dot(own_rows, correction, precision=HIGHEST)
    col_coupled = col_scaled - 0.5 * jnp.dot(own_cols, correction, precision=HIGHEST)
    left = jnp.concatenate([row_coupled, own_rows], axis=1)
    right = jnp.concatenate([own_cols, col_coupled], axis=1)
    return matrix - lax.dot_general(left, right, (((1,), (1,)), ((), ())), precision=HIGHEST)


def dot(a, b, over=((1,), (0,))):
    return lax.dot_general(
        a, b, (over, ((), ())), precision=HIGHEST, preferred_element_type=jnp.float32
    )


def dot_nt(a, b):
    return dot(a, b, ((1,), (1,)))


def dot_tn(a, b):
    return dot(a, b, ((0,), (0,)))


def iota(shape, axis):
    return lax.broadcasted_iota(jnp.int32, shape, axis)


def beyond(x, limit):
    return jnp.max(jnp.where(jnp.abs(x) <= limit, 0.0, 1.0), keepdims=True)


def fold(square):
    group = iota((8, LANES), 1) // B
    packed = square[0:8]
    for k in range(1, B // 8):
        packed = jnp.where(group == k, pltpu.roll(square[8 * k : 8 * k + 8], B * k, 1), packed)
    return packed


def unfold(packed):
    parts = [packed] + [pltpu.roll(packed, LANES - B * k, 1) for k in range(1, B // 8)]
    return jnp.concatenate(parts, axis=0)[:, :B]


def partial_kernel(a_ref, strip_ref, out_ref):
    first_col = lax.axis_index("col") == 0
    strip = strip_ref[...]
    start = jnp.where(first_col, 2 * B, 0)
    below_t = jnp.where(iota(strip.shape, 1) >= start, strip, 0.0)
    padded = jnp.concatenate([below_t, jnp.zeros((LANES - B, strip.shape[1]), jnp.float32)], axis=0)
    a = a_ref[...]
    rows = a.shape[0]
    product = dot_nt(a, padded)
    zero = jnp.zeros((B, rows), jnp.float32)
    panel = jnp.transpose(
        jnp.concatenate([zero, strip[:, :rows], strip[:, rows:], zero], axis=0)
    )
    lane = iota((rows, LANES), 1)
    piece = jnp.where(lane < B, product, panel)
    piece = jnp.where(lane >= 3 * B, pltpu.roll(a[:, :LANES], 2 * B, 1), piece)
    out_ref[:, 0:PIECE, :] = piece.reshape(COLS, PIECE, LANES)
    gram = fold(dot_nt(below_t, padded))
    gram = gram + jnp.where(beyond(piece, VALUE_MAX) > 0.0, jnp.inf, 0.0)
    corner = fold(pltpu.roll(panel[B : 2 * B], LANES - B, 1))
    out_ref[:, PIECE : PIECE + 8, :] = jnp.broadcast_to(gram[None], (COLS, 8, LANES))
    out_ref[:, PIECE + 8 : PIECE + 16, :] = jnp.broadcast_to(corner[None], (COLS, 8, LANES))


def placed(blocks):
    wide = []
    for block, quarter in blocks:
        block = jnp.concatenate([block, jnp.zeros((B, LANES - B), jnp.float32)], axis=1)
        wide.append(pltpu.roll(block, B * quarter, 1) if quarter else block)
    return jnp.concatenate(wide, axis=0)


def factor_kernel(in_ref, out_ref, own_ref, vectors_ref):
    row_at = lax.axis_index("row")
    col_at = lax.axis_index("col")
    gram = unfold(jnp.sum(in_ref[:, PIECE : PIECE + 8, :], axis=0))
    sub = iota((B, B), 0)
    lane = iota((B, B), 1)
    eye = jnp.where(sub == lane, 1.0, 0.0)

    def column(of, j):
        return jnp.broadcast_to(of[:, j : j + 1], (B, B))

    def total(x):
        return jnp.sum(x, axis=0, keepdims=True)

    work = unfold(in_ref[0, PIECE + 8 : PIECE + 16, :])
    coef = eye
    image = gram
    top = jnp.zeros((B, B), jnp.float32)
    coefs = jnp.zeros((B, B), jnp.float32)
    images = jnp.zeros((B, B), jnp.float32)
    wrong = jnp.zeros((1, B), jnp.float32)
    x_top, x_coef, x_image = column(work, 0), column(coef, 0), column(image, 0)
    for j in range(B):
        pivot = x_top[j : j + 1, :]
        norm2 = total(x_top * x_top + x_coef * x_image)
        inner = total(x_top * work + x_coef * image)
        wrong = jnp.where(norm2 > 0.0, wrong, 1.0)
        norm = norm2 * lax.rsqrt(norm2)
        scale = lax.rsqrt(2.0 * (norm2 + jnp.abs(pivot) * norm) + EPS)
        signed = jnp.where(pivot >= 0.0, norm, -norm)
        v_top = scale * jnp.where(sub == j, x_top + signed, x_top)
        v_coef = scale * x_coef
        v_image = scale * x_image
        top = jnp.where(lane == j, v_top, top)
        coefs = jnp.where(lane == j, v_coef, coefs)
        images = jnp.where(lane == j, v_image, images)
        if j + 1 < B:
            y_top, y_coef, y_image = column(work, j + 1), column(coef, j + 1), column(image, j + 1)
            near = total(x_top * y_top + x_coef * y_image)
            near = (2.0 * scale) * (near + signed * y_top[j : j + 1, :])
            twice = (2.0 * scale) * (inner + signed * work[j : j + 1, :])
            work = work - v_top * twice
            coef = coef - v_coef * twice
            image = image - v_image * twice
            x_top = jnp.where(sub > j, y_top - v_top * near, 0.0)
            x_coef = y_coef - v_coef * near
            x_image = y_image - v_image * near
    vectors = jnp.concatenate([coefs, top], axis=0)
    overlap = dot_tn(vectors, jnp.concatenate([images, top], axis=0))
    upper = jnp.where(sub < lane, overlap, 0.0)
    triangle = 2.0 * eye
    for k in range(B - 1, 0, -1):
        triangle = triangle - (2.0 * column(upper, k)) * triangle[k : k + 1, :]
    vectors_t = dot(vectors, triangle)
    vectors_ref[0] = vectors
    vectors_ref[1] = vectors_t
    diag = jnp.sum(jnp.where(sub == lane, gram, 0.0), axis=1, keepdims=True)
    growth = total(jnp.abs(coefs) * jnp.sqrt(diag))
    wrong = jnp.where(growth <= AMPLIFY_MAX, wrong, 1.0)
    outside = jnp.where((diag >= GRAM_MIN) & (diag <= GRAM_MAX), 0.0, 1.0)
    wrong = jnp.maximum(jnp.max(wrong, keepdims=True), jnp.max(outside, keepdims=True))
    wrong = jnp.maximum(wrong, beyond(vectors_t, MIXED_MAX))
    mix = placed([(vectors_t[:B], 0), (coefs, 1), (vectors_t[B:], 0), (top, 1)])
    lane = iota((PIECE, LANES), 1)
    panel = in_ref[row_at // 2, 0:PIECE, :]
    panel = jnp.where(row_at % 2 == 0, panel, pltpu.roll(panel, LANES - B, 1))
    other = pltpu.roll(in_ref[0, 0:PIECE, :], LANES - B, 1)
    at = iota((PIECE, LANES), 0) + (row_at * COLS + col_at) * PIECE
    piece = jnp.where(at < 2 * B, 0.0, panel)
    piece = jnp.where(lane < B, jnp.sum(in_ref[:, 0:PIECE, :], axis=0), piece)
    piece = jnp.where(lane >= 2 * B, other, piece)
    piece = jnp.where(lane >= 3 * B, jnp.where(at - B == lane - 3 * B, 1.0, 0.0), piece)
    piece = dot(piece, mix)
    half = PIECE // 2
    own_ref[...] = jnp.where(
        lane[:half] < 2 * B, piece[:half], pltpu.roll(piece[half:], LANES // 2, 1)
    )
    rows = PIECE // 4
    packed = piece[:rows]
    for k in (1, 2, 3):
        moved = pltpu.roll(piece, B * k, 1)[rows * k : rows * (k + 1)]
        packed = jnp.where(lane[:rows] // B == k, moved, packed)
    packed = packed + jnp.where(wrong > 0.0, jnp.inf, 0.0)
    out_ref[...] = jnp.broadcast_to(packed[None], (ROWS, rows, LANES))


def side_kernel(panel_ref, strip_ref, vectors_ref, mixed_ref, right_ref):
    first_col = lax.axis_index("col") == 0
    vectors = vectors_ref[0]
    strip = strip_ref[...]
    lane_c = iota(strip.shape, 1)
    below_t = jnp.where(lane_c >= jnp.where(first_col, 2 * B, 0), strip, 0.0)
    unit_t = jnp.where(first_col & (iota(strip.shape, 0) == lane_c - B), 1.0, 0.0)
    right_ref[...] = dot_tn(vectors, jnp.concatenate([below_t, unit_t], axis=0))
    panel = panel_ref[:, 0:PIECE, :]
    source = iota(panel.shape, 0)
    order = iota(panel.shape, 1) + lax.axis_index("col") * PIECE
    lane = iota(panel.shape, 2)
    panel = jnp.where((source == 0) & (order < 2 * B) & (lane < 2 * B), 0.0, panel)
    unit = jnp.where((source == 0) & (order - B == lane - 3 * B), 1.0, 0.0)
    panel = jnp.where(lane >= 3 * B, unit, panel).reshape(COLS * PIECE, LANES)
    vectors_t = vectors_ref[1]
    zero = jnp.zeros((B, B), jnp.float32)
    mix = placed([(zero, 0), (vectors_t[:B], 0), (vectors_t[:B], 1), (vectors_t[B:], 0)])
    mixed = dot(panel, mix)
    moved = pltpu.roll(mixed, LANES - B, 1).reshape(COLS, PIECE, LANES)
    mixed = mixed.reshape(COLS, PIECE, LANES)
    rows = PIECE // 4
    group = iota((COLS * 2 * rows, LANES), 1) // B
    packed = jnp.zeros((COLS * 2 * rows, LANES), jnp.float32)
    for k in range(4):
        at = slice(rows * k, rows * (k + 1))
        part = jnp.concatenate([mixed[:, at], moved[:, at]], axis=1).reshape(COLS * 2 * rows, LANES)
        part = pltpu.roll(part, B * k, 1) if k else part
        packed = jnp.where(group == k, part, packed)
    mixed_ref[...] = packed


def unfold_rows(block):
    flat = block.reshape(COLS * 8, LANES)
    upper = pltpu.roll(flat, LANES // 2, 1).reshape(block.shape)
    return jnp.concatenate([block, upper], axis=1).reshape(COLS * PIECE, LANES)


def inner_kernel(in_ref, own_ref, mixed_ref, out_ref, ok_ref):
    half = PIECE // 2
    got = in_ref[...]
    ok_ref[0, 0] = 1 - jnp.max(beyond(got.reshape(-1, LANES), FINITE_MAX)).astype(jnp.int32)
    pairs = got.reshape(COLS, 2, PIECE // 4, LANES)
    columns = jnp.concatenate([pairs[:, 0], pairs[:, 1]], axis=1)
    square = dot_tn(mixed_ref[...], columns.reshape(COLS * half, LANES))
    inner = square[:B]
    for k in (1, 2, 3):
        inner = inner + pltpu.roll(square[B * k : B * (k + 1)], LANES - B * k, 1)
    out_ref[:, 0:half, :] = jnp.broadcast_to(own_ref[...][None], (COLS, half, LANES))
    out_ref[:, half : 2 * half, :] = columns
    out_ref[:, 2 * half : 3 * half, :] = jnp.broadcast_to(fold(inner)[None], (COLS, half, LANES))


def update_kernel(a_ref, in_ref, right_ref, out_ref):
    half = PIECE // 2
    inner = unfold(jnp.sum(in_ref[:, 2 * half : 3 * half, :], axis=0))
    shift = 0.5 * (inner + jnp.transpose(inner))
    left = unfold_rows(in_ref[:, 0:half, :])[:, : 2 * B]
    zero = jnp.zeros((B, B), jnp.float32)
    shift = jnp.concatenate([zero, shift], axis=0)
    shift = jnp.concatenate([shift, jnp.zeros((2 * B, B), jnp.float32)], axis=1)
    left = left - dot(left, shift)
    flat = in_ref[:, half : 2 * half, :].reshape(COLS * half, LANES)
    quarter = [flat] + [pltpu.roll(flat, LANES - B * k, 1) for k in (1, 2, 3)]
    quarter = [part.reshape(COLS, half, LANES) for part in quarter]
    halves = []
    for k in range(2):
        at = slice(k * half // 2, (k + 1) * half // 2)
        unfolded = jnp.concatenate([part[:, at] for part in quarter], axis=1)
        halves.append(jnp.transpose(unfolded.reshape(COLS * PIECE, LANES))[:B])
    right = jnp.concatenate([right_ref[...], jnp.concatenate(halves, axis=1)], axis=0)
    out_ref[...] = a_ref[...] - dot(left, right)


def call(kernel, *shapes, smem=()):
    vmem = pl.BlockSpec(memory_space=pltpu.VMEM)
    specs = [
        pl.BlockSpec(memory_space=pltpu.SMEM) if k in smem else vmem for k in range(len(shapes))
    ]
    return pl.pallas_call(
        kernel,
        out_shape=list(shapes),
        out_specs=specs,
        compiler_params=pltpu.CompilerParams(vmem_limit_bytes=32 * 1024 * 1024),
    )


def array(*shape, dtype=jnp.float32):
    return jax.ShapeDtypeStruct(shape, dtype)


def spread(strip):
    strip = lax.optimization_barrier(jnp.where(lax.axis_index("row") == 0, strip, 0.0))
    for pairs in (
        [(0, 16)],
        [(0, 8), (16, 24)],
        [(8 * x, 8 * x + 2) for x in range(4)],
        [(8 * x + z, 8 * x + (z + 2 if z else 6)) for x in range(4) for z in (0, 2)],
        [(k, k + 1) for k in range(0, ROWS, 2)],
    ):
        strip = strip + lax.ppermute(strip, "row", pairs)
    return strip


def on_device(matrix):
    strip = spread(matrix[:B, :])
    (sent,) = call(partial_kernel, array(COLS, 2 * PIECE, LANES))(matrix, strip)
    panel = lax.all_to_all(sent, "col", 0, 0)
    sent, own, vectors = call(
        factor_kernel,
        array(ROWS, PIECE // 4, LANES),
        array(PIECE // 2, LANES),
        array(2, 2 * B, B),
    )(panel)
    mixed, right = call(side_kernel, array(LANES, LANES), array(B, matrix.shape[1]))(
        panel, strip, vectors
    )
    got = lax.all_to_all(sent, "row", 0, 0)
    sent, fine = call(
        inner_kernel,
        array(COLS, 3 * PIECE // 2, LANES),
        array(1, 1, dtype=jnp.int32),
        smem=(1,),
    )(got, own, mixed)
    got = lax.all_to_all(sent, "col", 0, 0)
    (fast,) = call(update_kernel, array(*matrix.shape))(matrix, got, right)
    return lax.cond(fine[0, 0] > 0, lambda: fast, lambda: general_path(matrix, strip))


def solution(mesh):
    return jax.shard_map(
        on_device,
        mesh=mesh,
        in_specs=(P("row", "col"),),
        out_specs=P("row", "col"),
        check_vma=False,
    )
```

```python
import jax
import jax.numpy as jnp
from jax import lax
from jax.experimental import pallas as pl
from jax.experimental.pallas import tpu as pltpu
from jax.sharding import PartitionSpec as P

B = 32
ROWS = 32
COLS = 16
PIECE = 16
LANES = 128
EPS = 1e-06
AMPLIFY_MAX = 16.0
GRAM_MIN = 1e-06
GRAM_MAX = 1e08
VALUE_MAX = 1e12
MIXED_MAX = 1e08
FINITE_MAX = 3e38

HIGHEST = lax.Precision.HIGHEST


def gather(shard, axis, count):
    return lax.all_to_all(jnp.broadcast_to(shard[None], (count, *shard.shape)), axis, 0, 0)


def householder(panel_cols):
    count = panel_cols.shape[0]
    width = panel_cols.shape[1]
    rows_at = jnp.arange(count, dtype=jnp.int32)

    def sweep(column_at, carried):
        working, reflectors = carried
        column = lax.dynamic_slice_in_dim(working, column_at, 1, 1)[:, 0]
        pivot = width + column_at
        below = jnp.where(rows_at >= pivot, column, 0.0)
        col_norm = jnp.sqrt(jnp.sum(below * below))
        pivot_value = lax.dynamic_slice_in_dim(column, pivot, 1, 0)[0]
        pivot_sign = jnp.where(pivot_value >= 0.0, 1.0, -1.0)
        vector = below + jnp.where(rows_at == pivot, pivot_sign * col_norm, 0.0)
        vector = vector / jnp.sqrt(jnp.sum(vector * vector) + EPS)
        weights = jnp.dot(vector, working, precision=HIGHEST)
        working = working - 2.0 * vector[:, None] * weights[None, :]
        reflectors = lax.dynamic_update_slice_in_dim(reflectors, vector[:, None], column_at, 1)
        return (working, reflectors)

    finished, reflectors = lax.fori_loop(0, width, sweep, (panel_cols, jnp.zeros_like(panel_cols)))
    gram = jnp.dot(reflectors.T, reflectors, precision=HIGHEST)
    order = jnp.arange(width, dtype=jnp.int32)

    def extend(column_at, triangle):
        earlier = jnp.where(
            order < column_at, lax.dynamic_slice_in_dim(gram, column_at, 1, 1)[:, 0], 0.0
        )
        column = -2.0 * jnp.dot(triangle, earlier, precision=HIGHEST) + jnp.where(
            order == column_at, 2.0, 0.0
        )
        return lax.dynamic_update_slice_in_dim(triangle, column[:, None], column_at, 1)

    triangle = lax.fori_loop(0, width, extend, jnp.zeros((width, width), panel_cols.dtype))
    return (reflectors, triangle)


def general_path(matrix, strip):
    rows_dev = matrix.shape[0]
    cols_dev = matrix.shape[1]
    row_at = lax.axis_index("row")
    col_at = lax.axis_index("col")
    gathered = gather(strip[:B], "col", COLS).transpose(0, 2, 1).reshape(COLS * cols_dev, B)
    rows_at = jnp.arange(gathered.shape[0], dtype=jnp.int32)
    panel_cols = jnp.where(rows_at[:, None] >= B, gathered, 0.0)
    reflectors, triangle = householder(panel_cols)
    own_rows = lax.dynamic_slice_in_dim(reflectors, row_at * rows_dev, rows_dev, 0)
    own_cols = lax.dynamic_slice_in_dim(reflectors, col_at * cols_dev, cols_dev, 0)
    row_product = jnp.sum(gather(jnp.dot(matrix, own_cols, precision=HIGHEST), "col", COLS), axis=0)
    row_scaled = jnp.dot(row_product, triangle, precision=HIGHEST)
    whole = gather(row_scaled, "row", ROWS).reshape(ROWS * rows_dev, B)
    inner = jnp.dot(reflectors.T, whole, precision=HIGHEST)
    col_scaled = lax.dynamic_slice_in_dim(whole, col_at * cols_dev, cols_dev, 0)
    correction = jnp.dot(triangle.T, inner, precision=HIGHEST)
    row_coupled = row_scaled - 0.5 * jnp.dot(own_rows, correction, precision=HIGHEST)
    col_coupled = col_scaled - 0.5 * jnp.dot(own_cols, correction, precision=HIGHEST)
    left = jnp.concatenate([row_coupled, own_rows], axis=1)
    right = jnp.concatenate([own_cols, col_coupled], axis=1)
    return matrix - lax.dot_general(left, right, (((1,), (1,)), ((), ())), precision=HIGHEST)


def dot(a, b, over=((1,), (0,))):
    return lax.dot_general(
        a, b, (over, ((), ())), precision=HIGHEST, preferred_element_type=jnp.float32
    )


def dot_nt(a, b):
    return dot(a, b, ((1,), (1,)))


def dot_tn(a, b):
    return dot(a, b, ((0,), (0,)))


def iota(shape, axis):
    return lax.broadcasted_iota(jnp.int32, shape, axis)


def beyond(x, limit):
    return jnp.max(jnp.where(jnp.abs(x) <= limit, 0.0, 1.0), keepdims=True)


def fold(square):
    group = iota((8, LANES), 1) // B
    packed = square[0:8]
    for k in range(1, B // 8):
        packed = jnp.where(group == k, pltpu.roll(square[8 * k : 8 * k + 8], B * k, 1), packed)
    return packed


def unfold(packed):
    parts = [packed] + [pltpu.roll(packed, LANES - B * k, 1) for k in range(1, B // 8)]
    return jnp.concatenate(parts, axis=0)[:, :B]


def partial_kernel(a_ref, strip_ref, out_ref):
    first_col = lax.axis_index("col") == 0
    strip = strip_ref[...]
    start = jnp.where(first_col, 2 * B, 0)
    below_t = jnp.where(iota(strip.shape, 1) >= start, strip, 0.0)
    padded = jnp.concatenate([below_t, jnp.zeros((LANES - B, strip.shape[1]), jnp.float32)], axis=0)
    a = a_ref[...]
    rows = a.shape[0]
    product = dot_nt(a, padded)
    zero = jnp.zeros((B, rows), jnp.float32)
    panel = jnp.transpose(
        jnp.concatenate([zero, strip[:, :rows], strip[:, rows:], zero], axis=0)
    )
    lane = iota((rows, LANES), 1)
    piece = jnp.where(lane < B, product, panel)
    piece = jnp.where(lane >= 3 * B, pltpu.roll(a[:, :LANES], 2 * B, 1), piece)
    out_ref[:, 0:PIECE, :] = piece.reshape(COLS, PIECE, LANES)
    gram = fold(dot_nt(below_t, padded))
    gram = gram + jnp.where(beyond(piece, VALUE_MAX) > 0.0, jnp.inf, 0.0)
    corner = fold(pltpu.roll(panel[B : 2 * B], LANES - B, 1))
    out_ref[:, PIECE : PIECE + 8, :] = jnp.broadcast_to(gram[None], (COLS, 8, LANES))
    out_ref[:, PIECE + 8 : PIECE + 16, :] = jnp.broadcast_to(corner[None], (COLS, 8, LANES))


def placed(blocks):
    wide = []
    for block, quarter in blocks:
        block = jnp.concatenate([block, jnp.zeros((B, LANES - B), jnp.float32)], axis=1)
        wide.append(pltpu.roll(block, B * quarter, 1) if quarter else block)
    return jnp.concatenate(wide, axis=0)


def factor_kernel(in_ref, out_ref, own_ref, vectors_ref):
    row_at = lax.axis_index("row")
    col_at = lax.axis_index("col")
    gram = unfold(jnp.sum(in_ref[:, PIECE : PIECE + 8, :], axis=0))
    sub = iota((B, B), 0)
    lane = iota((B, B), 1)
    eye = jnp.where(sub == lane, 1.0, 0.0)

    def column(of, j):
        return jnp.broadcast_to(of[:, j : j + 1], (B, B))

    def total(x):
        return jnp.sum(x, axis=0, keepdims=True)

    work = unfold(in_ref[0, PIECE + 8 : PIECE + 16, :])
    coef = eye
    image = gram
    top = jnp.zeros((B, B), jnp.float32)
    coefs = jnp.zeros((B, B), jnp.float32)
    images = jnp.zeros((B, B), jnp.float32)
    wrong = jnp.zeros((1, B), jnp.float32)
    x_top, x_coef, x_image = column(work, 0), column(coef, 0), column(image, 0)
    for j in range(B):
        pivot = x_top[j : j + 1, :]
        norm2 = total(x_top * x_top + x_coef * x_image)
        inner = total(x_top * work + x_coef * image)
        wrong = jnp.where(norm2 > 0.0, wrong, 1.0)
        norm = norm2 * lax.rsqrt(norm2)
        scale = lax.rsqrt(2.0 * (norm2 + jnp.abs(pivot) * norm) + EPS)
        signed = jnp.where(pivot >= 0.0, norm, -norm)
        v_top = scale * jnp.where(sub == j, x_top + signed, x_top)
        v_coef = scale * x_coef
        v_image = scale * x_image
        top = jnp.where(lane == j, v_top, top)
        coefs = jnp.where(lane == j, v_coef, coefs)
        images = jnp.where(lane == j, v_image, images)
        if j + 1 < B:
            y_top, y_coef, y_image = column(work, j + 1), column(coef, j + 1), column(image, j + 1)
            near = total(x_top * y_top + x_coef * y_image)
            near = (2.0 * scale) * (near + signed * y_top[j : j + 1, :])
            twice = (2.0 * scale) * (inner + signed * work[j : j + 1, :])
            work = work - v_top * twice
            coef = coef - v_coef * twice
            image = image - v_image * twice
            x_top = jnp.where(sub > j, y_top - v_top * near, 0.0)
            x_coef = y_coef - v_coef * near
            x_image = y_image - v_image * near
    vectors = jnp.concatenate([coefs, top], axis=0)
    overlap = dot_tn(vectors, jnp.concatenate([images, top], axis=0))
    upper = jnp.where(sub < lane, overlap, 0.0)
    triangle = 2.0 * eye
    for k in range(B - 1, 0, -1):
        triangle = triangle - (2.0 * column(upper, k)) * triangle[k : k + 1, :]
    vectors_t = dot(vectors, triangle)
    vectors_ref[0] = vectors
    vectors_ref[1] = vectors_t
    diag = jnp.sum(jnp.where(sub == lane, gram, 0.0), axis=1, keepdims=True)
    growth = total(jnp.abs(coefs) * jnp.sqrt(diag))
    wrong = jnp.where(growth <= AMPLIFY_MAX, wrong, 1.0)
    outside = jnp.where((diag >= GRAM_MIN) & (diag <= GRAM_MAX), 0.0, 1.0)
    wrong = jnp.maximum(jnp.max(wrong, keepdims=True), jnp.max(outside, keepdims=True))
    wrong = jnp.maximum(wrong, beyond(vectors_t, MIXED_MAX))
    mix = placed([(vectors_t[:B], 0), (coefs, 1), (vectors_t[B:], 0), (top, 1)])
    lane = iota((PIECE, LANES), 1)
    panel = in_ref[row_at // 2, 0:PIECE, :]
    panel = jnp.where(row_at % 2 == 0, panel, pltpu.roll(panel, LANES - B, 1))
    other = pltpu.roll(in_ref[0, 0:PIECE, :], LANES - B, 1)
    at = iota((PIECE, LANES), 0) + (row_at * COLS + col_at) * PIECE
    piece = jnp.where(at < 2 * B, 0.0, panel)
    piece = jnp.where(lane < B, jnp.sum(in_ref[:, 0:PIECE, :], axis=0), piece)
    piece = jnp.where(lane >= 2 * B, other, piece)
    piece = jnp.where(lane >= 3 * B, jnp.where(at - B == lane - 3 * B, 1.0, 0.0), piece)
    piece = dot(piece, mix)
    half = PIECE // 2
    own_ref[...] = jnp.where(
        lane[:half] < 2 * B, piece[:half], pltpu.roll(piece[half:], LANES // 2, 1)
    )
    rows = PIECE // 4
    packed = piece[:rows]
    for k in (1, 2, 3):
        moved = pltpu.roll(piece, B * k, 1)[rows * k : rows * (k + 1)]
        packed = jnp.where(lane[:rows] // B == k, moved, packed)
    packed = packed + jnp.where(wrong > 0.0, jnp.inf, 0.0)
    out_ref[...] = jnp.broadcast_to(packed[None], (ROWS, rows, LANES))


def side_kernel(panel_ref, strip_ref, vectors_ref, mixed_ref, right_ref):
    first_col = lax.axis_index("col") == 0
    vectors = vectors_ref[0]
    strip = strip_ref[...]
    lane_c = iota(strip.shape, 1)
    below_t = jnp.where(lane_c >= jnp.where(first_col, 2 * B, 0), strip, 0.0)
    unit_t = jnp.where(first_col & (iota(strip.shape, 0) == lane_c - B), 1.0, 0.0)
    right_ref[...] = dot_tn(vectors, jnp.concatenate([below_t, unit_t], axis=0))
    panel = panel_ref[:, 0:PIECE, :]
    source = iota(panel.shape, 0)
    order = iota(panel.shape, 1) + lax.axis_index("col") * PIECE
    lane = iota(panel.shape, 2)
    panel = jnp.where((source == 0) & (order < 2 * B) & (lane < 2 * B), 0.0, panel)
    unit = jnp.where((source == 0) & (order - B == lane - 3 * B), 1.0, 0.0)
    panel = jnp.where(lane >= 3 * B, unit, panel).reshape(COLS * PIECE, LANES)
    vectors_t = vectors_ref[1]
    zero = jnp.zeros((B, B), jnp.float32)
    mix = placed([(zero, 0), (vectors_t[:B], 0), (vectors_t[:B], 1), (vectors_t[B:], 0)])
    mixed = dot(panel, mix)
    moved = pltpu.roll(mixed, LANES - B, 1).reshape(COLS, PIECE, LANES)
    mixed = mixed.reshape(COLS, PIECE, LANES)
    rows = PIECE // 4
    group = iota((COLS * 2 * rows, LANES), 1) // B
    packed = jnp.zeros((COLS * 2 * rows, LANES), jnp.float32)
    for k in range(4):
        at = slice(rows * k, rows * (k + 1))
        part = jnp.concatenate([mixed[:, at], moved[:, at]], axis=1).reshape(COLS * 2 * rows, LANES)
        part = pltpu.roll(part, B * k, 1) if k else part
        packed = jnp.where(group == k, part, packed)
    mixed_ref[...] = packed


def unfold_rows(block):
    flat = block.reshape(COLS * 8, LANES)
    upper = pltpu.roll(flat, LANES // 2, 1).reshape(block.shape)
    return jnp.concatenate([block, upper], axis=1).reshape(COLS * PIECE, LANES)


def inner_kernel(in_ref, own_ref, mixed_ref, out_ref, ok_ref):
    half = PIECE // 2
    got = in_ref[...]
    ok_ref[0, 0] = 1 - jnp.max(beyond(got.reshape(-1, LANES), FINITE_MAX)).astype(jnp.int32)
    pairs = got.reshape(COLS, 2, PIECE // 4, LANES)
    columns = jnp.concatenate([pairs[:, 0], pairs[:, 1]], axis=1)
    square = dot_tn(mixed_ref[...], columns.reshape(COLS * half, LANES))
    inner = square[:B]
    for k in (1, 2, 3):
        inner = inner + pltpu.roll(square[B * k : B * (k + 1)], LANES - B * k, 1)
    out_ref[:, 0:half, :] = jnp.broadcast_to(own_ref[...][None], (COLS, half, LANES))
    out_ref[:, half : 2 * half, :] = columns
    out_ref[:, 2 * half : 3 * half, :] = jnp.broadcast_to(fold(inner)[None], (COLS, half, LANES))


def update_kernel(a_ref, in_ref, right_ref, out_ref):
    half = PIECE // 2
    inner = unfold(jnp.sum(in_ref[:, 2 * half : 3 * half, :], axis=0))
    shift = 0.5 * (inner + jnp.transpose(inner))
    left = unfold_rows(in_ref[:, 0:half, :])[:, : 2 * B]
    zero = jnp.zeros((B, B), jnp.float32)
    shift = jnp.concatenate([zero, shift], axis=0)
    shift = jnp.concatenate([shift, jnp.zeros((2 * B, B), jnp.float32)], axis=1)
    left = left - dot(left, shift)
    flat = in_ref[:, half : 2 * half, :].reshape(COLS * half, LANES)
    quarter = [flat] + [pltpu.roll(flat, LANES - B * k, 1) for k in (1, 2, 3)]
    quarter = [part.reshape(COLS, half, LANES) for part in quarter]
    halves = []
    for k in range(2):
        at = slice(k * half // 2, (k + 1) * half // 2)
        unfolded = jnp.concatenate([part[:, at] for part in quarter], axis=1)
        halves.append(jnp.transpose(unfolded.reshape(COLS * PIECE, LANES))[:B])
    right = jnp.concatenate([right_ref[...], jnp.concatenate(halves, axis=1)], axis=0)
    out_ref[...] = a_ref[...] - dot(left, right)


def call(kernel, *shapes, smem=()):
    vmem = pl.BlockSpec(memory_space=pltpu.VMEM)
    specs = [
        pl.BlockSpec(memory_space=pltpu.SMEM) if k in smem else vmem for k in range(len(shapes))
    ]
    return pl.pallas_call(
        kernel,
        out_shape=list(shapes),
        out_specs=specs,
        compiler_params=pltpu.CompilerParams(vmem_limit_bytes=32 * 1024 * 1024),
    )


def array(*shape, dtype=jnp.float32):
    return jax.ShapeDtypeStruct(shape, dtype)


def spread(strip):
    strip = lax.optimization_barrier(jnp.where(lax.axis_index("row") == 0, strip, 0.0))
    chips = [(8 * x + core) for x in range(4) for core in range(2)]
    for pairs in (
        [(0, 16)],
        [(0, 8), (16, 24)],
        [(8 * x, 8 * x + 1) for x in range(4)],
        [(k, k + 2) for k in chips],
        [(k + z, k + (z + 2 if z else 6)) for k in chips for z in (0, 2)],
    ):
        strip = strip + lax.ppermute(strip, "row", pairs)
    return strip


def on_device(matrix):
    strip = spread(matrix[:B, :])
    (sent,) = call(partial_kernel, array(COLS, 2 * PIECE, LANES))(matrix, strip)
    panel = lax.all_to_all(sent, "col", 0, 0)
    sent, own, vectors = call(
        factor_kernel,
        array(ROWS, PIECE // 4, LANES),
        array(PIECE // 2, LANES),
        array(2, 2 * B, B),
    )(panel)
    mixed, right = call(side_kernel, array(LANES, LANES), array(B, matrix.shape[1]))(
        panel, strip, vectors
    )
    got = lax.all_to_all(sent, "row", 0, 0)
    sent, fine = call(
        inner_kernel,
        array(COLS, 3 * PIECE // 2, LANES),
        array(1, 1, dtype=jnp.int32),
        smem=(1,),
    )(got, own, mixed)
    got = lax.all_to_all(sent, "col", 0, 0)
    (fast,) = call(update_kernel, array(*matrix.shape))(matrix, got, right)
    return lax.cond(fine[0, 0] > 0, lambda: fast, lambda: general_path(matrix, strip))


def solution(mesh):
    return jax.shard_map(
        on_device,
        mesh=mesh,
        in_specs=(P("row", "col"),),
        out_specs=P("row", "col"),
        check_vma=False,
    )
```

```python
import jax
import jax.numpy as jnp
from jax import lax
from jax.experimental import pallas as pl
from jax.experimental.pallas import tpu as pltpu
from jax.sharding import PartitionSpec as P

B = 32
ROWS = 32
COLS = 16
PIECE = 16
LANES = 128
EPS = 1e-06
AMPLIFY_MAX = 16.0
GRAM_MIN = 1e-06
GRAM_MAX = 1e08
VALUE_MAX = 1e12
MIXED_MAX = 1e08
FINITE_MAX = 3e38

HIGHEST = lax.Precision.HIGHEST


def gather(shard, axis, count):
    return lax.all_to_all(jnp.broadcast_to(shard[None], (count, *shard.shape)), axis, 0, 0)


def householder(panel_cols):
    count = panel_cols.shape[0]
    width = panel_cols.shape[1]
    rows_at = jnp.arange(count, dtype=jnp.int32)

    def sweep(column_at, carried):
        working, reflectors = carried
        column = lax.dynamic_slice_in_dim(working, column_at, 1, 1)[:, 0]
        pivot = width + column_at
        below = jnp.where(rows_at >= pivot, column, 0.0)
        col_norm = jnp.sqrt(jnp.sum(below * below))
        pivot_value = lax.dynamic_slice_in_dim(column, pivot, 1, 0)[0]
        pivot_sign = jnp.where(pivot_value >= 0.0, 1.0, -1.0)
        vector = below + jnp.where(rows_at == pivot, pivot_sign * col_norm, 0.0)
        vector = vector / jnp.sqrt(jnp.sum(vector * vector) + EPS)
        weights = jnp.dot(vector, working, precision=HIGHEST)
        working = working - 2.0 * vector[:, None] * weights[None, :]
        reflectors = lax.dynamic_update_slice_in_dim(reflectors, vector[:, None], column_at, 1)
        return (working, reflectors)

    finished, reflectors = lax.fori_loop(0, width, sweep, (panel_cols, jnp.zeros_like(panel_cols)))
    gram = jnp.dot(reflectors.T, reflectors, precision=HIGHEST)
    order = jnp.arange(width, dtype=jnp.int32)

    def extend(column_at, triangle):
        earlier = jnp.where(
            order < column_at, lax.dynamic_slice_in_dim(gram, column_at, 1, 1)[:, 0], 0.0
        )
        column = -2.0 * jnp.dot(triangle, earlier, precision=HIGHEST) + jnp.where(
            order == column_at, 2.0, 0.0
        )
        return lax.dynamic_update_slice_in_dim(triangle, column[:, None], column_at, 1)

    triangle = lax.fori_loop(0, width, extend, jnp.zeros((width, width), panel_cols.dtype))
    return (reflectors, triangle)


def general_path(matrix, strip):
    rows_dev = matrix.shape[0]
    cols_dev = matrix.shape[1]
    row_at = lax.axis_index("row")
    col_at = lax.axis_index("col")
    gathered = gather(strip[:B], "col", COLS).transpose(0, 2, 1).reshape(COLS * cols_dev, B)
    rows_at = jnp.arange(gathered.shape[0], dtype=jnp.int32)
    panel_cols = jnp.where(rows_at[:, None] >= B, gathered, 0.0)
    reflectors, triangle = householder(panel_cols)
    own_rows = lax.dynamic_slice_in_dim(reflectors, row_at * rows_dev, rows_dev, 0)
    own_cols = lax.dynamic_slice_in_dim(reflectors, col_at * cols_dev, cols_dev, 0)
    row_product = jnp.sum(gather(jnp.dot(matrix, own_cols, precision=HIGHEST), "col", COLS), axis=0)
    row_scaled = jnp.dot(row_product, triangle, precision=HIGHEST)
    whole = gather(row_scaled, "row", ROWS).reshape(ROWS * rows_dev, B)
    inner = jnp.dot(reflectors.T, whole, precision=HIGHEST)
    col_scaled = lax.dynamic_slice_in_dim(whole, col_at * cols_dev, cols_dev, 0)
    correction = jnp.dot(triangle.T, inner, precision=HIGHEST)
    row_coupled = row_scaled - 0.5 * jnp.dot(own_rows, correction, precision=HIGHEST)
    col_coupled = col_scaled - 0.5 * jnp.dot(own_cols, correction, precision=HIGHEST)
    left = jnp.concatenate([row_coupled, own_rows], axis=1)
    right = jnp.concatenate([own_cols, col_coupled], axis=1)
    return matrix - lax.dot_general(left, right, (((1,), (1,)), ((), ())), precision=HIGHEST)


def dot(a, b, over=((1,), (0,))):
    return lax.dot_general(
        a, b, (over, ((), ())), precision=HIGHEST, preferred_element_type=jnp.float32
    )


def dot_nt(a, b):
    return dot(a, b, ((1,), (1,)))


def dot_tn(a, b):
    return dot(a, b, ((0,), (0,)))


def iota(shape, axis):
    return lax.broadcasted_iota(jnp.int32, shape, axis)


def beyond(x, limit):
    return jnp.max(jnp.where(jnp.abs(x) <= limit, 0.0, 1.0), keepdims=True)


def fold(square):
    group = iota((8, LANES), 1) // B
    packed = square[0:8]
    for k in range(1, B // 8):
        packed = jnp.where(group == k, pltpu.roll(square[8 * k : 8 * k + 8], B * k, 1), packed)
    return packed


def unfold(packed):
    parts = [packed] + [pltpu.roll(packed, LANES - B * k, 1) for k in range(1, B // 8)]
    return jnp.concatenate(parts, axis=0)[:, :B]


def partial_kernel(a_ref, strip_ref, out_ref):
    first_col = lax.axis_index("col") == 0
    strip = strip_ref[...]
    start = jnp.where(first_col, 2 * B, 0)
    below_t = jnp.where(iota(strip.shape, 1) >= start, strip, 0.0)
    padded = jnp.concatenate([below_t, jnp.zeros((LANES - B, strip.shape[1]), jnp.float32)], axis=0)
    a = a_ref[...]
    rows = a.shape[0]
    product = dot_nt(a, padded)
    zero = jnp.zeros((B, rows), jnp.float32)
    panel = jnp.transpose(
        jnp.concatenate([zero, strip[:, :rows], strip[:, rows:], zero], axis=0)
    )
    lane = iota((rows, LANES), 1)
    piece = jnp.where(lane < B, product, panel)
    piece = jnp.where(lane >= 3 * B, pltpu.roll(a[:, :LANES], 2 * B, 1), piece)
    out_ref[:, 0:PIECE, :] = piece.reshape(COLS, PIECE, LANES)
    gram = fold(dot_nt(below_t, padded))
    gram = gram + jnp.where(beyond(piece, VALUE_MAX) > 0.0, jnp.inf, 0.0)
    corner = fold(pltpu.roll(panel[B : 2 * B], LANES - B, 1))
    out_ref[:, PIECE : PIECE + 8, :] = jnp.broadcast_to(gram[None], (COLS, 8, LANES))
    out_ref[:, PIECE + 8 : PIECE + 16, :] = jnp.broadcast_to(corner[None], (COLS, 8, LANES))


def placed(blocks):
    wide = []
    for block, quarter in blocks:
        block = jnp.concatenate([block, jnp.zeros((B, LANES - B), jnp.float32)], axis=1)
        wide.append(pltpu.roll(block, B * quarter, 1) if quarter else block)
    return jnp.concatenate(wide, axis=0)


def factor_kernel(in_ref, out_ref, own_ref, vectors_ref):
    row_at = lax.axis_index("row")
    col_at = lax.axis_index("col")
    gram = unfold(jnp.sum(in_ref[:, PIECE : PIECE + 8, :], axis=0))
    sub = iota((B, B), 0)
    lane = iota((B, B), 1)
    eye = jnp.where(sub == lane, 1.0, 0.0)

    def column(of, j):
        return jnp.broadcast_to(of[:, j : j + 1], (B, B))

    def total(x):
        return jnp.sum(x, axis=0, keepdims=True)

    work = unfold(in_ref[0, PIECE + 8 : PIECE + 16, :])
    coef = eye
    image = gram
    top = jnp.zeros((B, B), jnp.float32)
    coefs = jnp.zeros((B, B), jnp.float32)
    images = jnp.zeros((B, B), jnp.float32)
    wrong = jnp.zeros((1, B), jnp.float32)
    x_top, x_coef, x_image = column(work, 0), column(coef, 0), column(image, 0)
    for j in range(B):
        pivot = x_top[j : j + 1, :]
        norm2 = total(x_top * x_top + x_coef * x_image)
        inner = total(x_top * work + x_coef * image)
        wrong = jnp.where(norm2 > 0.0, wrong, 1.0)
        norm = norm2 * lax.rsqrt(norm2)
        scale = lax.rsqrt(2.0 * (norm2 + jnp.abs(pivot) * norm) + EPS)
        signed = jnp.where(pivot >= 0.0, norm, -norm)
        v_top = scale * jnp.where(sub == j, x_top + signed, x_top)
        v_coef = scale * x_coef
        v_image = scale * x_image
        top = jnp.where(lane == j, v_top, top)
        coefs = jnp.where(lane == j, v_coef, coefs)
        images = jnp.where(lane == j, v_image, images)
        if j + 1 < B:
            y_top, y_coef, y_image = column(work, j + 1), column(coef, j + 1), column(image, j + 1)
            near = total(x_top * y_top + x_coef * y_image)
            near = (2.0 * scale) * (near + signed * y_top[j : j + 1, :])
            twice = (2.0 * scale) * (inner + signed * work[j : j + 1, :])
            work = work - v_top * twice
            coef = coef - v_coef * twice
            image = image - v_image * twice
            x_top = jnp.where(sub > j, y_top - v_top * near, 0.0)
            x_coef = y_coef - v_coef * near
            x_image = y_image - v_image * near
    vectors = jnp.concatenate([coefs, top], axis=0)
    overlap = dot_tn(vectors, jnp.concatenate([images, top], axis=0))
    upper = jnp.where(sub < lane, overlap, 0.0)
    triangle = 2.0 * eye
    for k in range(B - 1, 0, -1):
        triangle = triangle - (2.0 * column(upper, k)) * triangle[k : k + 1, :]
    vectors_t = dot(vectors, triangle)
    vectors_ref[0] = vectors
    vectors_ref[1] = vectors_t
    diag = jnp.sum(jnp.where(sub == lane, gram, 0.0), axis=1, keepdims=True)
    growth = total(jnp.abs(coefs) * jnp.sqrt(diag))
    wrong = jnp.where(growth <= AMPLIFY_MAX, wrong, 1.0)
    outside = jnp.where((diag >= GRAM_MIN) & (diag <= GRAM_MAX), 0.0, 1.0)
    wrong = jnp.maximum(jnp.max(wrong, keepdims=True), jnp.max(outside, keepdims=True))
    wrong = jnp.maximum(wrong, beyond(vectors_t, MIXED_MAX))
    mix = placed([(vectors_t[:B], 0), (coefs, 1), (vectors_t[B:], 0), (top, 1)])
    lane = iota((PIECE, LANES), 1)
    panel = in_ref[row_at // 2, 0:PIECE, :]
    panel = jnp.where(row_at % 2 == 0, panel, pltpu.roll(panel, LANES - B, 1))
    other = pltpu.roll(in_ref[0, 0:PIECE, :], LANES - B, 1)
    at = iota((PIECE, LANES), 0) + (row_at * COLS + col_at) * PIECE
    piece = jnp.where(at < 2 * B, 0.0, panel)
    piece = jnp.where(lane < B, jnp.sum(in_ref[:, 0:PIECE, :], axis=0), piece)
    piece = jnp.where(lane >= 2 * B, other, piece)
    piece = jnp.where(lane >= 3 * B, jnp.where(at - B == lane - 3 * B, 1.0, 0.0), piece)
    piece = dot(piece, mix)
    half = PIECE // 2
    own_ref[...] = jnp.where(
        lane[:half] < 2 * B, piece[:half], pltpu.roll(piece[half:], LANES // 2, 1)
    )
    rows = PIECE // 4
    packed = piece[:rows]
    for k in (1, 2, 3):
        moved = pltpu.roll(piece, B * k, 1)[rows * k : rows * (k + 1)]
        packed = jnp.where(lane[:rows] // B == k, moved, packed)
    packed = packed + jnp.where(wrong > 0.0, jnp.inf, 0.0)
    out_ref[...] = jnp.broadcast_to(packed[None], (ROWS, rows, LANES))


def side_kernel(panel_ref, strip_ref, vectors_ref, mixed_ref, right_ref):
    first_col = lax.axis_index("col") == 0
    vectors = vectors_ref[0]
    strip = strip_ref[...]
    lane_c = iota(strip.shape, 1)
    below_t = jnp.where(lane_c >= jnp.where(first_col, 2 * B, 0), strip, 0.0)
    unit_t = jnp.where(first_col & (iota(strip.shape, 0) == lane_c - B), 1.0, 0.0)
    right_ref[...] = dot_tn(vectors, jnp.concatenate([below_t, unit_t], axis=0))
    panel = panel_ref[:, 0:PIECE, :]
    source = iota(panel.shape, 0)
    order = iota(panel.shape, 1) + lax.axis_index("col") * PIECE
    lane = iota(panel.shape, 2)
    panel = jnp.where((source == 0) & (order < 2 * B) & (lane < 2 * B), 0.0, panel)
    unit = jnp.where((source == 0) & (order - B == lane - 3 * B), 1.0, 0.0)
    panel = jnp.where(lane >= 3 * B, unit, panel).reshape(COLS * PIECE, LANES)
    vectors_t = vectors_ref[1]
    zero = jnp.zeros((B, B), jnp.float32)
    mix = placed([(zero, 0), (vectors_t[:B], 0), (vectors_t[:B], 1), (vectors_t[B:], 0)])
    mixed = dot(panel, mix)
    moved = pltpu.roll(mixed, LANES - B, 1).reshape(COLS, PIECE, LANES)
    mixed = mixed.reshape(COLS, PIECE, LANES)
    rows = PIECE // 4
    group = iota((COLS * 2 * rows, LANES), 1) // B
    packed = jnp.zeros((COLS * 2 * rows, LANES), jnp.float32)
    for k in range(4):
        at = slice(rows * k, rows * (k + 1))
        part = jnp.concatenate([mixed[:, at], moved[:, at]], axis=1).reshape(COLS * 2 * rows, LANES)
        part = pltpu.roll(part, B * k, 1) if k else part
        packed = jnp.where(group == k, part, packed)
    mixed_ref[...] = packed


def unfold_rows(block):
    flat = block.reshape(COLS * 8, LANES)
    upper = pltpu.roll(flat, LANES // 2, 1).reshape(block.shape)
    return jnp.concatenate([block, upper], axis=1).reshape(COLS * PIECE, LANES)


def inner_kernel(in_ref, own_ref, mixed_ref, out_ref, ok_ref):
    half = PIECE // 2
    got = in_ref[...]
    ok_ref[0, 0] = 1 - jnp.max(beyond(got.reshape(-1, LANES), FINITE_MAX)).astype(jnp.int32)
    pairs = got.reshape(COLS, 2, PIECE // 4, LANES)
    columns = jnp.concatenate([pairs[:, 0], pairs[:, 1]], axis=1)
    square = dot_tn(mixed_ref[...], columns.reshape(COLS * half, LANES))
    inner = square[:B]
    for k in (1, 2, 3):
        inner = inner + pltpu.roll(square[B * k : B * (k + 1)], LANES - B * k, 1)
    out_ref[:, 0:half, :] = jnp.broadcast_to(own_ref[...][None], (COLS, half, LANES))
    out_ref[:, half : 2 * half, :] = columns
    out_ref[:, 2 * half : 3 * half, :] = jnp.broadcast_to(fold(inner)[None], (COLS, half, LANES))


def update_kernel(a_ref, in_ref, right_ref, out_ref):
    half = PIECE // 2
    inner = unfold(jnp.sum(in_ref[:, 2 * half : 3 * half, :], axis=0))
    shift = 0.5 * (inner + jnp.transpose(inner))
    left = unfold_rows(in_ref[:, 0:half, :])[:, : 2 * B]
    zero = jnp.zeros((B, B), jnp.float32)
    shift = jnp.concatenate([zero, shift], axis=0)
    shift = jnp.concatenate([shift, jnp.zeros((2 * B, B), jnp.float32)], axis=1)
    left = left - dot(left, shift)
    flat = in_ref[:, half : 2 * half, :].reshape(COLS * half, LANES)
    quarter = [flat] + [pltpu.roll(flat, LANES - B * k, 1) for k in (1, 2, 3)]
    quarter = [part.reshape(COLS, half, LANES) for part in quarter]
    halves = []
    for k in range(2):
        at = slice(k * half // 2, (k + 1) * half // 2)
        unfolded = jnp.concatenate([part[:, at] for part in quarter], axis=1)
        halves.append(jnp.transpose(unfolded.reshape(COLS * PIECE, LANES))[:B])
    right = jnp.concatenate([right_ref[...], jnp.concatenate(halves, axis=1)], axis=0)
    out_ref[...] = a_ref[...] - dot(left, right)


def call(kernel, *shapes, smem=()):
    vmem = pl.BlockSpec(memory_space=pltpu.VMEM)
    specs = [
        pl.BlockSpec(memory_space=pltpu.SMEM) if k in smem else vmem for k in range(len(shapes))
    ]
    return pl.pallas_call(
        kernel,
        out_shape=list(shapes),
        out_specs=specs,
        compiler_params=pltpu.CompilerParams(vmem_limit_bytes=32 * 1024 * 1024),
    )


def array(*shape, dtype=jnp.float32):
    return jax.ShapeDtypeStruct(shape, dtype)


def spread(strip):
    strip = lax.optimization_barrier(jnp.where(lax.axis_index("row") == 0, strip, 0.0))
    for pairs in (
        [(0, 16)],
        [(0, 8), (16, 24)],
        [(8 * x, 8 * x + 6) for x in range(4)],
        [(8 * x + z, 8 * x + (4 if z else 2)) for x in range(4) for z in (0, 6)],
        [(k, k + 1) for k in range(0, ROWS, 2)],
    ):
        strip = strip + lax.ppermute(strip, "row", pairs)
    return strip


def on_device(matrix):
    strip = spread(matrix[:B, :])
    (sent,) = call(partial_kernel, array(COLS, 2 * PIECE, LANES))(matrix, strip)
    panel = lax.all_to_all(sent, "col", 0, 0)
    sent, own, vectors = call(
        factor_kernel,
        array(ROWS, PIECE // 4, LANES),
        array(PIECE // 2, LANES),
        array(2, 2 * B, B),
    )(panel)
    mixed, right = call(side_kernel, array(LANES, LANES), array(B, matrix.shape[1]))(
        panel, strip, vectors
    )
    got = lax.all_to_all(sent, "row", 0, 0)
    sent, fine = call(
        inner_kernel,
        array(COLS, 3 * PIECE // 2, LANES),
        array(1, 1, dtype=jnp.int32),
        smem=(1,),
    )(got, own, mixed)
    got = lax.all_to_all(sent, "col", 0, 0)
    (fast,) = call(update_kernel, array(*matrix.shape))(matrix, got, right)
    return lax.cond(fine[0, 0] > 0, lambda: fast, lambda: general_path(matrix, strip))


def solution(mesh):
    return jax.shard_map(
        on_device,
        mesh=mesh,
        in_specs=(P("row", "col"),),
        out_specs=P("row", "col"),
        check_vma=False,
    )
```

```python
import jax
import jax.numpy as jnp
from jax import lax
from jax.experimental import pallas as pl
from jax.experimental.pallas import tpu as pltpu
from jax.sharding import PartitionSpec as P

B = 32
ROWS = 32
COLS = 16
PIECE = 16
LANES = 128
EPS = 1e-06
AMPLIFY_MAX = 16.0
GRAM_MIN = 1e-06
GRAM_MAX = 1e08
VALUE_MAX = 1e12
MIXED_MAX = 1e08
FINITE_MAX = 3e38

HIGHEST = lax.Precision.HIGHEST


def gather(shard, axis, count):
    return lax.all_to_all(jnp.broadcast_to(shard[None], (count, *shard.shape)), axis, 0, 0)


def householder(panel_cols):
    count = panel_cols.shape[0]
    width = panel_cols.shape[1]
    rows_at = jnp.arange(count, dtype=jnp.int32)

    def sweep(column_at, carried):
        working, reflectors = carried
        column = lax.dynamic_slice_in_dim(working, column_at, 1, 1)[:, 0]
        pivot = width + column_at
        below = jnp.where(rows_at >= pivot, column, 0.0)
        col_norm = jnp.sqrt(jnp.sum(below * below))
        pivot_value = lax.dynamic_slice_in_dim(column, pivot, 1, 0)[0]
        pivot_sign = jnp.where(pivot_value >= 0.0, 1.0, -1.0)
        vector = below + jnp.where(rows_at == pivot, pivot_sign * col_norm, 0.0)
        vector = vector / jnp.sqrt(jnp.sum(vector * vector) + EPS)
        weights = jnp.dot(vector, working, precision=HIGHEST)
        working = working - 2.0 * vector[:, None] * weights[None, :]
        reflectors = lax.dynamic_update_slice_in_dim(reflectors, vector[:, None], column_at, 1)
        return (working, reflectors)

    finished, reflectors = lax.fori_loop(0, width, sweep, (panel_cols, jnp.zeros_like(panel_cols)))
    gram = jnp.dot(reflectors.T, reflectors, precision=HIGHEST)
    order = jnp.arange(width, dtype=jnp.int32)

    def extend(column_at, triangle):
        earlier = jnp.where(
            order < column_at, lax.dynamic_slice_in_dim(gram, column_at, 1, 1)[:, 0], 0.0
        )
        column = -2.0 * jnp.dot(triangle, earlier, precision=HIGHEST) + jnp.where(
            order == column_at, 2.0, 0.0
        )
        return lax.dynamic_update_slice_in_dim(triangle, column[:, None], column_at, 1)

    triangle = lax.fori_loop(0, width, extend, jnp.zeros((width, width), panel_cols.dtype))
    return (reflectors, triangle)


def general_path(matrix, strip):
    rows_dev = matrix.shape[0]
    cols_dev = matrix.shape[1]
    row_at = lax.axis_index("row")
    col_at = lax.axis_index("col")
    gathered = gather(strip[:B], "col", COLS).transpose(0, 2, 1).reshape(COLS * cols_dev, B)
    rows_at = jnp.arange(gathered.shape[0], dtype=jnp.int32)
    panel_cols = jnp.where(rows_at[:, None] >= B, gathered, 0.0)
    reflectors, triangle = householder(panel_cols)
    own_rows = lax.dynamic_slice_in_dim(reflectors, row_at * rows_dev, rows_dev, 0)
    own_cols = lax.dynamic_slice_in_dim(reflectors, col_at * cols_dev, cols_dev, 0)
    row_product = jnp.sum(gather(jnp.dot(matrix, own_cols, precision=HIGHEST), "col", COLS), axis=0)
    row_scaled = jnp.dot(row_product, triangle, precision=HIGHEST)
    whole = gather(row_scaled, "row", ROWS).reshape(ROWS * rows_dev, B)
    inner = jnp.dot(reflectors.T, whole, precision=HIGHEST)
    col_scaled = lax.dynamic_slice_in_dim(whole, col_at * cols_dev, cols_dev, 0)
    correction = jnp.dot(triangle.T, inner, precision=HIGHEST)
    row_coupled = row_scaled - 0.5 * jnp.dot(own_rows, correction, precision=HIGHEST)
    col_coupled = col_scaled - 0.5 * jnp.dot(own_cols, correction, precision=HIGHEST)
    left = jnp.concatenate([row_coupled, own_rows], axis=1)
    right = jnp.concatenate([own_cols, col_coupled], axis=1)
    return matrix - lax.dot_general(left, right, (((1,), (1,)), ((), ())), precision=HIGHEST)


def dot(a, b, over=((1,), (0,))):
    return lax.dot_general(
        a, b, (over, ((), ())), precision=HIGHEST, preferred_element_type=jnp.float32
    )


def dot_nt(a, b):
    return dot(a, b, ((1,), (1,)))


def dot_tn(a, b):
    return dot(a, b, ((0,), (0,)))


def iota(shape, axis):
    return lax.broadcasted_iota(jnp.int32, shape, axis)


def beyond(x, limit):
    return jnp.max(jnp.where(jnp.abs(x) <= limit, 0.0, 1.0), keepdims=True)


def fold(square):
    group = iota((8, LANES), 1) // B
    packed = square[0:8]
    for k in range(1, B // 8):
        packed = jnp.where(group == k, pltpu.roll(square[8 * k : 8 * k + 8], B * k, 1), packed)
    return packed


def unfold(packed):
    parts = [packed] + [pltpu.roll(packed, LANES - B * k, 1) for k in range(1, B // 8)]
    return jnp.concatenate(parts, axis=0)[:, :B]


def partial_kernel(a_ref, strip_ref, out_ref):
    first_col = lax.axis_index("col") == 0
    strip = strip_ref[...]
    start = jnp.where(first_col, 2 * B, 0)
    below_t = jnp.where(iota(strip.shape, 1) >= start, strip, 0.0)
    padded = jnp.concatenate([below_t, jnp.zeros((LANES - B, strip.shape[1]), jnp.float32)], axis=0)
    a = a_ref[...]
    rows = a.shape[0]
    product = dot_nt(a, padded)
    zero = jnp.zeros((B, rows), jnp.float32)
    panel = jnp.transpose(
        jnp.concatenate([zero, strip[:, :rows], strip[:, rows:], zero], axis=0)
    )
    lane = iota((rows, LANES), 1)
    piece = jnp.where(lane < B, product, panel)
    piece = jnp.where(lane >= 3 * B, pltpu.roll(a[:, :LANES], 2 * B, 1), piece)
    out_ref[:, 0:PIECE, :] = piece.reshape(COLS, PIECE, LANES)
    gram = fold(dot_nt(below_t, padded))
    gram = gram + jnp.where(beyond(piece, VALUE_MAX) > 0.0, jnp.inf, 0.0)
    corner = fold(pltpu.roll(panel[B : 2 * B], LANES - B, 1))
    out_ref[:, PIECE : PIECE + 8, :] = jnp.broadcast_to(gram[None], (COLS, 8, LANES))
    out_ref[:, PIECE + 8 : PIECE + 16, :] = jnp.broadcast_to(corner[None], (COLS, 8, LANES))


def placed(blocks):
    wide = []
    for block, quarter in blocks:
        block = jnp.concatenate([block, jnp.zeros((B, LANES - B), jnp.float32)], axis=1)
        wide.append(pltpu.roll(block, B * quarter, 1) if quarter else block)
    return jnp.concatenate(wide, axis=0)


def factor_kernel(in_ref, out_ref, own_ref, vectors_ref):
    row_at = lax.axis_index("row")
    col_at = lax.axis_index("col")
    gram = unfold(jnp.sum(in_ref[:, PIECE : PIECE + 8, :], axis=0))
    sub = iota((B, B), 0)
    lane = iota((B, B), 1)
    eye = jnp.where(sub == lane, 1.0, 0.0)

    def column(of, j):
        return jnp.broadcast_to(of[:, j : j + 1], (B, B))

    def total(x):
        return jnp.sum(x, axis=0, keepdims=True)

    work = unfold(in_ref[0, PIECE + 8 : PIECE + 16, :])
    coef = eye
    image = gram
    top = jnp.zeros((B, B), jnp.float32)
    coefs = jnp.zeros((B, B), jnp.float32)
    images = jnp.zeros((B, B), jnp.float32)
    wrong = jnp.zeros((1, B), jnp.float32)
    x_top, x_coef, x_image = column(work, 0), column(coef, 0), column(image, 0)
    for j in range(B):
        pivot = x_top[j : j + 1, :]
        norm2 = total(x_top * x_top + x_coef * x_image)
        inner = total(x_top * work + x_coef * image)
        wrong = jnp.where(norm2 > 0.0, wrong, 1.0)
        norm = norm2 * lax.rsqrt(norm2)
        scale = lax.rsqrt(2.0 * (norm2 + jnp.abs(pivot) * norm) + EPS)
        signed = jnp.where(pivot >= 0.0, norm, -norm)
        v_top = scale * jnp.where(sub == j, x_top + signed, x_top)
        v_coef = scale * x_coef
        v_image = scale * x_image
        top = jnp.where(lane == j, v_top, top)
        coefs = jnp.where(lane == j, v_coef, coefs)
        images = jnp.where(lane == j, v_image, images)
        if j + 1 < B:
            y_top, y_coef, y_image = column(work, j + 1), column(coef, j + 1), column(image, j + 1)
            near = total(x_top * y_top + x_coef * y_image)
            near = (2.0 * scale) * (near + signed * y_top[j : j + 1, :])
            twice = (2.0 * scale) * (inner + signed * work[j : j + 1, :])
            work = work - v_top * twice
            coef = coef - v_coef * twice
            image = image - v_image * twice
            x_top = jnp.where(sub > j, y_top - v_top * near, 0.0)
            x_coef = y_coef - v_coef * near
            x_image = y_image - v_image * near
    vectors = jnp.concatenate([coefs, top], axis=0)
    overlap = dot_tn(vectors, jnp.concatenate([images, top], axis=0))
    upper = jnp.where(sub < lane, overlap, 0.0)
    triangle = 2.0 * eye
    for k in range(B - 1, 0, -1):
        triangle = triangle - (2.0 * column(upper, k)) * triangle[k : k + 1, :]
    vectors_t = dot(vectors, triangle)
    vectors_ref[0] = vectors
    vectors_ref[1] = vectors_t
    diag = jnp.sum(jnp.where(sub == lane, gram, 0.0), axis=1, keepdims=True)
    growth = total(jnp.abs(coefs) * jnp.sqrt(diag))
    wrong = jnp.where(growth <= AMPLIFY_MAX, wrong, 1.0)
    outside = jnp.where((diag >= GRAM_MIN) & (diag <= GRAM_MAX), 0.0, 1.0)
    wrong = jnp.maximum(jnp.max(wrong, keepdims=True), jnp.max(outside, keepdims=True))
    wrong = jnp.maximum(wrong, beyond(vectors_t, MIXED_MAX))
    mix = placed([(vectors_t[:B], 0), (coefs, 1), (vectors_t[B:], 0), (top, 1)])
    lane = iota((PIECE, LANES), 1)
    panel = in_ref[row_at // 2, 0:PIECE, :]
    panel = jnp.where(row_at % 2 == 0, panel, pltpu.roll(panel, LANES - B, 1))
    other = pltpu.roll(in_ref[0, 0:PIECE, :], LANES - B, 1)
    at = iota((PIECE, LANES), 0) + (row_at * COLS + col_at) * PIECE
    piece = jnp.where(at < 2 * B, 0.0, panel)
    piece = jnp.where(lane < B, jnp.sum(in_ref[:, 0:PIECE, :], axis=0), piece)
    piece = jnp.where(lane >= 2 * B, other, piece)
    piece = jnp.where(lane >= 3 * B, jnp.where(at - B == lane - 3 * B, 1.0, 0.0), piece)
    piece = dot(piece, mix)
    half = PIECE // 2
    own_ref[...] = jnp.where(
        lane[:half] < 2 * B, piece[:half], pltpu.roll(piece[half:], LANES // 2, 1)
    )
    rows = PIECE // 4
    packed = piece[:rows]
    for k in (1, 2, 3):
        moved = pltpu.roll(piece, B * k, 1)[rows * k : rows * (k + 1)]
        packed = jnp.where(lane[:rows] // B == k, moved, packed)
    packed = packed + jnp.where(wrong > 0.0, jnp.inf, 0.0)
    out_ref[...] = jnp.broadcast_to(packed[None], (ROWS, rows, LANES))


def side_kernel(panel_ref, strip_ref, vectors_ref, mixed_ref, right_ref):
    first_col = lax.axis_index("col") == 0
    vectors = vectors_ref[0]
    strip = strip_ref[...]
    lane_c = iota(strip.shape, 1)
    below_t = jnp.where(lane_c >= jnp.where(first_col, 2 * B, 0), strip, 0.0)
    unit_t = jnp.where(first_col & (iota(strip.shape, 0) == lane_c - B), 1.0, 0.0)
    right_ref[...] = dot_tn(vectors, jnp.concatenate([below_t, unit_t], axis=0))
    panel = panel_ref[:, 0:PIECE, :]
    source = iota(panel.shape, 0)
    order = iota(panel.shape, 1) + lax.axis_index("col") * PIECE
    lane = iota(panel.shape, 2)
    panel = jnp.where((source == 0) & (order < 2 * B) & (lane < 2 * B), 0.0, panel)
    unit = jnp.where((source == 0) & (order - B == lane - 3 * B), 1.0, 0.0)
    panel = jnp.where(lane >= 3 * B, unit, panel).reshape(COLS * PIECE, LANES)
    vectors_t = vectors_ref[1]
    zero = jnp.zeros((B, B), jnp.float32)
    mix = placed([(zero, 0), (vectors_t[:B], 0), (vectors_t[:B], 1), (vectors_t[B:], 0)])
    mixed = dot(panel, mix)
    moved = pltpu.roll(mixed, LANES - B, 1).reshape(COLS, PIECE, LANES)
    mixed = mixed.reshape(COLS, PIECE, LANES)
    rows = PIECE // 4
    group = iota((COLS * 2 * rows, LANES), 1) // B
    packed = jnp.zeros((COLS * 2 * rows, LANES), jnp.float32)
    for k in range(4):
        at = slice(rows * k, rows * (k + 1))
        part = jnp.concatenate([mixed[:, at], moved[:, at]], axis=1).reshape(COLS * 2 * rows, LANES)
        part = pltpu.roll(part, B * k, 1) if k else part
        packed = jnp.where(group == k, part, packed)
    mixed_ref[...] = packed


def unfold_rows(block):
    flat = block.reshape(COLS * 8, LANES)
    upper = pltpu.roll(flat, LANES // 2, 1).reshape(block.shape)
    return jnp.concatenate([block, upper], axis=1).reshape(COLS * PIECE, LANES)


def inner_kernel(in_ref, own_ref, mixed_ref, out_ref, ok_ref):
    half = PIECE // 2
    got = in_ref[...]
    ok_ref[0, 0] = 1 - jnp.max(beyond(got.reshape(-1, LANES), FINITE_MAX)).astype(jnp.int32)
    pairs = got.reshape(COLS, 2, PIECE // 4, LANES)
    columns = jnp.concatenate([pairs[:, 0], pairs[:, 1]], axis=1)
    square = dot_tn(mixed_ref[...], columns.reshape(COLS * half, LANES))
    inner = square[:B]
    for k in (1, 2, 3):
        inner = inner + pltpu.roll(square[B * k : B * (k + 1)], LANES - B * k, 1)
    out_ref[:, 0:half, :] = jnp.broadcast_to(own_ref[...][None], (COLS, half, LANES))
    out_ref[:, half : 2 * half, :] = columns
    out_ref[:, 2 * half : 3 * half, :] = jnp.broadcast_to(fold(inner)[None], (COLS, half, LANES))


def update_kernel(a_ref, in_ref, right_ref, out_ref):
    half = PIECE // 2
    inner = unfold(jnp.sum(in_ref[:, 2 * half : 3 * half, :], axis=0))
    shift = 0.5 * (inner + jnp.transpose(inner))
    left = unfold_rows(in_ref[:, 0:half, :])[:, : 2 * B]
    zero = jnp.zeros((B, B), jnp.float32)
    shift = jnp.concatenate([zero, shift], axis=0)
    shift = jnp.concatenate([shift, jnp.zeros((2 * B, B), jnp.float32)], axis=1)
    left = left - dot(left, shift)
    flat = in_ref[:, half : 2 * half, :].reshape(COLS * half, LANES)
    quarter = [flat] + [pltpu.roll(flat, LANES - B * k, 1) for k in (1, 2, 3)]
    quarter = [part.reshape(COLS, half, LANES) for part in quarter]
    halves = []
    for k in range(2):
        at = slice(k * half // 2, (k + 1) * half // 2)
        unfolded = jnp.concatenate([part[:, at] for part in quarter], axis=1)
        halves.append(jnp.transpose(unfolded.reshape(COLS * PIECE, LANES))[:B])
    right = jnp.concatenate([right_ref[...], jnp.concatenate(halves, axis=1)], axis=0)
    out_ref[...] = a_ref[...] - dot(left, right)


def call(kernel, *shapes, smem=()):
    vmem = pl.BlockSpec(memory_space=pltpu.VMEM)
    specs = [
        pl.BlockSpec(memory_space=pltpu.SMEM) if k in smem else vmem for k in range(len(shapes))
    ]
    return pl.pallas_call(
        kernel,
        out_shape=list(shapes),
        out_specs=specs,
        compiler_params=pltpu.CompilerParams(vmem_limit_bytes=32 * 1024 * 1024),
    )


def array(*shape, dtype=jnp.float32):
    return jax.ShapeDtypeStruct(shape, dtype)


def spread(strip):
    strip = lax.optimization_barrier(jnp.where(lax.axis_index("row") == 0, strip, 0.0))
    first, second = [], []
    for x in range(4):
        for col in range(COLS):
            near, far = (2, 6) if col < COLS // 2 else (6, 2)
            first.append((8 * x * COLS + col, (8 * x + near) * COLS + col))
            second.append(((8 * x + near) * COLS + col, (8 * x + 4) * COLS + col))
            second.append((8 * x * COLS + col, (8 * x + far) * COLS + col))
    for axes, pairs in (
        ("row", [(0, 16)]),
        ("row", [(0, 8), (16, 24)]),
        (("row", "col"), first),
        (("row", "col"), second),
        ("row", [(k, k + 1) for k in range(0, ROWS, 2)]),
    ):
        strip = strip + lax.ppermute(strip, axes, pairs)
    return strip


def on_device(matrix):
    strip = spread(matrix[:B, :])
    (sent,) = call(partial_kernel, array(COLS, 2 * PIECE, LANES))(matrix, strip)
    panel = lax.all_to_all(sent, "col", 0, 0)
    sent, own, vectors = call(
        factor_kernel,
        array(ROWS, PIECE // 4, LANES),
        array(PIECE // 2, LANES),
        array(2, 2 * B, B),
    )(panel)
    mixed, right = call(side_kernel, array(LANES, LANES), array(B, matrix.shape[1]))(
        panel, strip, vectors
    )
    got = lax.all_to_all(sent, "row", 0, 0)
    sent, fine = call(
        inner_kernel,
        array(COLS, 3 * PIECE // 2, LANES),
        array(1, 1, dtype=jnp.int32),
        smem=(1,),
    )(got, own, mixed)
    got = lax.all_to_all(sent, "col", 0, 0)
    (fast,) = call(update_kernel, array(*matrix.shape))(matrix, got, right)
    return lax.cond(fine[0, 0] > 0, lambda: fast, lambda: general_path(matrix, strip))


def solution(mesh):
    return jax.shard_map(
        on_device,
        mesh=mesh,
        in_specs=(P("row", "col"),),
        out_specs=P("row", "col"),
        check_vma=False,
    )
```

```python
import jax
import jax.numpy as jnp
from jax import lax
from jax.experimental import pallas as pl
from jax.experimental.pallas import tpu as pltpu
from jax.sharding import PartitionSpec as P

B = 32
ROWS = 32
COLS = 16
PIECE = 16
LANES = 128
EPS = 1e-06
AMPLIFY_MAX = 16.0
GRAM_MIN = 1e-06
GRAM_MAX = 1e08
VALUE_MAX = 1e12
MIXED_MAX = 1e08
FINITE_MAX = 3e38

HIGHEST = lax.Precision.HIGHEST


def gather(shard, axis, count):
    return lax.all_to_all(jnp.broadcast_to(shard[None], (count, *shard.shape)), axis, 0, 0)


def householder(panel_cols):
    count = panel_cols.shape[0]
    width = panel_cols.shape[1]
    rows_at = jnp.arange(count, dtype=jnp.int32)

    def sweep(column_at, carried):
        working, reflectors = carried
        column = lax.dynamic_slice_in_dim(working, column_at, 1, 1)[:, 0]
        pivot = width + column_at
        below = jnp.where(rows_at >= pivot, column, 0.0)
        col_norm = jnp.sqrt(jnp.sum(below * below))
        pivot_value = lax.dynamic_slice_in_dim(column, pivot, 1, 0)[0]
        pivot_sign = jnp.where(pivot_value >= 0.0, 1.0, -1.0)
        vector = below + jnp.where(rows_at == pivot, pivot_sign * col_norm, 0.0)
        vector = vector / jnp.sqrt(jnp.sum(vector * vector) + EPS)
        weights = jnp.dot(vector, working, precision=HIGHEST)
        working = working - 2.0 * vector[:, None] * weights[None, :]
        reflectors = lax.dynamic_update_slice_in_dim(reflectors, vector[:, None], column_at, 1)
        return (working, reflectors)

    finished, reflectors = lax.fori_loop(0, width, sweep, (panel_cols, jnp.zeros_like(panel_cols)))
    gram = jnp.dot(reflectors.T, reflectors, precision=HIGHEST)
    order = jnp.arange(width, dtype=jnp.int32)

    def extend(column_at, triangle):
        earlier = jnp.where(
            order < column_at, lax.dynamic_slice_in_dim(gram, column_at, 1, 1)[:, 0], 0.0
        )
        column = -2.0 * jnp.dot(triangle, earlier, precision=HIGHEST) + jnp.where(
            order == column_at, 2.0, 0.0
        )
        return lax.dynamic_update_slice_in_dim(triangle, column[:, None], column_at, 1)

    triangle = lax.fori_loop(0, width, extend, jnp.zeros((width, width), panel_cols.dtype))
    return (reflectors, triangle)


def general_path(matrix, strip):
    rows_dev = matrix.shape[0]
    cols_dev = matrix.shape[1]
    row_at = lax.axis_index("row")
    col_at = lax.axis_index("col")
    gathered = gather(strip[:B], "col", COLS).transpose(0, 2, 1).reshape(COLS * cols_dev, B)
    rows_at = jnp.arange(gathered.shape[0], dtype=jnp.int32)
    panel_cols = jnp.where(rows_at[:, None] >= B, gathered, 0.0)
    reflectors, triangle = householder(panel_cols)
    own_rows = lax.dynamic_slice_in_dim(reflectors, row_at * rows_dev, rows_dev, 0)
    own_cols = lax.dynamic_slice_in_dim(reflectors, col_at * cols_dev, cols_dev, 0)
    row_product = jnp.sum(gather(jnp.dot(matrix, own_cols, precision=HIGHEST), "col", COLS), axis=0)
    row_scaled = jnp.dot(row_product, triangle, precision=HIGHEST)
    whole = gather(row_scaled, "row", ROWS).reshape(ROWS * rows_dev, B)
    inner = jnp.dot(reflectors.T, whole, precision=HIGHEST)
    col_scaled = lax.dynamic_slice_in_dim(whole, col_at * cols_dev, cols_dev, 0)
    correction = jnp.dot(triangle.T, inner, precision=HIGHEST)
    row_coupled = row_scaled - 0.5 * jnp.dot(own_rows, correction, precision=HIGHEST)
    col_coupled = col_scaled - 0.5 * jnp.dot(own_cols, correction, precision=HIGHEST)
    left = jnp.concatenate([row_coupled, own_rows], axis=1)
    right = jnp.concatenate([own_cols, col_coupled], axis=1)
    return matrix - lax.dot_general(left, right, (((1,), (1,)), ((), ())), precision=HIGHEST)


def dot(a, b, over=((1,), (0,))):
    return lax.dot_general(
        a, b, (over, ((), ())), precision=HIGHEST, preferred_element_type=jnp.float32
    )


def dot_nt(a, b):
    return dot(a, b, ((1,), (1,)))


def dot_tn(a, b):
    return dot(a, b, ((0,), (0,)))


def iota(shape, axis):
    return lax.broadcasted_iota(jnp.int32, shape, axis)


def beyond(x, limit):
    return jnp.max(jnp.where(jnp.abs(x) <= limit, 0.0, 1.0), keepdims=True)


def fold(square):
    group = iota((8, LANES), 1) // B
    packed = square[0:8]
    for k in range(1, B // 8):
        packed = jnp.where(group == k, pltpu.roll(square[8 * k : 8 * k + 8], B * k, 1), packed)
    return packed


def unfold(packed):
    parts = [packed] + [pltpu.roll(packed, LANES - B * k, 1) for k in range(1, B // 8)]
    return jnp.concatenate(parts, axis=0)[:, :B]


def partial_kernel(a_ref, strip_ref, out_ref):
    first_col = lax.axis_index("col") == 0
    strip = strip_ref[...]
    start = jnp.where(first_col, 2 * B, 0)
    below_t = jnp.where(iota(strip.shape, 1) >= start, strip, 0.0)
    padded = jnp.concatenate([below_t, jnp.zeros((LANES - B, strip.shape[1]), jnp.float32)], axis=0)
    a = a_ref[...]
    rows = a.shape[0]
    product = dot_nt(a, padded)
    zero = jnp.zeros((B, rows), jnp.float32)
    panel = jnp.transpose(
        jnp.concatenate([zero, strip[:, :rows], strip[:, rows:], zero], axis=0)
    )
    lane = iota((rows, LANES), 1)
    piece = jnp.where(lane < B, product, panel)
    piece = jnp.where(lane >= 3 * B, pltpu.roll(a[:, :LANES], 2 * B, 1), piece)
    out_ref[:, 0:PIECE, :] = piece.reshape(COLS, PIECE, LANES)
    gram = fold(dot_nt(below_t, padded))
    gram = gram + jnp.where(beyond(piece, VALUE_MAX) > 0.0, jnp.inf, 0.0)
    corner = fold(pltpu.roll(panel[B : 2 * B], LANES - B, 1))
    out_ref[:, PIECE : PIECE + 8, :] = jnp.broadcast_to(gram[None], (COLS, 8, LANES))
    out_ref[:, PIECE + 8 : PIECE + 16, :] = jnp.broadcast_to(corner[None], (COLS, 8, LANES))


def placed(blocks):
    wide = []
    for block, quarter in blocks:
        block = jnp.concatenate([block, jnp.zeros((B, LANES - B), jnp.float32)], axis=1)
        wide.append(pltpu.roll(block, B * quarter, 1) if quarter else block)
    return jnp.concatenate(wide, axis=0)


def factor_kernel(in_ref, out_ref, own_ref, vectors_ref):
    row_at = lax.axis_index("row")
    col_at = lax.axis_index("col")
    gram = unfold(jnp.sum(in_ref[:, PIECE : PIECE + 8, :], axis=0))
    sub = iota((B, B), 0)
    lane = iota((B, B), 1)
    eye = jnp.where(sub == lane, 1.0, 0.0)

    def column(of, j):
        return jnp.broadcast_to(of[:, j : j + 1], (B, B))

    def total(x):
        return jnp.sum(x, axis=0, keepdims=True)

    work = unfold(in_ref[0, PIECE + 8 : PIECE + 16, :])
    coef = eye
    image = gram
    top = jnp.zeros((B, B), jnp.float32)
    coefs = jnp.zeros((B, B), jnp.float32)
    images = jnp.zeros((B, B), jnp.float32)
    wrong = jnp.zeros((1, B), jnp.float32)
    x_top, x_coef, x_image = column(work, 0), column(coef, 0), column(image, 0)
    for j in range(B):
        pivot = x_top[j : j + 1, :]
        norm2 = total(x_top * x_top + x_coef * x_image)
        inner = total(x_top * work + x_coef * image)
        wrong = jnp.where(norm2 > 0.0, wrong, 1.0)
        norm = norm2 * lax.rsqrt(norm2)
        scale = lax.rsqrt(2.0 * (norm2 + jnp.abs(pivot) * norm) + EPS)
        signed = jnp.where(pivot >= 0.0, norm, -norm)
        v_top = scale * jnp.where(sub == j, x_top + signed, x_top)
        v_coef = scale * x_coef
        v_image = scale * x_image
        top = jnp.where(lane == j, v_top, top)
        coefs = jnp.where(lane == j, v_coef, coefs)
        images = jnp.where(lane == j, v_image, images)
        if j + 1 < B:
            y_top, y_coef, y_image = column(work, j + 1), column(coef, j + 1), column(image, j + 1)
            near = total(x_top * y_top + x_coef * y_image)
            near = (2.0 * scale) * (near + signed * y_top[j : j + 1, :])
            twice = (2.0 * scale) * (inner + signed * work[j : j + 1, :])
            work = work - v_top * twice
            coef = coef - v_coef * twice
            image = image - v_image * twice
            x_top = jnp.where(sub > j, y_top - v_top * near, 0.0)
            x_coef = y_coef - v_coef * near
            x_image = y_image - v_image * near
    vectors = jnp.concatenate([coefs, top], axis=0)
    overlap = dot_tn(vectors, jnp.concatenate([images, top], axis=0))
    upper = jnp.where(sub < lane, overlap, 0.0)
    triangle = 2.0 * eye
    for k in range(B - 1, 0, -1):
        triangle = triangle - (2.0 * column(upper, k)) * triangle[k : k + 1, :]
    vectors_t = dot(vectors, triangle)
    vectors_ref[0] = vectors
    vectors_ref[1] = vectors_t
    diag = jnp.sum(jnp.where(sub == lane, gram, 0.0), axis=1, keepdims=True)
    growth = total(jnp.abs(coefs) * jnp.sqrt(diag))
    wrong = jnp.where(growth <= AMPLIFY_MAX, wrong, 1.0)
    outside = jnp.where((diag >= GRAM_MIN) & (diag <= GRAM_MAX), 0.0, 1.0)
    wrong = jnp.maximum(jnp.max(wrong, keepdims=True), jnp.max(outside, keepdims=True))
    wrong = jnp.maximum(wrong, beyond(vectors_t, MIXED_MAX))
    mix = placed([(vectors_t[:B], 0), (coefs, 1), (vectors_t[B:], 0), (top, 1)])
    lane = iota((PIECE, LANES), 1)
    panel = in_ref[row_at // 2, 0:PIECE, :]
    panel = jnp.where(row_at % 2 == 0, panel, pltpu.roll(panel, LANES - B, 1))
    other = pltpu.roll(in_ref[0, 0:PIECE, :], LANES - B, 1)
    at = iota((PIECE, LANES), 0) + (row_at * COLS + col_at) * PIECE
    piece = jnp.where(at < 2 * B, 0.0, panel)
    piece = jnp.where(lane < B, jnp.sum(in_ref[:, 0:PIECE, :], axis=0), piece)
    piece = jnp.where(lane >= 2 * B, other, piece)
    piece = jnp.where(lane >= 3 * B, jnp.where(at - B == lane - 3 * B, 1.0, 0.0), piece)
    piece = dot(piece, mix)
    half = PIECE // 2
    own_ref[...] = jnp.where(
        lane[:half] < 2 * B, piece[:half], pltpu.roll(piece[half:], LANES // 2, 1)
    )
    rows = PIECE // 4
    packed = piece[:rows]
    for k in (1, 2, 3):
        moved = pltpu.roll(piece, B * k, 1)[rows * k : rows * (k + 1)]
        packed = jnp.where(lane[:rows] // B == k, moved, packed)
    packed = packed + jnp.where(wrong > 0.0, jnp.inf, 0.0)
    out_ref[...] = jnp.broadcast_to(packed[None], (ROWS, rows, LANES))


def side_kernel(panel_ref, strip_ref, vectors_ref, mixed_ref, right_ref):
    first_col = lax.axis_index("col") == 0
    vectors = vectors_ref[0]
    strip = strip_ref[...]
    lane_c = iota(strip.shape, 1)
    below_t = jnp.where(lane_c >= jnp.where(first_col, 2 * B, 0), strip, 0.0)
    unit_t = jnp.where(first_col & (iota(strip.shape, 0) == lane_c - B), 1.0, 0.0)
    right_ref[...] = dot_tn(vectors, jnp.concatenate([below_t, unit_t], axis=0))
    panel = panel_ref[:, 0:PIECE, :]
    source = iota(panel.shape, 0)
    order = iota(panel.shape, 1) + lax.axis_index("col") * PIECE
    lane = iota(panel.shape, 2)
    panel = jnp.where((source == 0) & (order < 2 * B) & (lane < 2 * B), 0.0, panel)
    unit = jnp.where((source == 0) & (order - B == lane - 3 * B), 1.0, 0.0)
    panel = jnp.where(lane >= 3 * B, unit, panel).reshape(COLS * PIECE, LANES)
    vectors_t = vectors_ref[1]
    zero = jnp.zeros((B, B), jnp.float32)
    mix = placed([(zero, 0), (vectors_t[:B], 0), (vectors_t[:B], 1), (vectors_t[B:], 0)])
    mixed = dot(panel, mix)
    moved = pltpu.roll(mixed, LANES - B, 1).reshape(COLS, PIECE, LANES)
    mixed = mixed.reshape(COLS, PIECE, LANES)
    rows = PIECE // 4
    group = iota((COLS * 2 * rows, LANES), 1) // B
    packed = jnp.zeros((COLS * 2 * rows, LANES), jnp.float32)
    for k in range(4):
        at = slice(rows * k, rows * (k + 1))
        part = jnp.concatenate([mixed[:, at], moved[:, at]], axis=1).reshape(COLS * 2 * rows, LANES)
        part = pltpu.roll(part, B * k, 1) if k else part
        packed = jnp.where(group == k, part, packed)
    mixed_ref[...] = packed


def unfold_rows(block):
    flat = block.reshape(COLS * 8, LANES)
    upper = pltpu.roll(flat, LANES // 2, 1).reshape(block.shape)
    return jnp.concatenate([block, upper], axis=1).reshape(COLS * PIECE, LANES)


def inner_kernel(in_ref, own_ref, mixed_ref, out_ref, ok_ref):
    half = PIECE // 2
    got = in_ref[...]
    ok_ref[0, 0] = 1 - jnp.max(beyond(got.reshape(-1, LANES), FINITE_MAX)).astype(jnp.int32)
    pairs = got.reshape(COLS, 2, PIECE // 4, LANES)
    columns = jnp.concatenate([pairs[:, 0], pairs[:, 1]], axis=1)
    square = dot_tn(mixed_ref[...], columns.reshape(COLS * half, LANES))
    inner = square[:B]
    for k in (1, 2, 3):
        inner = inner + pltpu.roll(square[B * k : B * (k + 1)], LANES - B * k, 1)
    out_ref[:, 0:half, :] = jnp.broadcast_to(own_ref[...][None], (COLS, half, LANES))
    out_ref[:, half : 2 * half, :] = columns
    out_ref[:, 2 * half : 3 * half, :] = jnp.broadcast_to(fold(inner)[None], (COLS, half, LANES))


def update_kernel(a_ref, in_ref, right_ref, out_ref):
    half = PIECE // 2
    inner = unfold(jnp.sum(in_ref[:, 2 * half : 3 * half, :], axis=0))
    shift = 0.5 * (inner + jnp.transpose(inner))
    left = unfold_rows(in_ref[:, 0:half, :])[:, : 2 * B]
    zero = jnp.zeros((B, B), jnp.float32)
    shift = jnp.concatenate([zero, shift], axis=0)
    shift = jnp.concatenate([shift, jnp.zeros((2 * B, B), jnp.float32)], axis=1)
    left = left - dot(left, shift)
    flat = in_ref[:, half : 2 * half, :].reshape(COLS * half, LANES)
    quarter = [flat] + [pltpu.roll(flat, LANES - B * k, 1) for k in (1, 2, 3)]
    quarter = [part.reshape(COLS, half, LANES) for part in quarter]
    halves = []
    for k in range(2):
        at = slice(k * half // 2, (k + 1) * half // 2)
        unfolded = jnp.concatenate([part[:, at] for part in quarter], axis=1)
        halves.append(jnp.transpose(unfolded.reshape(COLS * PIECE, LANES))[:B])
    right = jnp.concatenate([right_ref[...], jnp.concatenate(halves, axis=1)], axis=0)
    out_ref[...] = a_ref[...] - dot(left, right)


def call(kernel, *shapes, smem=()):
    vmem = pl.BlockSpec(memory_space=pltpu.VMEM)
    specs = [
        pl.BlockSpec(memory_space=pltpu.SMEM) if k in smem else vmem for k in range(len(shapes))
    ]
    return pl.pallas_call(
        kernel,
        out_shape=list(shapes),
        out_specs=specs,
        compiler_params=pltpu.CompilerParams(vmem_limit_bytes=32 * 1024 * 1024),
    )


def array(*shape, dtype=jnp.float32):
    return jax.ShapeDtypeStruct(shape, dtype)


def spread(strip):
    strip = lax.optimization_barrier(jnp.where(lax.axis_index("row") == 0, strip, 0.0))
    first, second = [], []
    for x in range(4):
        for col in range(COLS):
            near, far = (2, 6) if col < 3 * COLS // 4 else (6, 2)
            first.append((8 * x * COLS + col, (8 * x + near) * COLS + col))
            second.append(((8 * x + near) * COLS + col, (8 * x + 4) * COLS + col))
            second.append((8 * x * COLS + col, (8 * x + far) * COLS + col))
    for axes, pairs in (
        ("row", [(0, 8)]),
        ("row", [(0, 24), (8, 16)]),
        (("row", "col"), first),
        (("row", "col"), second),
        ("row", [(k, k + 1) for k in range(0, ROWS, 2)]),
    ):
        strip = strip + lax.ppermute(strip, axes, pairs)
    return strip


def on_device(matrix):
    strip = spread(matrix[:B, :])
    (sent,) = call(partial_kernel, array(COLS, 2 * PIECE, LANES))(matrix, strip)
    panel = lax.all_to_all(sent, "col", 0, 0)
    sent, own, vectors = call(
        factor_kernel,
        array(ROWS, PIECE // 4, LANES),
        array(PIECE // 2, LANES),
        array(2, 2 * B, B),
    )(panel)
    mixed, right = call(side_kernel, array(LANES, LANES), array(B, matrix.shape[1]))(
        panel, strip, vectors
    )
    got = lax.all_to_all(sent, "row", 0, 0)
    sent, fine = call(
        inner_kernel,
        array(COLS, 3 * PIECE // 2, LANES),
        array(1, 1, dtype=jnp.int32),
        smem=(1,),
    )(got, own, mixed)
    got = lax.all_to_all(sent, "col", 0, 0)
    (fast,) = call(update_kernel, array(*matrix.shape))(matrix, got, right)
    return lax.cond(fine[0, 0] > 0, lambda: fast, lambda: general_path(matrix, strip))


def solution(mesh):
    return jax.shard_map(
        on_device,
        mesh=mesh,
        in_specs=(P("row", "col"),),
        out_specs=P("row", "col"),
        check_vma=False,
    )
```

```python
import jax
import jax.numpy as jnp
from jax import lax
from jax.experimental import pallas as pl
from jax.experimental.pallas import tpu as pltpu
from jax.sharding import PartitionSpec as P

B = 32
ROWS = 32
COLS = 16
PIECE = 16
LANES = 128
EPS = 1e-06
AMPLIFY_MAX = 16.0
GRAM_MIN = 1e-06
GRAM_MAX = 1e08
VALUE_MAX = 1e12
MIXED_MAX = 1e08
FINITE_MAX = 3e38

HIGHEST = lax.Precision.HIGHEST


def gather(shard, axis, count):
    return lax.all_to_all(jnp.broadcast_to(shard[None], (count, *shard.shape)), axis, 0, 0)


def householder(panel_cols):
    count = panel_cols.shape[0]
    width = panel_cols.shape[1]
    rows_at = jnp.arange(count, dtype=jnp.int32)

    def sweep(column_at, carried):
        working, reflectors = carried
        column = lax.dynamic_slice_in_dim(working, column_at, 1, 1)[:, 0]
        pivot = width + column_at
        below = jnp.where(rows_at >= pivot, column, 0.0)
        col_norm = jnp.sqrt(jnp.sum(below * below))
        pivot_value = lax.dynamic_slice_in_dim(column, pivot, 1, 0)[0]
        pivot_sign = jnp.where(pivot_value >= 0.0, 1.0, -1.0)
        vector = below + jnp.where(rows_at == pivot, pivot_sign * col_norm, 0.0)
        vector = vector / jnp.sqrt(jnp.sum(vector * vector) + EPS)
        weights = jnp.dot(vector, working, precision=HIGHEST)
        working = working - 2.0 * vector[:, None] * weights[None, :]
        reflectors = lax.dynamic_update_slice_in_dim(reflectors, vector[:, None], column_at, 1)
        return (working, reflectors)

    finished, reflectors = lax.fori_loop(0, width, sweep, (panel_cols, jnp.zeros_like(panel_cols)))
    gram = jnp.dot(reflectors.T, reflectors, precision=HIGHEST)
    order = jnp.arange(width, dtype=jnp.int32)

    def extend(column_at, triangle):
        earlier = jnp.where(
            order < column_at, lax.dynamic_slice_in_dim(gram, column_at, 1, 1)[:, 0], 0.0
        )
        column = -2.0 * jnp.dot(triangle, earlier, precision=HIGHEST) + jnp.where(
            order == column_at, 2.0, 0.0
        )
        return lax.dynamic_update_slice_in_dim(triangle, column[:, None], column_at, 1)

    triangle = lax.fori_loop(0, width, extend, jnp.zeros((width, width), panel_cols.dtype))
    return (reflectors, triangle)


def general_path(matrix, strip):
    rows_dev = matrix.shape[0]
    cols_dev = matrix.shape[1]
    row_at = lax.axis_index("row")
    col_at = lax.axis_index("col")
    gathered = gather(strip[:B], "col", COLS).transpose(0, 2, 1).reshape(COLS * cols_dev, B)
    rows_at = jnp.arange(gathered.shape[0], dtype=jnp.int32)
    panel_cols = jnp.where(rows_at[:, None] >= B, gathered, 0.0)
    reflectors, triangle = householder(panel_cols)
    own_rows = lax.dynamic_slice_in_dim(reflectors, row_at * rows_dev, rows_dev, 0)
    own_cols = lax.dynamic_slice_in_dim(reflectors, col_at * cols_dev, cols_dev, 0)
    row_product = jnp.sum(gather(jnp.dot(matrix, own_cols, precision=HIGHEST), "col", COLS), axis=0)
    row_scaled = jnp.dot(row_product, triangle, precision=HIGHEST)
    whole = gather(row_scaled, "row", ROWS).reshape(ROWS * rows_dev, B)
    inner = jnp.dot(reflectors.T, whole, precision=HIGHEST)
    col_scaled = lax.dynamic_slice_in_dim(whole, col_at * cols_dev, cols_dev, 0)
    correction = jnp.dot(triangle.T, inner, precision=HIGHEST)
    row_coupled = row_scaled - 0.5 * jnp.dot(own_rows, correction, precision=HIGHEST)
    col_coupled = col_scaled - 0.5 * jnp.dot(own_cols, correction, precision=HIGHEST)
    left = jnp.concatenate([row_coupled, own_rows], axis=1)
    right = jnp.concatenate([own_cols, col_coupled], axis=1)
    return matrix - lax.dot_general(left, right, (((1,), (1,)), ((), ())), precision=HIGHEST)


def dot(a, b, over=((1,), (0,))):
    return lax.dot_general(
        a, b, (over, ((), ())), precision=HIGHEST, preferred_element_type=jnp.float32
    )


def dot_nt(a, b):
    return dot(a, b, ((1,), (1,)))


def dot_tn(a, b):
    return dot(a, b, ((0,), (0,)))


def iota(shape, axis):
    return lax.broadcasted_iota(jnp.int32, shape, axis)


def beyond(x, limit):
    return jnp.max(jnp.where(jnp.abs(x) <= limit, 0.0, 1.0), keepdims=True)


def fold(square):
    group = iota((8, LANES), 1) // B
    packed = square[0:8]
    for k in range(1, B // 8):
        packed = jnp.where(group == k, pltpu.roll(square[8 * k : 8 * k + 8], B * k, 1), packed)
    return packed


def unfold(packed):
    parts = [packed] + [pltpu.roll(packed, LANES - B * k, 1) for k in range(1, B // 8)]
    return jnp.concatenate(parts, axis=0)[:, :B]


def partial_kernel(a_ref, strip_ref, out_ref):
    first_col = lax.axis_index("col") == 0
    strip = strip_ref[...]
    start = jnp.where(first_col, 2 * B, 0)
    below_t = jnp.where(iota(strip.shape, 1) >= start, strip, 0.0)
    padded = jnp.concatenate([below_t, jnp.zeros((LANES - B, strip.shape[1]), jnp.float32)], axis=0)
    a = a_ref[...]
    rows = a.shape[0]
    product = dot_nt(a, padded)
    zero = jnp.zeros((B, rows), jnp.float32)
    panel = jnp.transpose(
        jnp.concatenate([zero, strip[:, :rows], strip[:, rows:], zero], axis=0)
    )
    lane = iota((rows, LANES), 1)
    piece = jnp.where(lane < B, product, panel)
    piece = jnp.where(lane >= 3 * B, pltpu.roll(a[:, :LANES], 2 * B, 1), piece)
    out_ref[:, 0:PIECE, :] = piece.reshape(COLS, PIECE, LANES)
    gram = fold(dot_nt(below_t, padded))
    gram = gram + jnp.where(beyond(piece, VALUE_MAX) > 0.0, jnp.inf, 0.0)
    corner = fold(pltpu.roll(panel[B : 2 * B], LANES - B, 1))
    out_ref[:, PIECE : PIECE + 8, :] = jnp.broadcast_to(gram[None], (COLS, 8, LANES))
    out_ref[:, PIECE + 8 : PIECE + 16, :] = jnp.broadcast_to(corner[None], (COLS, 8, LANES))


def placed(blocks):
    wide = []
    for block, quarter in blocks:
        block = jnp.concatenate([block, jnp.zeros((B, LANES - B), jnp.float32)], axis=1)
        wide.append(pltpu.roll(block, B * quarter, 1) if quarter else block)
    return jnp.concatenate(wide, axis=0)


def factor_kernel(in_ref, out_ref, own_ref, vectors_ref):
    row_at = lax.axis_index("row")
    col_at = lax.axis_index("col")
    gram = unfold(jnp.sum(in_ref[:, PIECE : PIECE + 8, :], axis=0))
    sub = iota((B, B), 0)
    lane = iota((B, B), 1)
    eye = jnp.where(sub == lane, 1.0, 0.0)

    def column(of, j):
        return jnp.broadcast_to(of[:, j : j + 1], (B, B))

    def total(x):
        return jnp.sum(x, axis=0, keepdims=True)

    work = unfold(in_ref[0, PIECE + 8 : PIECE + 16, :])
    coef = eye
    image = gram
    top = jnp.zeros((B, B), jnp.float32)
    coefs = jnp.zeros((B, B), jnp.float32)
    images = jnp.zeros((B, B), jnp.float32)
    wrong = jnp.zeros((1, B), jnp.float32)
    x_top, x_coef, x_image = column(work, 0), column(coef, 0), column(image, 0)
    for j in range(B):
        pivot = x_top[j : j + 1, :]
        norm2 = total(x_top * x_top + x_coef * x_image)
        inner = total(x_top * work + x_coef * image)
        wrong = jnp.where(norm2 > 0.0, wrong, 1.0)
        norm = norm2 * lax.rsqrt(norm2)
        scale = lax.rsqrt(2.0 * (norm2 + jnp.abs(pivot) * norm) + EPS)
        signed = jnp.where(pivot >= 0.0, norm, -norm)
        v_top = scale * jnp.where(sub == j, x_top + signed, x_top)
        v_coef = scale * x_coef
        v_image = scale * x_image
        top = jnp.where(lane == j, v_top, top)
        coefs = jnp.where(lane == j, v_coef, coefs)
        images = jnp.where(lane == j, v_image, images)
        if j + 1 < B:
            y_top, y_coef, y_image = column(work, j + 1), column(coef, j + 1), column(image, j + 1)
            near = total(x_top * y_top + x_coef * y_image)
            near = (2.0 * scale) * (near + signed * y_top[j : j + 1, :])
            twice = (2.0 * scale) * (inner + signed * work[j : j + 1, :])
            work = work - v_top * twice
            coef = coef - v_coef * twice
            image = image - v_image * twice
            x_top = jnp.where(sub > j, y_top - v_top * near, 0.0)
            x_coef = y_coef - v_coef * near
            x_image = y_image - v_image * near
    vectors = jnp.concatenate([coefs, top], axis=0)
    overlap = dot_tn(vectors, jnp.concatenate([images, top], axis=0))
    upper = jnp.where(sub < lane, overlap, 0.0)
    triangle = 2.0 * eye
    for k in range(B - 1, 0, -1):
        triangle = triangle - (2.0 * column(upper, k)) * triangle[k : k + 1, :]
    vectors_t = dot(vectors, triangle)
    vectors_ref[0] = vectors
    vectors_ref[1] = vectors_t
    diag = jnp.sum(jnp.where(sub == lane, gram, 0.0), axis=1, keepdims=True)
    growth = total(jnp.abs(coefs) * jnp.sqrt(diag))
    wrong = jnp.where(growth <= AMPLIFY_MAX, wrong, 1.0)
    outside = jnp.where((diag >= GRAM_MIN) & (diag <= GRAM_MAX), 0.0, 1.0)
    wrong = jnp.maximum(jnp.max(wrong, keepdims=True), jnp.max(outside, keepdims=True))
    wrong = jnp.maximum(wrong, beyond(vectors_t, MIXED_MAX))
    mix = placed([(vectors_t[:B], 0), (coefs, 1), (vectors_t[B:], 0), (top, 1)])
    lane = iota((PIECE, LANES), 1)
    panel = in_ref[row_at // 2, 0:PIECE, :]
    panel = jnp.where(row_at % 2 == 0, panel, pltpu.roll(panel, LANES - B, 1))
    other = pltpu.roll(in_ref[0, 0:PIECE, :], LANES - B, 1)
    at = iota((PIECE, LANES), 0) + (row_at * COLS + col_at) * PIECE
    piece = jnp.where(at < 2 * B, 0.0, panel)
    piece = jnp.where(lane < B, jnp.sum(in_ref[:, 0:PIECE, :], axis=0), piece)
    piece = jnp.where(lane >= 2 * B, other, piece)
    piece = jnp.where(lane >= 3 * B, jnp.where(at - B == lane - 3 * B, 1.0, 0.0), piece)
    piece = dot(piece, mix)
    half = PIECE // 2
    own_ref[...] = jnp.where(
        lane[:half] < 2 * B, piece[:half], pltpu.roll(piece[half:], LANES // 2, 1)
    )
    rows = PIECE // 4
    packed = piece[:rows]
    for k in (1, 2, 3):
        moved = pltpu.roll(piece, B * k, 1)[rows * k : rows * (k + 1)]
        packed = jnp.where(lane[:rows] // B == k, moved, packed)
    packed = packed + jnp.where(wrong > 0.0, jnp.inf, 0.0)
    out_ref[...] = jnp.broadcast_to(packed[None], (ROWS, rows, LANES))


def side_kernel(panel_ref, strip_ref, vectors_ref, mixed_ref, right_ref):
    first_col = lax.axis_index("col") == 0
    vectors = vectors_ref[0]
    strip = strip_ref[...]
    lane_c = iota(strip.shape, 1)
    below_t = jnp.where(lane_c >= jnp.where(first_col, 2 * B, 0), strip, 0.0)
    unit_t = jnp.where(first_col & (iota(strip.shape, 0) == lane_c - B), 1.0, 0.0)
    right_ref[...] = dot_tn(vectors, jnp.concatenate([below_t, unit_t], axis=0))
    panel = panel_ref[:, 0:PIECE, :]
    source = iota(panel.shape, 0)
    order = iota(panel.shape, 1) + lax.axis_index("col") * PIECE
    lane = iota(panel.shape, 2)
    panel = jnp.where((source == 0) & (order < 2 * B) & (lane < 2 * B), 0.0, panel)
    unit = jnp.where((source == 0) & (order - B == lane - 3 * B), 1.0, 0.0)
    panel = jnp.where(lane >= 3 * B, unit, panel).reshape(COLS * PIECE, LANES)
    vectors_t = vectors_ref[1]
    zero = jnp.zeros((B, B), jnp.float32)
    mix = placed([(zero, 0), (vectors_t[:B], 0), (vectors_t[:B], 1), (vectors_t[B:], 0)])
    mixed = dot(panel, mix)
    moved = pltpu.roll(mixed, LANES - B, 1).reshape(COLS, PIECE, LANES)
    mixed = mixed.reshape(COLS, PIECE, LANES)
    rows = PIECE // 4
    group = iota((COLS * 2 * rows, LANES), 1) // B
    packed = jnp.zeros((COLS * 2 * rows, LANES), jnp.float32)
    for k in range(4):
        at = slice(rows * k, rows * (k + 1))
        part = jnp.concatenate([mixed[:, at], moved[:, at]], axis=1).reshape(COLS * 2 * rows, LANES)
        part = pltpu.roll(part, B * k, 1) if k else part
        packed = jnp.where(group == k, part, packed)
    mixed_ref[...] = packed


def unfold_rows(block):
    flat = block.reshape(COLS * 8, LANES)
    upper = pltpu.roll(flat, LANES // 2, 1).reshape(block.shape)
    return jnp.concatenate([block, upper], axis=1).reshape(COLS * PIECE, LANES)


def inner_kernel(in_ref, own_ref, mixed_ref, out_ref, ok_ref):
    half = PIECE // 2
    got = in_ref[...]
    ok_ref[0, 0] = 1 - jnp.max(beyond(got.reshape(-1, LANES), FINITE_MAX)).astype(jnp.int32)
    pairs = got.reshape(COLS, 2, PIECE // 4, LANES)
    columns = jnp.concatenate([pairs[:, 0], pairs[:, 1]], axis=1)
    square = dot_tn(mixed_ref[...], columns.reshape(COLS * half, LANES))
    inner = square[:B]
    for k in (1, 2, 3):
        inner = inner + pltpu.roll(square[B * k : B * (k + 1)], LANES - B * k, 1)
    out_ref[:, 0:half, :] = jnp.broadcast_to(own_ref[...][None], (COLS, half, LANES))
    out_ref[:, half : 2 * half, :] = columns
    out_ref[:, 2 * half : 3 * half, :] = jnp.broadcast_to(fold(inner)[None], (COLS, half, LANES))


def update_kernel(a_ref, in_ref, right_ref, out_ref):
    half = PIECE // 2
    inner = unfold(jnp.sum(in_ref[:, 2 * half : 3 * half, :], axis=0))
    shift = 0.5 * (inner + jnp.transpose(inner))
    left = unfold_rows(in_ref[:, 0:half, :])[:, : 2 * B]
    zero = jnp.zeros((B, B), jnp.float32)
    shift = jnp.concatenate([zero, shift], axis=0)
    shift = jnp.concatenate([shift, jnp.zeros((2 * B, B), jnp.float32)], axis=1)
    left = left - dot(left, shift)
    flat = in_ref[:, half : 2 * half, :].reshape(COLS * half, LANES)
    quarter = [flat] + [pltpu.roll(flat, LANES - B * k, 1) for k in (1, 2, 3)]
    quarter = [part.reshape(COLS, half, LANES) for part in quarter]
    halves = []
    for k in range(2):
        at = slice(k * half // 2, (k + 1) * half // 2)
        unfolded = jnp.concatenate([part[:, at] for part in quarter], axis=1)
        halves.append(jnp.transpose(unfolded.reshape(COLS * PIECE, LANES))[:B])
    right = jnp.concatenate([right_ref[...], jnp.concatenate(halves, axis=1)], axis=0)
    out_ref[...] = a_ref[...] - dot(left, right)


def call(kernel, *shapes, smem=()):
    vmem = pl.BlockSpec(memory_space=pltpu.VMEM)
    specs = [
        pl.BlockSpec(memory_space=pltpu.SMEM) if k in smem else vmem for k in range(len(shapes))
    ]
    return pl.pallas_call(
        kernel,
        out_shape=list(shapes),
        out_specs=specs,
        compiler_params=pltpu.CompilerParams(vmem_limit_bytes=32 * 1024 * 1024),
    )


def array(*shape, dtype=jnp.float32):
    return jax.ShapeDtypeStruct(shape, dtype)


def spread(strip):
    strip = lax.optimization_barrier(jnp.where(lax.axis_index("row") == 0, strip, 0.0))
    first, second = [], []
    for x in range(4):
        for col in range(COLS):
            near, far = (2, 6) if col < 3 * COLS // 4 else (6, 2)
            first.append((8 * x * COLS + col, (8 * x + near) * COLS + col))
            second.append(((8 * x + near) * COLS + col, (8 * x + 4) * COLS + col))
            second.append((8 * x * COLS + col, (8 * x + far) * COLS + col))
    for axes, pairs in (
        ("row", [(0, 8)]),
        ("row", [(0, 24), (8, 16)]),
        (("row", "col"), first),
        (("row", "col"), second),
        ("row", [(k, k + 1) for k in range(0, ROWS, 2)]),
    ):
        strip = strip + lax.ppermute(strip, axes, pairs)
    return strip


def on_device(matrix):
    strip = spread(matrix[:B, :])
    (sent,) = call(partial_kernel, array(COLS, 2 * PIECE, LANES))(matrix, strip)
    panel = lax.all_to_all(sent, "col", 0, 0)
    sent, own, vectors = call(
        factor_kernel,
        array(ROWS, PIECE // 4, LANES),
        array(PIECE // 2, LANES),
        array(2, 2 * B, B),
    )(panel)
    got = lax.all_to_all(sent, "row", 0, 0)
    got, panel = lax.optimization_barrier((got, panel))
    mixed, right = call(side_kernel, array(LANES, LANES), array(B, matrix.shape[1]))(
        panel, strip, vectors
    )
    sent, fine = call(
        inner_kernel,
        array(COLS, 3 * PIECE // 2, LANES),
        array(1, 1, dtype=jnp.int32),
        smem=(1,),
    )(got, own, mixed)
    got = lax.all_to_all(sent, "col", 0, 0)
    (fast,) = call(update_kernel, array(*matrix.shape))(matrix, got, right)
    return lax.cond(fine[0, 0] > 0, lambda: fast, lambda: general_path(matrix, strip))


def solution(mesh):
    return jax.shard_map(
        on_device,
        mesh=mesh,
        in_specs=(P("row", "col"),),
        out_specs=P("row", "col"),
        check_vma=False,
    )
```

```python
import jax
import jax.numpy as jnp
from jax import lax
from jax.experimental import pallas as pl
from jax.experimental.pallas import tpu as pltpu
from jax.sharding import PartitionSpec as P

B = 32
ROWS = 32
COLS = 16
PIECE = 16
LANES = 128
EPS = 1e-06
AMPLIFY_MAX = 16.0
GRAM_MIN = 1e-06
GRAM_MAX = 1e08
VALUE_MAX = 1e12
MIXED_MAX = 1e08
FINITE_MAX = 3e38

HIGHEST = lax.Precision.HIGHEST


def gather(shard, axis, count):
    return lax.all_to_all(jnp.broadcast_to(shard[None], (count, *shard.shape)), axis, 0, 0)


def householder(panel_cols):
    count = panel_cols.shape[0]
    width = panel_cols.shape[1]
    rows_at = jnp.arange(count, dtype=jnp.int32)

    def sweep(column_at, carried):
        working, reflectors = carried
        column = lax.dynamic_slice_in_dim(working, column_at, 1, 1)[:, 0]
        pivot = width + column_at
        below = jnp.where(rows_at >= pivot, column, 0.0)
        col_norm = jnp.sqrt(jnp.sum(below * below))
        pivot_value = lax.dynamic_slice_in_dim(column, pivot, 1, 0)[0]
        pivot_sign = jnp.where(pivot_value >= 0.0, 1.0, -1.0)
        vector = below + jnp.where(rows_at == pivot, pivot_sign * col_norm, 0.0)
        vector = vector / jnp.sqrt(jnp.sum(vector * vector) + EPS)
        weights = jnp.dot(vector, working, precision=HIGHEST)
        working = working - 2.0 * vector[:, None] * weights[None, :]
        reflectors = lax.dynamic_update_slice_in_dim(reflectors, vector[:, None], column_at, 1)
        return (working, reflectors)

    finished, reflectors = lax.fori_loop(0, width, sweep, (panel_cols, jnp.zeros_like(panel_cols)))
    gram = jnp.dot(reflectors.T, reflectors, precision=HIGHEST)
    order = jnp.arange(width, dtype=jnp.int32)

    def extend(column_at, triangle):
        earlier = jnp.where(
            order < column_at, lax.dynamic_slice_in_dim(gram, column_at, 1, 1)[:, 0], 0.0
        )
        column = -2.0 * jnp.dot(triangle, earlier, precision=HIGHEST) + jnp.where(
            order == column_at, 2.0, 0.0
        )
        return lax.dynamic_update_slice_in_dim(triangle, column[:, None], column_at, 1)

    triangle = lax.fori_loop(0, width, extend, jnp.zeros((width, width), panel_cols.dtype))
    return (reflectors, triangle)


def general_path(matrix, strip):
    rows_dev = matrix.shape[0]
    cols_dev = matrix.shape[1]
    row_at = lax.axis_index("row")
    col_at = lax.axis_index("col")
    gathered = gather(strip[:B], "col", COLS).transpose(0, 2, 1).reshape(COLS * cols_dev, B)
    rows_at = jnp.arange(gathered.shape[0], dtype=jnp.int32)
    panel_cols = jnp.where(rows_at[:, None] >= B, gathered, 0.0)
    reflectors, triangle = householder(panel_cols)
    own_rows = lax.dynamic_slice_in_dim(reflectors, row_at * rows_dev, rows_dev, 0)
    own_cols = lax.dynamic_slice_in_dim(reflectors, col_at * cols_dev, cols_dev, 0)
    row_product = jnp.sum(gather(jnp.dot(matrix, own_cols, precision=HIGHEST), "col", COLS), axis=0)
    row_scaled = jnp.dot(row_product, triangle, precision=HIGHEST)
    whole = gather(row_scaled, "row", ROWS).reshape(ROWS * rows_dev, B)
    inner = jnp.dot(reflectors.T, whole, precision=HIGHEST)
    col_scaled = lax.dynamic_slice_in_dim(whole, col_at * cols_dev, cols_dev, 0)
    correction = jnp.dot(triangle.T, inner, precision=HIGHEST)
    row_coupled = row_scaled - 0.5 * jnp.dot(own_rows, correction, precision=HIGHEST)
    col_coupled = col_scaled - 0.5 * jnp.dot(own_cols, correction, precision=HIGHEST)
    left = jnp.concatenate([row_coupled, own_rows], axis=1)
    right = jnp.concatenate([own_cols, col_coupled], axis=1)
    return matrix - lax.dot_general(left, right, (((1,), (1,)), ((), ())), precision=HIGHEST)


def dot(a, b, over=((1,), (0,))):
    return lax.dot_general(
        a, b, (over, ((), ())), precision=HIGHEST, preferred_element_type=jnp.float32
    )


def dot_nt(a, b):
    return dot(a, b, ((1,), (1,)))


def dot_tn(a, b):
    return dot(a, b, ((0,), (0,)))


def iota(shape, axis):
    return lax.broadcasted_iota(jnp.int32, shape, axis)


def beyond(x, limit):
    return jnp.max(jnp.where(jnp.abs(x) <= limit, 0.0, 1.0), keepdims=True)


def fold(square):
    group = iota((8, LANES), 1) // B
    packed = square[0:8]
    for k in range(1, B // 8):
        packed = jnp.where(group == k, pltpu.roll(square[8 * k : 8 * k + 8], B * k, 1), packed)
    return packed


def unfold(packed):
    parts = [packed] + [pltpu.roll(packed, LANES - B * k, 1) for k in range(1, B // 8)]
    return jnp.concatenate(parts, axis=0)[:, :B]


def partial_kernel(a_ref, strip_ref, out_ref):
    first_col = lax.axis_index("col") == 0
    strip = strip_ref[...]
    start = jnp.where(first_col, 2 * B, 0)
    below_t = jnp.where(iota(strip.shape, 1) >= start, strip, 0.0)
    padded = jnp.concatenate([below_t, jnp.zeros((LANES - B, strip.shape[1]), jnp.float32)], axis=0)
    a = a_ref[...]
    rows = a.shape[0]
    product = dot_nt(a, padded)
    zero = jnp.zeros((B, rows), jnp.float32)
    panel = jnp.transpose(
        jnp.concatenate([zero, strip[:, :rows], strip[:, rows:], zero], axis=0)
    )
    lane = iota((rows, LANES), 1)
    piece = jnp.where(lane < B, product, panel)
    piece = jnp.where(lane >= 3 * B, pltpu.roll(a[:, :LANES], 2 * B, 1), piece)
    out_ref[:, 0:PIECE, :] = piece.reshape(COLS, PIECE, LANES)
    gram = fold(dot_nt(below_t, padded))
    gram = gram + jnp.where(beyond(piece, VALUE_MAX) > 0.0, jnp.inf, 0.0)
    corner = fold(pltpu.roll(panel[B : 2 * B], LANES - B, 1))
    out_ref[:, PIECE : PIECE + 8, :] = jnp.broadcast_to(gram[None], (COLS, 8, LANES))
    out_ref[:, PIECE + 8 : PIECE + 16, :] = jnp.broadcast_to(corner[None], (COLS, 8, LANES))


def placed(blocks):
    wide = []
    for block, quarter in blocks:
        block = jnp.concatenate([block, jnp.zeros((B, LANES - B), jnp.float32)], axis=1)
        wide.append(pltpu.roll(block, B * quarter, 1) if quarter else block)
    return jnp.concatenate(wide, axis=0)


def factor_kernel(in_ref, out_ref, own_ref, vectors_ref):
    row_at = lax.axis_index("row")
    col_at = lax.axis_index("col")
    gram = unfold(jnp.sum(in_ref[:, PIECE : PIECE + 8, :], axis=0))
    sub = iota((B, B), 0)
    lane = iota((B, B), 1)
    eye = jnp.where(sub == lane, 1.0, 0.0)

    def column(of, j):
        return jnp.broadcast_to(of[:, j : j + 1], (B, B))

    def total(x):
        return jnp.sum(x, axis=0, keepdims=True)

    work = unfold(in_ref[0, PIECE + 8 : PIECE + 16, :])
    coef = eye
    image = gram
    top = jnp.zeros((B, B), jnp.float32)
    coefs = jnp.zeros((B, B), jnp.float32)
    images = jnp.zeros((B, B), jnp.float32)
    wrong = jnp.zeros((1, B), jnp.float32)
    x_top, x_coef, x_image = column(work, 0), column(coef, 0), column(image, 0)
    for j in range(B):
        pivot = x_top[j : j + 1, :]
        norm2 = total(x_top * x_top + x_coef * x_image)
        inner = total(x_top * work + x_coef * image)
        wrong = jnp.where(norm2 > 0.0, wrong, 1.0)
        norm = norm2 * lax.rsqrt(norm2)
        scale = lax.rsqrt(2.0 * (norm2 + jnp.abs(pivot) * norm) + EPS)
        signed = jnp.where(pivot >= 0.0, norm, -norm)
        v_top = scale * jnp.where(sub == j, x_top + signed, x_top)
        v_coef = scale * x_coef
        v_image = scale * x_image
        top = jnp.where(lane == j, v_top, top)
        coefs = jnp.where(lane == j, v_coef, coefs)
        images = jnp.where(lane == j, v_image, images)
        if j + 1 < B:
            y_top, y_coef, y_image = column(work, j + 1), column(coef, j + 1), column(image, j + 1)
            near = total(x_top * y_top + x_coef * y_image)
            near = (2.0 * scale) * (near + signed * y_top[j : j + 1, :])
            twice = (2.0 * scale) * (inner + signed * work[j : j + 1, :])
            work = work - v_top * twice
            coef = coef - v_coef * twice
            image = image - v_image * twice
            x_top = jnp.where(sub > j, y_top - v_top * near, 0.0)
            x_coef = y_coef - v_coef * near
            x_image = y_image - v_image * near
    vectors = jnp.concatenate([coefs, top], axis=0)
    overlap = dot_tn(vectors, jnp.concatenate([images, top], axis=0))
    upper = jnp.where(sub < lane, overlap, 0.0)
    triangle = 2.0 * eye
    for k in range(B - 1, 0, -1):
        triangle = triangle - (2.0 * column(upper, k)) * triangle[k : k + 1, :]
    vectors_t = dot(vectors, triangle)
    vectors_ref[0] = vectors
    vectors_ref[1] = vectors_t
    diag = jnp.sum(jnp.where(sub == lane, gram, 0.0), axis=1, keepdims=True)
    growth = total(jnp.abs(coefs) * jnp.sqrt(diag))
    wrong = jnp.where(growth <= AMPLIFY_MAX, wrong, 1.0)
    outside = jnp.where((diag >= GRAM_MIN) & (diag <= GRAM_MAX), 0.0, 1.0)
    wrong = jnp.maximum(jnp.max(wrong, keepdims=True), jnp.max(outside, keepdims=True))
    wrong = jnp.maximum(wrong, beyond(vectors_t, MIXED_MAX))
    mix = placed([(vectors_t[:B], 0), (coefs, 1), (vectors_t[B:], 0), (top, 1)])
    lane = iota((PIECE, LANES), 1)
    panel = in_ref[row_at // 2, 0:PIECE, :]
    panel = jnp.where(row_at % 2 == 0, panel, pltpu.roll(panel, LANES - B, 1))
    other = pltpu.roll(in_ref[0, 0:PIECE, :], LANES - B, 1)
    at = iota((PIECE, LANES), 0) + (row_at * COLS + col_at) * PIECE
    piece = jnp.where(at < 2 * B, 0.0, panel)
    piece = jnp.where(lane < B, jnp.sum(in_ref[:, 0:PIECE, :], axis=0), piece)
    piece = jnp.where(lane >= 2 * B, other, piece)
    piece = jnp.where(lane >= 3 * B, jnp.where(at - B == lane - 3 * B, 1.0, 0.0), piece)
    piece = dot(piece, mix)
    half = PIECE // 2
    own_ref[...] = jnp.where(
        lane[:half] < 2 * B, piece[:half], pltpu.roll(piece[half:], LANES // 2, 1)
    )
    rows = PIECE // 4
    packed = piece[:rows]
    for k in (1, 2, 3):
        moved = pltpu.roll(piece, B * k, 1)[rows * k : rows * (k + 1)]
        packed = jnp.where(lane[:rows] // B == k, moved, packed)
    packed = packed + jnp.where(wrong > 0.0, jnp.inf, 0.0)
    out_ref[...] = jnp.broadcast_to(packed[None], (ROWS, rows, LANES))


def columns_kernel(strip_ref, vectors_ref, right_ref):
    first_col = lax.axis_index("col") == 0
    vectors = vectors_ref[0]
    strip = strip_ref[...]
    lane_c = iota(strip.shape, 1)
    below_t = jnp.where(lane_c >= jnp.where(first_col, 2 * B, 0), strip, 0.0)
    unit_t = jnp.where(first_col & (iota(strip.shape, 0) == lane_c - B), 1.0, 0.0)
    right_ref[...] = dot_tn(vectors, jnp.concatenate([below_t, unit_t], axis=0))


def rows_kernel(panel_ref, vectors_ref, mixed_ref):
    panel = panel_ref[:, 0:PIECE, :]
    source = iota(panel.shape, 0)
    order = iota(panel.shape, 1) + lax.axis_index("col") * PIECE
    lane = iota(panel.shape, 2)
    panel = jnp.where((source == 0) & (order < 2 * B) & (lane < 2 * B), 0.0, panel)
    unit = jnp.where((source == 0) & (order - B == lane - 3 * B), 1.0, 0.0)
    panel = jnp.where(lane >= 3 * B, unit, panel).reshape(COLS * PIECE, LANES)
    vectors_t = vectors_ref[1]
    zero = jnp.zeros((B, B), jnp.float32)
    mix = placed([(zero, 0), (vectors_t[:B], 0), (vectors_t[:B], 1), (vectors_t[B:], 0)])
    mixed = dot(panel, mix)
    moved = pltpu.roll(mixed, LANES - B, 1).reshape(COLS, PIECE, LANES)
    mixed = mixed.reshape(COLS, PIECE, LANES)
    rows = PIECE // 4
    group = iota((COLS * 2 * rows, LANES), 1) // B
    packed = jnp.zeros((COLS * 2 * rows, LANES), jnp.float32)
    for k in range(4):
        at = slice(rows * k, rows * (k + 1))
        part = jnp.concatenate([mixed[:, at], moved[:, at]], axis=1).reshape(COLS * 2 * rows, LANES)
        part = pltpu.roll(part, B * k, 1) if k else part
        packed = jnp.where(group == k, part, packed)
    mixed_ref[...] = packed


def unfold_rows(block):
    flat = block.reshape(COLS * 8, LANES)
    upper = pltpu.roll(flat, LANES // 2, 1).reshape(block.shape)
    return jnp.concatenate([block, upper], axis=1).reshape(COLS * PIECE, LANES)


def inner_kernel(in_ref, own_ref, mixed_ref, out_ref, ok_ref):
    half = PIECE // 2
    got = in_ref[...]
    ok_ref[0, 0] = 1 - jnp.max(beyond(got.reshape(-1, LANES), FINITE_MAX)).astype(jnp.int32)
    pairs = got.reshape(COLS, 2, PIECE // 4, LANES)
    columns = jnp.concatenate([pairs[:, 0], pairs[:, 1]], axis=1)
    square = dot_tn(mixed_ref[...], columns.reshape(COLS * half, LANES))
    inner = square[:B]
    for k in (1, 2, 3):
        inner = inner + pltpu.roll(square[B * k : B * (k + 1)], LANES - B * k, 1)
    out_ref[:, 0:half, :] = jnp.broadcast_to(own_ref[...][None], (COLS, half, LANES))
    out_ref[:, half : 2 * half, :] = columns
    out_ref[:, 2 * half : 3 * half, :] = jnp.broadcast_to(fold(inner)[None], (COLS, half, LANES))


def update_kernel(a_ref, in_ref, right_ref, out_ref):
    half = PIECE // 2
    inner = unfold(jnp.sum(in_ref[:, 2 * half : 3 * half, :], axis=0))
    shift = 0.5 * (inner + jnp.transpose(inner))
    left = unfold_rows(in_ref[:, 0:half, :])[:, : 2 * B]
    zero = jnp.zeros((B, B), jnp.float32)
    shift = jnp.concatenate([zero, shift], axis=0)
    shift = jnp.concatenate([shift, jnp.zeros((2 * B, B), jnp.float32)], axis=1)
    left = left - dot(left, shift)
    flat = in_ref[:, half : 2 * half, :].reshape(COLS * half, LANES)
    quarter = [flat] + [pltpu.roll(flat, LANES - B * k, 1) for k in (1, 2, 3)]
    quarter = [part.reshape(COLS, half, LANES) for part in quarter]
    halves = []
    for k in range(2):
        at = slice(k * half // 2, (k + 1) * half // 2)
        unfolded = jnp.concatenate([part[:, at] for part in quarter], axis=1)
        halves.append(jnp.transpose(unfolded.reshape(COLS * PIECE, LANES))[:B])
    right = jnp.concatenate([right_ref[...], jnp.concatenate(halves, axis=1)], axis=0)
    out_ref[...] = a_ref[...] - dot(left, right)


def call(kernel, *shapes, smem=()):
    vmem = pl.BlockSpec(memory_space=pltpu.VMEM)
    specs = [
        pl.BlockSpec(memory_space=pltpu.SMEM) if k in smem else vmem for k in range(len(shapes))
    ]
    return pl.pallas_call(
        kernel,
        out_shape=list(shapes),
        out_specs=specs,
        compiler_params=pltpu.CompilerParams(vmem_limit_bytes=32 * 1024 * 1024),
    )


def array(*shape, dtype=jnp.float32):
    return jax.ShapeDtypeStruct(shape, dtype)


def spread(strip):
    strip = lax.optimization_barrier(jnp.where(lax.axis_index("row") == 0, strip, 0.0))
    first, second = [], []
    for x in range(4):
        for col in range(COLS):
            near, far = (2, 6) if col < 3 * COLS // 4 else (6, 2)
            first.append((8 * x * COLS + col, (8 * x + near) * COLS + col))
            second.append(((8 * x + near) * COLS + col, (8 * x + 4) * COLS + col))
            second.append((8 * x * COLS + col, (8 * x + far) * COLS + col))
    for axes, pairs in (
        ("row", [(0, 8)]),
        ("row", [(0, 24), (8, 16)]),
        (("row", "col"), first),
        (("row", "col"), second),
        ("row", [(k, k + 1) for k in range(0, ROWS, 2)]),
    ):
        strip = strip + lax.ppermute(strip, axes, pairs)
    return strip


def on_device(matrix):
    strip = spread(matrix[:B, :])
    (sent,) = call(partial_kernel, array(COLS, 2 * PIECE, LANES))(matrix, strip)
    panel = lax.all_to_all(sent, "col", 0, 0)
    sent, own, vectors = call(
        factor_kernel,
        array(ROWS, PIECE // 4, LANES),
        array(PIECE // 2, LANES),
        array(2, 2 * B, B),
    )(panel)
    got = lax.all_to_all(sent, "row", 0, 0)
    got, panel = lax.optimization_barrier((got, panel))
    (mixed,) = call(rows_kernel, array(LANES, LANES))(panel, vectors)
    sent, fine = call(
        inner_kernel,
        array(COLS, 3 * PIECE // 2, LANES),
        array(1, 1, dtype=jnp.int32),
        smem=(1,),
    )(got, own, mixed)
    sent, vectors = lax.optimization_barrier((sent, vectors))
    (right,) = call(columns_kernel, array(B, matrix.shape[1]))(strip, vectors)
    got = lax.all_to_all(sent, "col", 0, 0)
    (fast,) = call(update_kernel, array(*matrix.shape))(matrix, got, right)
    return lax.cond(fine[0, 0] > 0, lambda: fast, lambda: general_path(matrix, strip))


def solution(mesh):
    return jax.shard_map(
        on_device,
        mesh=mesh,
        in_specs=(P("row", "col"),),
        out_specs=P("row", "col"),
        check_vma=False,
    )
```
